32 devices in a mesh: row: 8 (over z, x), col: 4 (over y, core).
Axes of the slice: x: 2, y: 2, z: 4, core: 2. Of those that a mesh axis runs over, the one named last changes fastest.
Arguments:
- object_field: float32 [2, 2048, 1024], P(None, 'row', 'col'), may hold values from -6 to 6
- probe: float32 [2, 4, 128, 128], replicated, may hold values from -3 to 3
- amplitudes: float32 [8, 4, 3, 4, 128, 128], P('row', 'col'), may hold values from 0.3 to 3
- offsets: int32 [8, 4, 3, 4, 2], P('row', 'col'), may hold values from -64 to 192, as said below
Outputs:
- object_new: float32 [2, 2048, 1024], P(None, 'row', 'col')
- probe_step: float32 [2, 4, 128, 128], replicated
The draws below stay inside these ranges and needn't reach their ends.
Inputs may be any that keep to these rules, and one draw needn't show every extreme that they name: `offsets`: in every batch of every device the first position is at (-64, -64) and the second at (192, 192).
All inputs are finite; a program needn't handle non-finite values.
Results may differ from the reference program's by a relative error of at most 0.0001.
Values sent between devices are 32-bit elements; how exact they have to be, the bound alone decides.
No kernel may reach another device: no remote copies, remote signals or barrier semaphores. Data moves between devices by JAX's collectives and lax.ppermute only.
A program may use at most 64 MiB of HBM per device.

```python
import math
import jax
import jax.numpy as jnp
from jax import lax

PATCH = 128
MODES = 4
TILE = 256
POS_DEV = 4
BATCHES = 3
GRID_ROWS = 8
GRID_COLS = 4
ROWS_ALL = 2048
COLS_ALL = 1024


def draw_offsets(key, part):
    half_patch = PATCH // 2
    values = jax.random.randint(key, (GRID_ROWS, GRID_COLS, BATCHES, POS_DEV, 2), -half_patch, TILE - half_patch + 1, dtype=jnp.int32)
    values = values.at[:, :, :, 0, :].set(-half_patch)
    values = values.at[:, :, :, 1, :].set(TILE - half_patch)
    return values


def level_of(rng, dims, split, least, high):
    def one(axis_at, parts):
        heights = jax.random.uniform(jax.random.fold_in(jax.random.fold_in(rng, 6), axis_at), (parts,), jnp.float32, least / len(split), high / len(split))
        return jnp.repeat(jnp.exp(heights), dims[axis_at] // parts).reshape((-1,) + (1,) * (len(dims) - axis_at - 1))

    level = one(*split[0])
    for cut in split[1:]:
        level = level * one(*cut)
    return level


def gaussian(key, extent, scale, most, cuts=(), kind=jnp.bfloat16):
    entries = jax.random.normal(key, extent, jnp.float32) * scale
    if len(cuts) > 0:
        entries = level_of(key, extent, cuts, -0.22, 0.18) * entries
    return jnp.clip(entries, min=-most, max=most).astype(kind)


def setup_inputs(seed: int = 0) -> dict:
    key_of = jax.random.split(jax.random.key(seed), 5)
    return {
        "object_field": gaussian(key_of[0], (2, ROWS_ALL, COLS_ALL), 1.0, 6.0, ((1, 8), (2, 4)), jnp.float32),
        "probe": gaussian(key_of[1], (2, MODES, PATCH, PATCH), 0.5, 3.0, (), jnp.float32),
        "amplitudes": jnp.clip(jnp.exp(math.log(3.0) - 2.3025851 * jax.random.uniform(key_of[2], (GRID_ROWS, GRID_COLS, BATCHES, POS_DEV, PATCH, PATCH), jnp.float32) ** level_of(key_of[2], (GRID_ROWS, GRID_COLS, BATCHES, POS_DEV, PATCH, PATCH), ((0, 8), (1, 4)), -0.2, 0.2)), 0.3, 3.0),
        "offsets": draw_offsets(jax.random.fold_in(key_of[4], 71), 0),
    }


AMP_FLOOR = 0.25
OBJECT_REG = 0.5
PROBE_REG = 1.0
PRECISE_DOT = lax.Precision.HIGHEST

def dft_tables(length):
    indices = jnp.arange(length, dtype=jnp.int32)
    product = indices[:, None] * indices[None, :] % length
    angles = product.astype(jnp.float32) * (2.0 * math.pi / length)
    factor_norm = 1.0 / math.sqrt(length)
    return (jnp.cos(angles) * factor_norm, -jnp.sin(angles) * factor_norm)

def transform(field_real, field_imag, table_real, table_imag, direction):
    signed = direction * table_imag
    left_real = jnp.einsum('jk,...kl->...jl', table_real, field_real, precision=PRECISE_DOT) - jnp.einsum('jk,...kl->...jl', signed, field_imag, precision=PRECISE_DOT)
    left_imag = jnp.einsum('jk,...kl->...jl', table_real, field_imag, precision=PRECISE_DOT) + jnp.einsum('jk,...kl->...jl', signed, field_real, precision=PRECISE_DOT)
    out_real = jnp.einsum('...jk,kl->...jl', left_real, table_real, precision=PRECISE_DOT) - jnp.einsum('...jk,kl->...jl', left_imag, signed, precision=PRECISE_DOT)
    out_imag = jnp.einsum('...jk,kl->...jl', left_imag, table_real, precision=PRECISE_DOT) + jnp.einsum('...jk,kl->...jl', left_real, signed, precision=PRECISE_DOT)
    return (out_real, out_imag)

def patch_terms(patch_real, patch_imag, probe_real, probe_imag, measured, table_real, table_imag):
    wave_real = probe_real[None] * patch_real[:, None] - probe_imag[None] * patch_imag[:, None]
    wave_imag = probe_real[None] * patch_imag[:, None] + probe_imag[None] * patch_real[:, None]
    far_real, far_imag = transform(wave_real, wave_imag, table_real, table_imag, 1.0)
    intensity = lax.optimization_barrier(jnp.sum(far_real * far_real + far_imag * far_imag, axis=1))
    factor = measured / jnp.maximum(jnp.sqrt(intensity), AMP_FLOOR) - 1.0
    change_real, change_imag = transform(factor[:, None] * far_real, factor[:, None] * far_imag, table_real, table_imag, -1.0)
    object_real = lax.optimization_barrier(jnp.sum(probe_real[None] * change_real + probe_imag[None] * change_imag, axis=1))
    object_imag = lax.optimization_barrier(jnp.sum(probe_real[None] * change_imag - probe_imag[None] * change_real, axis=1))
    gradient_real = lax.optimization_barrier(jnp.sum(patch_real[:, None] * change_real + patch_imag[:, None] * change_imag, axis=0))
    gradient_imag = lax.optimization_barrier(jnp.sum(patch_real[:, None] * change_imag - patch_imag[:, None] * change_real, axis=0))
    object_power = lax.optimization_barrier(jnp.sum(patch_real * patch_real + patch_imag * patch_imag, axis=0))
    return (object_real, object_imag, gradient_real, gradient_imag, object_power)

def reference(object_field, probe, amplitudes, offsets):
    half_patch = PATCH // 2
    table_real, table_imag = dft_tables(PATCH)
    probe_real, probe_imag = (probe[0], probe[1])
    lighting = lax.optimization_barrier(jnp.sum(probe_real * probe_real + probe_imag * probe_imag, axis=0))
    grad_real = jnp.zeros((MODES, PATCH, PATCH), jnp.float32)
    grad_imag = jnp.zeros((MODES, PATCH, PATCH), jnp.float32)
    power_total = jnp.zeros((PATCH, PATCH), jnp.float32)
    device_rows = jnp.arange(GRID_ROWS, dtype=jnp.int32)[:, None, None] * TILE
    device_cols = jnp.arange(GRID_COLS, dtype=jnp.int32)[None, :, None] * TILE
    blocks = GRID_ROWS * GRID_COLS
    zero_start = jnp.zeros((), jnp.int32)
    current_object = object_field
    for batch_index in range(BATCHES):
        padded = jnp.pad(current_object, ((0, 0), (half_patch, half_patch), (half_patch, half_patch)))
        row_starts = (device_rows + offsets[:, :, batch_index, :, 0] + half_patch).reshape(-1).astype(jnp.int32)
        col_starts = (device_cols + offsets[:, :, batch_index, :, 1] + half_patch).reshape(-1).astype(jnp.int32)

        def one_patch(row_start, col_start):
            return lax.dynamic_slice(padded, (zero_start, row_start, col_start), (2, PATCH, PATCH))
        patches = jax.vmap(one_patch)(row_starts, col_starts)
        measured = amplitudes[:, :, batch_index].reshape(blocks, POS_DEV, PATCH, PATCH)

        def per_block(pieces):
            block_patches, block_measured = pieces
            return patch_terms(block_patches[:, 0], block_patches[:, 1], probe_real, probe_imag, block_measured, table_real, table_imag)
        object_real, object_imag, block_real, block_imag, block_power = lax.map(per_block, (patches.reshape(blocks, POS_DEV, 2, PATCH, PATCH), measured))
        grad_real = grad_real + lax.optimization_barrier(jnp.sum(block_real, axis=0))
        grad_imag = grad_imag + lax.optimization_barrier(jnp.sum(block_imag, axis=0))
        power_total = power_total + lax.optimization_barrier(jnp.sum(block_power, axis=0))
        object_real = object_real.reshape(-1, PATCH, PATCH)
        object_imag = object_imag.reshape(-1, PATCH, PATCH)
        stacked = jnp.stack([object_real, object_imag, jnp.broadcast_to(lighting, object_real.shape)], axis=1)
        buffer = jnp.zeros((3, ROWS_ALL + PATCH, COLS_ALL + PATCH), jnp.float32)

        def add_patch(position, current):
            corner = (zero_start, row_starts[position].astype(jnp.int32), col_starts[position].astype(jnp.int32))
            region = lax.dynamic_slice(current, corner, (3, PATCH, PATCH))
            return lax.dynamic_update_slice(current, region + stacked[position], corner)
        buffer = lax.fori_loop(0, stacked.shape[0], add_patch, buffer)
        center = buffer[:, half_patch:half_patch + ROWS_ALL, half_patch:half_patch + COLS_ALL]
        current_object = current_object + center[0:2] / (center[2] + OBJECT_REG)
    root_power = jnp.sqrt(power_total + PROBE_REG)
    probe_step = jnp.stack([grad_real / root_power, grad_imag / root_power])
    return (current_object, probe_step)
```

```python
import functools
import math

import jax
import jax.numpy as jnp
import numpy as np
from jax import lax
from jax.experimental import pallas as pl
from jax.experimental.pallas import tpu as pltpu
from jax.sharding import PartitionSpec as P

AMP_FLOOR = 0.25
OBJECT_REG = 0.5
PROBE_REG = 1.0
MARK = 4096.0
F32 = jnp.float32
BF16 = jnp.bfloat16
LIMIT = 28 * 1024 * 1024


def tables(n):
    k = np.arange(n)
    angle = (np.outer(k, k) % n) * (2.0 * math.pi / n)
    re, im = np.cos(angle) / math.sqrt(n), -np.sin(angle) / math.sqrt(n)
    right = np.block([[re, im], [-im, re]]).astype(np.float32)
    left = np.block([[re, -im], [im, re]]).astype(np.float32)
    both = np.stack([right, left])
    high = both.astype(jnp.bfloat16)
    low = (both - high.astype(np.float32)).astype(jnp.bfloat16)
    return jnp.asarray(np.stack([high, low]))


def call(kernel, out, *args, smem=0, scratch=(), flops=0, aliases=None):
    vmem = pl.BlockSpec(memory_space=pltpu.VMEM)
    specs = [pl.BlockSpec(memory_space=pltpu.SMEM)] * smem + [vmem] * (len(args) - smem)
    nbytes = sum(math.prod(o.shape) * 4 for o in out) + sum(a.size * 4 for a in args)
    return pl.pallas_call(
        kernel,
        out_shape=tuple(out),
        in_specs=specs,
        out_specs=tuple([vmem] * len(out)),
        scratch_shapes=list(scratch),
        input_output_aliases=aliases or {},
        compiler_params=pltpu.CompilerParams(vmem_limit_bytes=LIMIT),
        cost_estimate=pl.CostEstimate(flops=flops, bytes_accessed=nbytes, transcendentals=0),
    )(*args)


def shape(*dims):
    return jax.ShapeDtypeStruct(dims, F32)


def split(x):
    high = x.astype(BF16)
    return high, (x - high.astype(F32)).astype(BF16)


def mm(a, b):
    return jnp.dot(a, b, preferred_element_type=F32)


def by_right(x, tab, which):
    high, low = split(x)
    t, u = tab[0, which], tab[1, which]
    return mm(high, t) + (mm(low, t) + mm(high, u))


def by_left(x, tab, which):
    high, low = split(x)
    t, u = tab[0, which], tab[1, which]
    return mm(t, high) + (mm(t, low) + mm(u, high))


def placed(value, down, right):
    n = value.shape[0]
    wide = pltpu.roll(jnp.concatenate([value, jnp.zeros_like(value)], axis=1), right, 1)
    return pltpu.roll(jnp.concatenate([wide, jnp.zeros((8, 2 * n), F32)], axis=0), down, 0)


def positions(batch, offs, ext, probe, amps, tab, terms, grads, first):
    _, modes, n, _ = probe.shape
    half = n // 2
    terms[...] = jnp.zeros_like(terms)
    if first:
        grads[...] = jnp.zeros_like(grads)

    def one(p, carry):
        row = offs[batch, p, 0] + half
        col = offs[batch, p, 1] + half
        block = jnp.minimum(col // n, ext.shape[2] // n - 2)
        base = pl.multiple_of(block * n, n)
        shift = col - base
        top = pl.multiple_of(jnp.minimum(row // 8, (ext.shape[1] - n) // 8 - 1) * 8, 8)
        down = row - top
        at = (pl.ds(top, n + 8), pl.ds(base, 2 * n))

        def cut(ch):
            wide = pltpu.roll(ext[(ch,) + at], n + 8 - down, 0)[:n]
            return pltpu.roll(wide, 2 * n - shift, 1)[:, :n]

        pr, pi = cut(0), cut(1)
        waves = []
        for m in range(modes):
            qr, qi = probe[0, m], probe[1, m]
            waves.append(jnp.concatenate([qr * pr - qi * pi, qr * pi + qi * pr], axis=1))
        y = by_right(jnp.concatenate(waves, axis=0), tab, 0)
        z = jnp.concatenate(
            [
                jnp.concatenate([y[m * n : (m + 1) * n, :n] for m in range(modes)], axis=1),
                jnp.concatenate([y[m * n : (m + 1) * n, n:] for m in range(modes)], axis=1),
            ],
            axis=0,
        )
        far = by_left(z, tab, 1)
        square = far * far
        square = square[:n] + square[n:]
        intensity = square[:, :n]
        for m in range(1, modes):
            intensity = intensity + square[:, m * n : (m + 1) * n]
        factor = amps[p] / jnp.maximum(jnp.sqrt(intensity), AMP_FLOOR) - 1.0
        wide = jnp.concatenate([factor] * modes, axis=1)
        h = by_left(far * jnp.concatenate([wide, wide], axis=0), tab, 0)
        h = jnp.concatenate(
            [
                jnp.concatenate([h[:n, m * n : (m + 1) * n], h[n:, m * n : (m + 1) * n]], axis=1)
                for m in range(modes)
            ],
            axis=0,
        )
        change = by_right(h, tab, 1)
        tr = ti = None
        for m in range(modes):
            cr, ci = change[m * n : (m + 1) * n, :n], change[m * n : (m + 1) * n, n:]
            qr, qi = probe[0, m], probe[1, m]
            ar, ai = qr * cr + qi * ci, qr * ci - qi * cr
            tr, ti = (ar, ai) if tr is None else (tr + ar, ti + ai)
            grads[m] = grads[m] + (pr * cr + pi * ci)
            grads[modes + m] = grads[modes + m] + (pr * ci - pi * cr)
        grads[2 * modes] = grads[2 * modes] + (pr * pr + pi * pi)
        for ch, t in ((0, tr), (1, ti)):
            terms[(ch,) + at] = terms[(ch,) + at] + placed(t, down, shift)
        return carry

    lax.fori_loop(0, amps.shape[0], one, 0)


def halo_kernel(offs_own, tile, above, below, left_out, right_out):
    rows, cols = tile.shape[1:]
    half = above.shape[1] - 8
    for out, cut in ((left_out, slice(0, 2 * half)), (right_out, slice(cols - 2 * half, cols))):
        lane = lax.broadcasted_iota(jnp.int32, (1, 2 * half), 1)
        keep = lane < half

        def pack(re, im):
            if out is left_out:
                return jnp.where(keep, re, pltpu.roll(im, half, 1))
            return jnp.where(keep, pltpu.roll(re, half, 1), im)

        out[:half] = pack(above[0, :half, cut], above[1, :half, cut])
        out[half : half + rows] = pack(tile[0, :, cut], tile[1, :, cut])
        out[half + rows : 2 * half + rows] = pack(below[0, :half, cut], below[1, :half, cut])
        out[2 * half + rows : 2 * half + rows + 8] = offs_own[...]
        out[2 * half + rows + 1 : 2 * half + rows + 2] = above[0, half : half + 1, : 2 * half]
        out[2 * half + rows + 2 : 2 * half + rows + 3] = below[0, half : half + 1, : 2 * half]


def put_halo(ext, tile, above, below, from_left, from_right):
    rows, cols = tile.shape[1:]
    half = above.shape[1] - 8
    lane = lax.broadcasted_iota(jnp.int32, (1, 2 * half), 1)
    keep = lane < half
    for ch in range(2):
        body = jnp.concatenate([above[ch, :half], tile[ch], below[ch, :half]], axis=0)
        lf, rt = from_left[: 2 * half + rows], from_right[: 2 * half + rows]
        lf = lf if ch == 0 else pltpu.roll(lf, half, 1)
        rt = rt if ch == 1 else pltpu.roll(rt, half, 1)
        tiles = [body[:, k * 2 * half : (k + 1) * 2 * half] for k in range(cols // (2 * half))]
        turned = [lf] + [pltpu.roll(t, half, 1) for t in tiles] + [rt]
        for k in range(len(turned) - 1):
            ext[ch, :, k * 2 * half : (k + 1) * 2 * half] = jnp.where(keep, turned[k], turned[k + 1])


def first_kernel(modes, offs, tile, above, below, from_left, from_right, probe, amps, tab,
                 ext, top, mid, bottom, grads, terms):
    n = probe.shape[2]
    put_halo(ext, tile, above, below, from_left, from_right)
    positions(0, offs, ext, probe, amps, tab, terms, grads, True)
    give_terms(n, terms, top, mid, bottom)


def give_terms(n, terms, top, mid, bottom):
    rows = terms.shape[1]
    top[...] = terms[:, :n]
    mid[...] = terms[:, n : rows - n]
    bottom[...] = terms[:, rows - n :]


def update(ext, old, weight, parts, from_left, from_right):
    left, middle, right = parts
    n = left.shape[2]
    cols = old.shape[2]
    for ch in range(2):
        ext[ch, :, :n] = old[ch, :, :n] + (left[ch] + from_left[ch]) * weight[:, :n]
        ext[ch, :, n : cols - n] = old[ch, :, n : cols - n] + middle[ch] * weight[:, n : cols - n]
        ext[ch, :, cols - n :] = old[ch, :, cols - n :] + (right[ch] + from_right[ch]) * weight[:, cols - n :]


def next_kernel(batch, offs, old, weight, left, middle, right, from_left, from_right, probe, amps, tab, grads_in,
                ext, top, mid, bottom, grads, terms):
    n = probe.shape[2]
    update(ext, old, weight, (left, middle, right), from_left, from_right)
    grads[...] = grads_in[...]
    positions(batch, offs, ext, probe, amps, tab, terms, grads, False)
    give_terms(n, terms, top, mid, bottom)


def row_kernel(top, mid, bottom, above, below, left, middle, right):
    n = top.shape[1]
    rows = 2 * n + mid.shape[1]
    cols = top.shape[2]
    for out, cut in ((left, slice(0, n)), (middle, slice(n, cols - n)), (right, slice(cols - n, cols))):
        out[:, :n] = top[:, :, cut] + above[:, :, cut]
        out[:, n : rows - n] = mid[:, :, cut]
        out[:, rows - n :] = bottom[:, :, cut] + below[:, :, cut]


def light_kernel(batch, around, probe, weight, light):
    _, modes, n, _ = probe.shape
    half = n // 2
    rows, cols = weight.shape
    tile_r, tile_c = rows - n, cols - n
    pos = around.shape[2]
    lit = None
    for m in range(modes):
        s = probe[0, m] * probe[0, m] + probe[1, m] * probe[1, m]
        lit = s if lit is None else lit + s
    light[...] = jnp.zeros_like(light)
    big = int(MARK)

    def one(i, carry):
        k, p = i // pos, i % pos
        there = around[k, batch, p, 0] > 0
        row = around[k, batch, p, 0] - big + half + (k // 3 - 1) * tile_r
        col = around[k, batch, p, 1] - big + half + (k % 3 - 1) * tile_c
        hit = there & (row > -n) & (row < rows) & (col > -n) & (col < cols)

        @pl.when(hit)
        def _():
            base = pl.multiple_of((col + n) // n * n, n)
            top = pl.multiple_of((row + n) // 8 * 8, 8)
            at = (pl.ds(top, n + 8), pl.ds(base, 2 * n))
            light[at] = light[at] + placed(lit, row + n - top, col + n - base)

        return carry

    lax.fori_loop(0, 9 * pos, one, 0)
    r = lax.broadcasted_iota(jnp.int32, (rows, cols), 0)
    c = lax.broadcasted_iota(jnp.int32, (rows, cols), 1)
    low_r = jnp.where(around[1, 0, 0, 0] > 0, 0, half)
    high_r = jnp.where(around[7, 0, 0, 0] > 0, rows, rows - half)
    low_c = jnp.where(around[3, 0, 0, 0] > 0, 0, half)
    high_c = jnp.where(around[5, 0, 0, 0] > 0, cols, cols - half)
    inside = (r >= low_r) & (r < high_r) & (c >= low_c) & (c < high_c)
    total = light[n : n + rows, n : n + cols]
    weight[...] = jnp.where(inside, 1.0 / (total + OBJECT_REG), 0.0)


def object_kernel(old, weight, left, middle, right, from_left, from_right, out, ext):
    n = left.shape[2]
    half = n // 2
    update(ext, old, weight, (left, middle, right), from_left, from_right)
    rows, cols = out.shape[1:]
    lane = lax.broadcasted_iota(jnp.int32, (1, n), 1)
    for ch in range(2):
        body = ext[ch, half : half + rows]
        turned = [pltpu.roll(body[:, k * n : (k + 1) * n], half, 1) for k in range(cols // n + 1)]
        for k in range(cols // n):
            out[ch, :, k * n : (k + 1) * n] = jnp.where(lane < half, turned[k], turned[k + 1])


def step_kernel(parts, out):
    total = parts[0]
    for i in range(1, parts.shape[0]):
        total = total + parts[i]
    each = total.shape[0] - out.shape[1]
    maps = total.shape[0] // each
    scale = 1.0 / jnp.sqrt(total[(maps - 1) * each :] + PROBE_REG)
    step = jnp.concatenate([total[m * each : (m + 1) * each] * scale for m in range(maps - 1)], axis=0)
    for i in range(out.shape[0]):
        out[i] = step


def shifted(value, axis, by):
    size = lax.axis_size(axis)
    return lax.ppermute(value, axis, [(i, i + by) for i in range(size) if 0 <= i + by < size])


def all_sum(grads):
    maps, n, _ = grads.shape
    axes = ("row", "col")
    devices = lax.axis_size("row") * lax.axis_size("col")
    if n % devices:
        total = lax.psum(grads, axes)
        return total[:-1] / jnp.sqrt(total[-1] + PROBE_REG)
    each = n // devices
    parts = grads.reshape(maps, devices, each, n).transpose(1, 0, 2, 3).reshape(devices, maps * each, n)
    parts = lax.all_to_all(parts, axes, 0, 0, tiled=True)
    (steps,) = call(step_kernel, [shape(devices, (maps - 1) * each, n)], parts)
    steps = lax.all_to_all(steps, axes, 0, 0, tiled=True)
    return steps.reshape(devices, maps - 1, each, n).transpose(1, 0, 2, 3).reshape(maps - 1, n, n)


def on_device(tile, probe, amplitudes, offsets):
    _, modes, n, _ = probe.shape
    half = n // 2
    _, rows, cols = tile.shape
    amps = amplitudes[0, 0]
    offs = offsets[0, 0]
    batches, pos = offs.shape[:2]
    count = batches * pos * 2
    tab = tables(n)
    fft_flops = pos * modes * 2 * 2 * 4 * 2 * n**3 * 3

    coded = offs.astype(F32).reshape(count) + MARK
    block = jnp.zeros((2, 8, cols), F32).at[0, 0, :count].set(coded)
    above = shifted(jnp.concatenate([tile[:, rows - half :], block], axis=1), "row", 1)
    below = shifted(jnp.concatenate([tile[:, :half], block], axis=1), "row", -1)
    own_rows = jnp.zeros((8, n), F32).at[0, :count].set(coded)
    to_left, to_right = call(halo_kernel, [shape(rows + n + 8, n)] * 2, own_rows, tile, above, below)
    from_right = shifted(to_left, "col", -1)
    from_left = shifted(to_right, "col", 1)

    big = [shape(2, rows + n, cols + n), shape(2, n, cols + n), shape(2, rows - n, cols + n), shape(2, n, cols + n),
           shape(2 * modes + 1, n, n)]
    scratch = [pltpu.VMEM((2, rows + n, cols + n), F32)]
    ext, top, mid, bottom, grads = call(
        functools.partial(first_kernel, modes), big, offs, tile, above, below, from_left, from_right, probe, amps[0], tab,
        smem=1, scratch=scratch, flops=fft_flops,
    )

    (above, below, from_left, from_right, own_rows, top) = lax.optimization_barrier(
        (above, below, from_left, from_right, own_rows, top)
    )
    end = rows + n
    around = jnp.stack([
        from_left[end + 1, :count], above[0, half, :count], from_right[end + 1, :count],
        from_left[end, :count], own_rows[0, :count], from_right[end, :count],
        from_left[end + 2, :count], below[0, half, :count], from_right[end + 2, :count],
    ]).astype(jnp.int32).reshape(9, batches, pos, 2)

    for batch in range(batches):
        above = shifted(bottom, "row", 1)
        below = shifted(top, "row", -1)
        around, top = lax.optimization_barrier((around, top))
        (weight,) = call(
            functools.partial(light_kernel, batch), [shape(rows + n, cols + n)], around, probe, smem=1,
            scratch=[pltpu.VMEM((rows + 3 * n, cols + 3 * n), F32)], flops=10**9,
        )
        left, middle, right = call(
            row_kernel, [shape(2, rows + n, n), shape(2, rows + n, cols - n), shape(2, rows + n, n)],
            top, mid, bottom, above, below,
        )
        from_right = shifted(left, "col", -1)
        from_left = shifted(right, "col", 1)
        if batch + 1 < batches:
            ext, top, mid, bottom, grads = call(
                functools.partial(next_kernel, batch + 1), big, offs, ext, weight, left, middle, right,
                from_left, from_right, probe, amps[batch + 1], tab, grads, smem=1, scratch=scratch, flops=fft_flops,
            )
    probe_step = all_sum(grads).reshape(2, modes, n, n)
    (object_new,) = call(
        object_kernel, [shape(2, rows, cols)], ext, weight, left, middle, right, from_left, from_right,
        scratch=scratch,
    )
    return object_new, probe_step


def solution(mesh):
    placed = (
        P(None, "row", "col"),
        P(),
        P("row", "col", None, None, None, None),
        P("row", "col", None, None, None),
    )
    return jax.shard_map(
        on_device,
        mesh=mesh,
        in_specs=placed,
        out_specs=(P(None, "row", "col"), P()),
        check_vma=False,
    )
```

```python
import functools
import math

import jax
import jax.numpy as jnp
import numpy as np
from jax import lax
from jax.experimental import pallas as pl
from jax.experimental.pallas import tpu as pltpu
from jax.sharding import PartitionSpec as P

AMP_FLOOR = 0.25
OBJECT_REG = 0.5
PROBE_REG = 1.0
MARK = 4096.0
F32 = jnp.float32
BF16 = jnp.bfloat16
LIMIT = 28 * 1024 * 1024


def tables(n):
    k = np.arange(n)
    angle = (np.outer(k, k) % n) * (2.0 * math.pi / n)
    re, im = np.cos(angle) / math.sqrt(n), -np.sin(angle) / math.sqrt(n)
    right = np.block([[re, im], [-im, re]]).astype(np.float32)
    left = np.block([[re, -im], [im, re]]).astype(np.float32)
    both = np.stack([right, left])
    high = both.astype(jnp.bfloat16)
    low = (both - high.astype(np.float32)).astype(jnp.bfloat16)
    return jnp.asarray(np.stack([high, low]))


def call(kernel, out, *args, smem=0, scratch=(), flops=0, aliases=None):
    vmem = pl.BlockSpec(memory_space=pltpu.VMEM)
    specs = [pl.BlockSpec(memory_space=pltpu.SMEM)] * smem + [vmem] * (len(args) - smem)
    nbytes = sum(math.prod(o.shape) * 4 for o in out) + sum(a.size * 4 for a in args)
    return pl.pallas_call(
        kernel,
        out_shape=tuple(out),
        in_specs=specs,
        out_specs=tuple([vmem] * len(out)),
        scratch_shapes=list(scratch),
        input_output_aliases=aliases or {},
        compiler_params=pltpu.CompilerParams(vmem_limit_bytes=LIMIT),
        cost_estimate=pl.CostEstimate(flops=flops, bytes_accessed=nbytes, transcendentals=0),
    )(*args)


def shape(*dims):
    return jax.ShapeDtypeStruct(dims, F32)


def split(x):
    high = x.astype(BF16)
    return high, (x - high.astype(F32)).astype(BF16)


def mm(a, b):
    return jnp.dot(a, b, preferred_element_type=F32)


def by_right(x, tab, which):
    high, low = split(x)
    t, u = tab[0, which], tab[1, which]
    return mm(high, t) + (mm(low, t) + mm(high, u))


def by_left(x, tab, which):
    high, low = split(x)
    t, u = tab[0, which], tab[1, which]
    return mm(t, high) + (mm(t, low) + mm(u, high))


def placed(value, down, right):
    n = value.shape[0]
    wide = pltpu.roll(jnp.concatenate([value, jnp.zeros_like(value)], axis=1), right, 1)
    return pltpu.roll(jnp.concatenate([wide, jnp.zeros((8, 2 * n), F32)], axis=0), down, 0)


def positions(batch, offs, ext, probe, amps, tab, terms, grads, first):
    _, modes, n, _ = probe.shape
    half = n // 2
    terms[...] = jnp.zeros_like(terms)
    if first:
        grads[...] = jnp.zeros_like(grads)

    def one(p, carry):
        row = offs[batch, p, 0] + half
        col = offs[batch, p, 1] + half
        block = jnp.minimum(col // n, ext.shape[2] // n - 2)
        base = pl.multiple_of(block * n, n)
        shift = col - base
        top = pl.multiple_of(jnp.minimum(row // 8, (ext.shape[1] - n) // 8 - 1) * 8, 8)
        down = row - top
        at = (pl.ds(top, n + 8), pl.ds(base, 2 * n))

        def cut(ch):
            wide = pltpu.roll(ext[(ch,) + at], n + 8 - down, 0)[:n]
            return pltpu.roll(wide, 2 * n - shift, 1)[:, :n]

        pr, pi = cut(0), cut(1)
        waves = []
        for m in range(modes):
            qr, qi = probe[0, m], probe[1, m]
            waves.append(jnp.concatenate([qr * pr - qi * pi, qr * pi + qi * pr], axis=1))
        y = by_right(jnp.concatenate(waves, axis=0), tab, 0)
        z = jnp.concatenate(
            [
                jnp.concatenate([y[m * n : (m + 1) * n, :n] for m in range(modes)], axis=1),
                jnp.concatenate([y[m * n : (m + 1) * n, n:] for m in range(modes)], axis=1),
            ],
            axis=0,
        )
        far = by_left(z, tab, 1)
        square = far * far
        square = square[:n] + square[n:]
        intensity = square[:, :n]
        for m in range(1, modes):
            intensity = intensity + square[:, m * n : (m + 1) * n]
        factor = amps[p] / jnp.maximum(jnp.sqrt(intensity), AMP_FLOOR) - 1.0
        wide = jnp.concatenate([factor] * modes, axis=1)
        h = by_left(far * jnp.concatenate([wide, wide], axis=0), tab, 0)
        h = jnp.concatenate(
            [
                jnp.concatenate([h[:n, m * n : (m + 1) * n], h[n:, m * n : (m + 1) * n]], axis=1)
                for m in range(modes)
            ],
            axis=0,
        )
        change = by_right(h, tab, 1)
        tr = ti = None
        for m in range(modes):
            cr, ci = change[m * n : (m + 1) * n, :n], change[m * n : (m + 1) * n, n:]
            qr, qi = probe[0, m], probe[1, m]
            ar, ai = qr * cr + qi * ci, qr * ci - qi * cr
            tr, ti = (ar, ai) if tr is None else (tr + ar, ti + ai)
            grads[m] = grads[m] + (pr * cr + pi * ci)
            grads[modes + m] = grads[modes + m] + (pr * ci - pi * cr)
        grads[2 * modes] = grads[2 * modes] + (pr * pr + pi * pi)
        for ch, t in ((0, tr), (1, ti)):
            terms[(ch,) + at] = terms[(ch,) + at] + placed(t, down, shift)
        return carry

    lax.fori_loop(0, amps.shape[0], one, 0)


def parity(axis):
    return lax.axis_index(axis) % 2


def ends(axis, length, width):
    near = (1 - parity(axis)) * (length - width)
    return pl.multiple_of(near, width), pl.multiple_of(length - width - near, width)


def lower(n):
    return lax.broadcasted_iota(jnp.int32, (1, n), 1) < n // 2


def pack_sides(re_low, im_low, re_high, im_high):
    half = re_low.shape[1] // 2
    keep = lower(2 * half)
    left = jnp.where(keep, re_low, pltpu.roll(im_low, half, 1))
    right = jnp.where(keep, pltpu.roll(re_high, half, 1), im_high)
    even = parity("col") == 0
    return jnp.where(even, right, left), jnp.where(even, left, right)


def by_side(first, second):
    even = parity("col") == 0
    return jnp.where(even, second, first), jnp.where(even, first, second)


def send_kernel(coded, tile, rows_1, rows_2, cols_1, cols_2):
    _, rows, cols = tile.shape
    n = coded.shape[1]
    half = n // 2
    for out, at in zip((rows_1, rows_2), ends("row", rows, half)):
        out[:, :half] = tile[:, pl.ds(at, half)]
        out[:, half:] = jnp.zeros((2, 8, cols), F32)
        out[0, half:, :n] = coded[...]
    first, second = pack_sides(tile[0, :, :n], tile[1, :, :n], tile[0, :, cols - n :], tile[1, :, cols - n :])
    for out, value in ((cols_1, first), (cols_2, second)):
        out[:rows] = value
        out[rows:] = coded[...]


def corner_kernel(cols_1, cols_2, out_1, out_2):
    n = cols_1.shape[1]
    half = n // 2
    rows = cols_1.shape[0] - 8
    for out, at in zip((out_1, out_2), ends("row", rows, half)):
        for k, ref in enumerate((cols_1, cols_2)):
            out[k, :half] = ref[pl.ds(at, half)]
            out[k, half:] = ref[rows:]


def put_halo(ext, tile, rows_1, rows_2, cols_1, cols_2, corner_1, corner_2):
    _, rows, cols = tile.shape
    n = cols_1.shape[1]
    half = n // 2
    keep = lower(n)
    even = parity("row") == 0
    above = jnp.where(even, rows_2[:, :half], rows_1[:, :half])
    below = jnp.where(even, rows_1[:, :half], rows_2[:, :half])
    strips = []
    for k, ref in enumerate((cols_1, cols_2)):
        c1, c2 = corner_1[k, :half], corner_2[k, :half]
        strips.append(jnp.concatenate([jnp.where(even, c2, c1), ref[:rows], jnp.where(even, c1, c2)], axis=0))
    left, right = by_side(*strips)
    for ch in range(2):
        body = jnp.concatenate([above[ch], tile[ch], below[ch]], axis=0)
        lf = left if ch == 0 else pltpu.roll(left, half, 1)
        rt = right if ch == 1 else pltpu.roll(right, half, 1)
        turned = [lf] + [pltpu.roll(body[:, k : k + n], half, 1) for k in range(0, cols, n)] + [rt]
        for k in range(len(turned) - 1):
            ext[ch, :, k * n : (k + 1) * n] = jnp.where(keep, turned[k], turned[k + 1])


def give(n, terms, cols_1, cols_2, mid_1, mid_2):
    _, rows, cols = terms.shape
    for out, at in zip((cols_1, cols_2), ends("col", cols, n)):
        out[...] = terms[:, :, pl.ds(at, n)]
    for out, at in zip((mid_1, mid_2), ends("row", rows, n)):
        out[...] = terms[:, pl.ds(at, n), n : cols - n]


def first_kernel(offs, tile, rows_1, rows_2, cols_1, cols_2, corner_1, corner_2, probe, amps, tab,
                 ext, terms, grads, *sends):
    put_halo(ext, tile, rows_1, rows_2, cols_1, cols_2, corner_1, corner_2)
    positions(0, offs, ext, probe, amps, tab, terms, grads, True)
    give(probe.shape[2], terms, *sends)


def side_kernel(terms, got_1, got_2, side_1, side_2, send_1, send_2):
    n = got_1.shape[2]
    _, rows, cols = terms.shape
    for side, got, at in zip((side_1, side_2), (got_1, got_2), ends("col", cols, n)):
        side[...] = terms[:, :, pl.ds(at, n)] + got[...]
    for out, at in zip((send_1, send_2), ends("row", rows, n)):
        for k, side in enumerate((side_1, side_2)):
            out[k] = side[:, pl.ds(at, n)]


def update(ext, old, weight, terms, side_1, side_2, mid_1, mid_2, ends_1, ends_2):
    n = side_1.shape[2]
    _, rows, cols = old.shape
    at_rows = ends("row", rows, n)
    inner = slice(n, cols - n)
    for ch in range(2):
        for k, (side, at) in enumerate(zip((side_1, side_2), ends("col", cols, n))):
            here = pl.ds(at, n)
            ext[ch, :, here] = old[ch, :, here] + side[ch] * weight[:, here]
            for got, top in zip((ends_1, ends_2), at_rows):
                there = pl.ds(top, n)
                ext[ch, there, here] = ext[ch, there, here] + got[k, ch] * weight[there, here]
        ext[ch, :, inner] = old[ch, :, inner] + terms[ch, :, inner] * weight[:, inner]
        for got, top in zip((mid_1, mid_2), at_rows):
            there = pl.ds(top, n)
            ext[ch, there, inner] = ext[ch, there, inner] + got[ch] * weight[there, inner]


def next_kernel(batch, offs, old, weight, old_terms, side_1, side_2, mid_1, mid_2, ends_1, ends_2, probe, amps, tab,
                grads_in, ext, terms, grads, *sends):
    update(ext, old, weight, old_terms, side_1, side_2, mid_1, mid_2, ends_1, ends_2)
    grads[...] = grads_in[...]
    positions(batch, offs, ext, probe, amps, tab, terms, grads, False)
    give(probe.shape[2], terms, *sends)


def last_kernel(batch, offs, old, weight, old_terms, side_1, side_2, mid_1, mid_2, ends_1, ends_2, probe, amps, tab,
                grads_in, ext, terms, keep, send, cols_1, cols_2, mids_1, mids_2, grads):
    n = probe.shape[2]
    half = n // 2
    update(ext, old, weight, old_terms, side_1, side_2, mid_1, mid_2, ends_1, ends_2)
    grads[...] = grads_in[...]
    positions(batch, offs, ext, probe, amps, tab, terms, grads, False)
    mine = pl.multiple_of(parity("col") * half, half)
    keep[...] = grads[:, pl.ds(mine, half)]
    send[...] = grads[:, pl.ds(pl.multiple_of(half - mine, half), half)]
    _, rows, cols = terms.shape
    first, second = pack_sides(terms[0, :, :n], terms[1, :, :n], terms[0, :, cols - n :], terms[1, :, cols - n :])
    cols_1[...] = first
    cols_2[...] = second
    for out, at in zip((mids_1, mids_2), ends("row", rows, half)):
        out[...] = terms[:, pl.ds(at, half), n : cols - n]


def last_side_kernel(terms, got_1, got_2, side, send_1, send_2):
    _, rows, cols = terms.shape
    n = got_1.shape[1]
    half = n // 2
    keep = lower(n)
    left, right = by_side(got_1[...], got_2[...])
    for ch in range(2):
        lf = pltpu.roll(left, half, 1) if ch == 0 else left
        rt = right if ch == 0 else pltpu.roll(right, half, 1)
        side[ch] = jnp.where(keep, terms[ch, :, cols - n :] + rt, terms[ch, :, :n] + lf)
    for out, at in zip((send_1, send_2), ends("row", rows, half)):
        out[...] = side[:, pl.ds(at, half)]


def object_kernel(old, weight, terms, side, mid_1, mid_2, ends_1, ends_2, out):
    _, rows, cols = old.shape
    n = side.shape[2]
    half = n // 2
    keep = lower(n)
    even = parity("row") == 0
    inner = slice(n, cols - n)
    own = slice(half, rows - half)
    tall = rows - n - 2 * half

    def tops(value, first, second):
        above, below = jnp.where(even, second, first), jnp.where(even, first, second)
        gap = jnp.zeros((tall, value.shape[1]), F32)
        return value + jnp.concatenate([above, gap, below], axis=0)

    for ch in range(2):
        edge = tops(side[ch, own], ends_1[ch], ends_2[ch])
        edge = jnp.where(keep, old[ch, own, cols - n :], old[ch, own, :n]) + edge * jnp.where(
            keep, weight[own, cols - n :], weight[own, :n])
        body = old[ch, own, inner] + tops(terms[ch, own, inner], mid_1[ch], mid_2[ch]) * weight[own, inner]
        edge = pltpu.roll(edge, half, 1)
        turned = [edge] + [pltpu.roll(body[:, k : k + n], half, 1) for k in range(0, cols - 2 * n, n)] + [edge]
        for k in range(len(turned) - 1):
            out[ch, :, k * n : (k + 1) * n] = jnp.where(keep, turned[k], turned[k + 1])


def light_kernel(batch, around, probe, weight, light):
    _, modes, n, _ = probe.shape
    half = n // 2
    rows, cols = weight.shape
    tile_r, tile_c = rows - n, cols - n
    pos = around.shape[2]
    lit = None
    for m in range(modes):
        s = probe[0, m] * probe[0, m] + probe[1, m] * probe[1, m]
        lit = s if lit is None else lit + s
    light[...] = jnp.zeros_like(light)
    big = int(MARK)

    def side(which, axis):
        step = 1 - 2 * parity(axis)
        return jnp.where(which == 0, 0, jnp.where(which == 1, step, -step))

    def one(i, carry):
        k, p = i // pos, i % pos
        there = around[k, batch, p, 0] > 0
        row = around[k, batch, p, 0] - big + half + side(k // 3, "row") * tile_r
        col = around[k, batch, p, 1] - big + half + side(k % 3, "col") * tile_c
        hit = there & (row > -n) & (row < rows) & (col > -n) & (col < cols)

        @pl.when(hit)
        def _():
            base = pl.multiple_of((col + n) // n * n, n)
            top = pl.multiple_of((row + n) // 8 * 8, 8)
            at = (pl.ds(top, n + 8), pl.ds(base, 2 * n))
            light[at] = light[at] + placed(lit, row + n - top, col + n - base)

        return carry

    lax.fori_loop(0, 9 * pos, one, 0)
    r = lax.broadcasted_iota(jnp.int32, (rows, cols), 0)
    c = lax.broadcasted_iota(jnp.int32, (rows, cols), 1)
    odd_r, odd_c = parity("row"), parity("col")
    low_r = jnp.where(around[6 - 3 * odd_r, 0, 0, 0] > 0, 0, half)
    high_r = jnp.where(around[3 + 3 * odd_r, 0, 0, 0] > 0, rows, rows - half)
    low_c = jnp.where(around[2 - odd_c, 0, 0, 0] > 0, 0, half)
    high_c = jnp.where(around[1 + odd_c, 0, 0, 0] > 0, cols, cols - half)
    inside = (r >= low_r) & (r < high_r) & (c >= low_c) & (c < high_c)
    total = light[n : n + rows, n : n + cols]
    weight[...] = jnp.where(inside, 1.0 / (total + OBJECT_REG), 0.0)


def parts_kernel(keep, got, parts):
    maps = keep.shape[0]
    each = parts.shape[1] // maps
    for m in range(maps):
        total = keep[m] + got[m]
        for i in range(parts.shape[0]):
            parts[i, m * each : (m + 1) * each] = total[i * each : (i + 1) * each]


def step_kernel(parts, out):
    total = parts[0]
    for i in range(1, parts.shape[0]):
        total = total + parts[i]
    each = total.shape[0] - out.shape[1]
    maps = total.shape[0] // each
    scale = 1.0 / jnp.sqrt(total[(maps - 1) * each :] + PROBE_REG)
    step = jnp.concatenate([total[m * each : (m + 1) * each] * scale for m in range(maps - 1)], axis=0)
    for i in range(out.shape[0]):
        out[i] = step


def join_kernel(mine, other, out):
    maps, n, _ = out.shape
    half = n // 2
    each = mine.shape[1] // maps
    at = pl.multiple_of(parity("col") * half, half)
    for ref, top in ((mine, at), (other, pl.multiple_of(half - at, half))):
        for m in range(maps):
            out[m, pl.ds(top, half)] = jnp.concatenate(
                [ref[i, m * each : (m + 1) * each] for i in range(ref.shape[0])], axis=0)


def swap(value, axis, phase):
    size = lax.axis_size(axis)
    pairs = [(i, i + 1) for i in range(phase, size - 1, 2)]
    return lax.ppermute(value, axis, pairs + [(j, i) for i, j in pairs])


def both(first, second, axis):
    return swap(first, axis, 0), swap(second, axis, 1)


def on_device(tile, probe, amplitudes, offsets):
    _, modes, n, _ = probe.shape
    half = n // 2
    _, rows, cols = tile.shape
    tall, wide = rows + n, cols + n
    amps = amplitudes[0, 0]
    offs = offsets[0, 0]
    batches, pos = offs.shape[:2]
    count = batches * pos * 2
    maps = 2 * modes + 1
    tab = tables(n)
    flops = pos * modes * 2 * 2 * 4 * 2 * n**3 * 3

    coded = offs.astype(F32).reshape(1, count) + MARK
    coded = jnp.pad(coded, ((0, 7), (0, n - count)))
    sends = call(send_kernel, [shape(2, half + 8, cols)] * 2 + [shape(rows + 8, n)] * 2, coded, tile)
    c1, c2 = both(*sends[2:], "col")
    r1, r2 = both(*sends[:2], "row")
    k1, k2 = both(*call(corner_kernel, [shape(2, half + 8, n)] * 2, c1, c2), "row")

    plain = [shape(2, tall, wide), shape(2, tall, wide), shape(maps, n, n)]
    messages = [shape(2, tall, n)] * 2 + [shape(2, n, cols - n)] * 2
    ext, terms, grads, *sends = call(
        first_kernel, plain + messages, offs, tile, r1, r2, c1, c2, k1, k2, probe, amps[0], tab, smem=1, flops=flops)

    coded, r1, r2, c1, c2, k1, k2, sends = lax.optimization_barrier((coded, r1, r2, c1, c2, k1, k2, sends))
    around = jnp.stack([
        coded[0, :count], c1[rows, :count], c2[rows, :count],
        r1[0, half, :count], k1[0, half, :count], k1[1, half, :count],
        r2[0, half, :count], k2[0, half, :count], k2[1, half, :count],
    ]).astype(jnp.int32).reshape(9, batches, pos, 2)

    for batch in range(batches):
        last = batch + 1 == batches
        c1, c2 = both(*sends[:2], "col")
        m1, m2 = both(*sends[2:4], "row")
        (weight,) = call(
            functools.partial(light_kernel, batch), [shape(tall, wide)], around, probe, smem=1,
            scratch=[pltpu.VMEM((tall + 2 * n, wide + 2 * n), F32)], flops=10**9)
        if last:
            side, *sends = call(last_side_kernel, [shape(2, tall, n)] + [shape(2, half, n)] * 2, terms, c1, c2)
            e1, e2 = both(*sends, "row")
            (object_new,) = call(object_kernel, [shape(2, rows, cols)], ext, weight, terms, side, m1, m2, e1, e2)
            break
        s1, s2, *sends = call(
            side_kernel, [shape(2, tall, n)] * 2 + [shape(2, 2, n, n)] * 2, terms, c1, c2)
        e1, e2 = both(*sends, "row")
        args = (offs, ext, weight, terms, s1, s2, m1, m2, e1, e2, probe, amps[batch + 1], tab, grads)
        if batch + 2 < batches:
            ext, terms, grads, *sends = call(
                functools.partial(next_kernel, batch + 1), plain + messages, *args, smem=1, flops=flops)
        else:
            ext, terms, keep, send, *sends = call(
                functools.partial(last_kernel, batch + 1),
                plain[:2] + [shape(maps, half, n)] * 2 + [shape(tall, n)] * 2 + [shape(2, half, cols - n)] * 2,
                *args, smem=1, flops=flops, scratch=[pltpu.VMEM((maps, n, n), F32)])
            probe_step = all_sum(keep, send)
    return object_new, probe_step.reshape(2, modes, n, n)


def all_sum(keep, send):
    maps, half, n = keep.shape
    axes = ("row", "col")
    across = lax.axis_size("col")
    devices = lax.axis_size("row") * across
    if across % 2 or half % (devices // 2):
        first = jnp.where(parity("col") == 0, keep, send)
        second = jnp.where(parity("col") == 0, send, keep)
        total = lax.psum(jnp.concatenate([first, second], axis=1), axes)
        return total[:-1] / jnp.sqrt(total[-1] + PROBE_REG)
    groups = [list(range(k, devices, 2)) for k in range(2)]
    each = 2 * half // devices
    (parts,) = call(parts_kernel, [shape(devices // 2, maps * each, n)], keep, swap(send, "col", 0))
    parts = lax.all_to_all(parts, axes, 0, 0, axis_index_groups=groups, tiled=True)
    (steps,) = call(step_kernel, [shape(devices // 2, (maps - 1) * each, n)], parts)
    steps = lax.all_to_all(steps, axes, 0, 0, axis_index_groups=groups, tiled=True)
    (out,) = call(join_kernel, [shape(maps - 1, n, n)], steps, swap(steps, "col", 0))
    return out


def solution(mesh):
    placed = (
        P(None, "row", "col"),
        P(),
        P("row", "col", None, None, None, None),
        P("row", "col", None, None, None),
    )
    return jax.shard_map(
        on_device,
        mesh=mesh,
        in_specs=placed,
        out_specs=(P(None, "row", "col"), P()),
        check_vma=False,
    )
```

```python
import functools
import math

import jax
import jax.numpy as jnp
import numpy as np
from jax import lax
from jax.experimental import pallas as pl
from jax.experimental.pallas import tpu as pltpu
from jax.sharding import PartitionSpec as P

AMP_FLOOR = 0.25
OBJECT_REG = 0.5
PROBE_REG = 1.0
MARK = 4096.0
F32 = jnp.float32
BF16 = jnp.bfloat16
LIMIT = 20 * 1024 * 1024


def tables(n):
    k = np.arange(n)
    angle = (np.outer(k, k) % n) * (2.0 * math.pi / n)
    re, im = np.cos(angle) / math.sqrt(n), -np.sin(angle) / math.sqrt(n)
    right = np.block([[re, im], [-im, re]]).astype(np.float32)
    left = np.block([[re, -im], [im, re]]).astype(np.float32)
    both = np.stack([right, left])
    high = both.astype(jnp.bfloat16)
    low = (both - high.astype(np.float32)).astype(jnp.bfloat16)
    return jnp.asarray(np.stack([high, low]))


def call(kernel, out, *args, smem=0, scratch=(), flops=0, aliases=None):
    vmem = pl.BlockSpec(memory_space=pltpu.VMEM)
    specs = [pl.BlockSpec(memory_space=pltpu.SMEM)] * smem + [vmem] * (len(args) - smem)
    nbytes = sum(math.prod(o.shape) * 4 for o in out) + sum(a.size * 4 for a in args)
    return pl.pallas_call(
        kernel,
        out_shape=tuple(out),
        in_specs=specs,
        out_specs=tuple([vmem] * len(out)),
        scratch_shapes=list(scratch),
        input_output_aliases=aliases or {},
        compiler_params=pltpu.CompilerParams(vmem_limit_bytes=LIMIT),
        cost_estimate=pl.CostEstimate(flops=flops, bytes_accessed=nbytes, transcendentals=0),
    )(*args)


def shape(*dims):
    return jax.ShapeDtypeStruct(dims, F32)


def split(x):
    high = x.astype(BF16)
    return high, (x - high.astype(F32)).astype(BF16)


def mm(a, b):
    return jnp.dot(a, b, preferred_element_type=F32)


def by_right(x, tab, which):
    high, low = split(x)
    t, u = tab[0, which], tab[1, which]
    return mm(high, t) + (mm(low, t) + mm(high, u))


def by_left(x, tab, which):
    high, low = split(x)
    t, u = tab[0, which], tab[1, which]
    return mm(t, high) + (mm(t, low) + mm(u, high))


def put(ref, lead, row, col, value):
    n = value.shape[0]
    tall, wide = ref.shape[len(lead) :]
    top = pl.multiple_of(jnp.minimum(row // 8, (tall - n) // 8 - 1) * 8, 8)
    base = pl.multiple_of(jnp.minimum(col // n, wide // n - 2) * n, n)
    down, right = row - top, col - base
    tiles = pltpu.roll(value.reshape(n // 8, 8, n), down & 7, 1)
    none = jnp.zeros((1, 8, n), F32)
    sub = lax.broadcasted_iota(jnp.int32, (1, 8, 1), 1)
    tiles = jnp.where(sub < down, jnp.concatenate([none, tiles], axis=0), jnp.concatenate([tiles, none], axis=0))
    moved = pltpu.roll(tiles.reshape(n + 8, n), right & (n - 1), 1)
    lane = lax.broadcasted_iota(jnp.int32, (1, n), 1)
    for at, here in ((base, lane >= right), (base + n, lane < right)):
        block = (*lead, pl.ds(top, n + 8), pl.ds(pl.multiple_of(at, n), n))
        ref[block] = ref[block] + jnp.where(here, moved, 0.0)


def cut(ref, lead, row, col, n):
    tall, wide = ref.shape[len(lead) :]
    top = pl.multiple_of(jnp.minimum(row // 8, (tall - n) // 8 - 1) * 8, 8)
    base = pl.multiple_of(jnp.minimum(col // n, wide // n - 2) * n, n)
    down, right = row - top, col - base
    lane = lax.broadcasted_iota(jnp.int32, (1, n), 1)
    left, after = (
        pltpu.roll(ref[(*lead, pl.ds(top, n + 8), pl.ds(pl.multiple_of(at, n), n))], (n - right) & (n - 1), 1)
        for at in (base, base + n)
    )
    tiles = jnp.where(lane < n - right, left, after).reshape(n // 8 + 1, 8, n)
    tiles = pltpu.roll(tiles, (8 - down) & 7, 1)
    sub = lax.broadcasted_iota(jnp.int32, (1, 8, 1), 1)
    return jnp.where(sub < 8 - down, tiles[:-1], tiles[1:]).reshape(n, n)


def positions(batch, offs, ext, probe, amps, tab, terms, grads, first):
    _, modes, n, _ = probe.shape
    half = n // 2
    terms[...] = jnp.zeros_like(terms)
    if first:
        grads[...] = jnp.zeros_like(grads)

    def one(p):
        row = offs[batch, p, 0] + half
        col = offs[batch, p, 1] + half
        pr, pi = cut(ext, (0,), row, col, n), cut(ext, (1,), row, col, n)
        waves = []
        for m in range(modes):
            qr, qi = probe[0, m], probe[1, m]
            waves.append(jnp.concatenate([qr * pr - qi * pi, qr * pi + qi * pr], axis=1))
        y = by_right(jnp.concatenate(waves, axis=0), tab, 0)
        z = jnp.concatenate(
            [
                jnp.concatenate([y[m * n : (m + 1) * n, :n] for m in range(modes)], axis=1),
                jnp.concatenate([y[m * n : (m + 1) * n, n:] for m in range(modes)], axis=1),
            ],
            axis=0,
        )
        far = by_left(z, tab, 1)
        square = far * far
        square = square[:n] + square[n:]
        intensity = square[:, :n]
        for m in range(1, modes):
            intensity = intensity + square[:, m * n : (m + 1) * n]
        factor = amps[batch, p] / jnp.maximum(jnp.sqrt(intensity), AMP_FLOOR) - 1.0
        wide = jnp.concatenate([factor] * modes, axis=1)
        h = by_left(far * jnp.concatenate([wide, wide], axis=0), tab, 0)
        h = jnp.concatenate(
            [
                jnp.concatenate([h[:n, m * n : (m + 1) * n], h[n:, m * n : (m + 1) * n]], axis=1)
                for m in range(modes)
            ],
            axis=0,
        )
        change = by_right(h, tab, 1)
        tr = ti = None
        for m in range(modes):
            cr, ci = change[m * n : (m + 1) * n, :n], change[m * n : (m + 1) * n, n:]
            qr, qi = probe[0, m], probe[1, m]
            ar, ai = qr * cr + qi * ci, qr * ci - qi * cr
            tr, ti = (ar, ai) if tr is None else (tr + ar, ti + ai)
            grads[m] = grads[m] + (pr * cr + pi * ci)
            grads[modes + m] = grads[modes + m] + (pr * ci - pi * cr)
        grads[2 * modes] = grads[2 * modes] + (pr * pr + pi * pi)
        put(terms, (0,), row, col, tr)
        put(terms, (1,), row, col, ti)

    for p in range(amps.shape[1]):
        one(p)


def parity(axis):
    return lax.axis_index(axis) % 2


def ends(axis, length, width):
    near = (1 - parity(axis)) * (length - width)
    return pl.multiple_of(near, width), pl.multiple_of(length - width - near, width)


def lower(n):
    return lax.broadcasted_iota(jnp.int32, (1, n), 1) < n // 2


def pack_sides(re_low, im_low, re_high, im_high):
    half = re_low.shape[1] // 2
    keep = lower(2 * half)
    left = jnp.where(keep, re_low, pltpu.roll(im_low, half, 1))
    right = jnp.where(keep, pltpu.roll(re_high, half, 1), im_high)
    even = parity("col") == 0
    return jnp.where(even, right, left), jnp.where(even, left, right)


def by_side(first, second):
    even = parity("col") == 0
    return jnp.where(even, second, first), jnp.where(even, first, second)


def send_kernel(offs, tile, rows_1, rows_2, cols_1, cols_2):
    _, rows, cols = tile.shape
    n = cols_1.shape[1]
    half = n // 2
    lane = lax.broadcasted_iota(jnp.int32, (8, n), 1)
    coded = jnp.zeros((8, n), jnp.int32)
    for i, index in enumerate(np.ndindex(offs.shape)):
        coded = jnp.where(lane == i, offs[index] + int(MARK), coded)
    coded = coded.astype(F32)
    for out, at in zip((rows_1, rows_2), ends("row", rows, half)):
        out[:, :half] = tile[:, pl.ds(at, half)]
        out[:, half:] = jnp.zeros((2, 8, cols), F32)
        out[0, half:, :n] = coded
    first, second = pack_sides(tile[0, :, :n], tile[1, :, :n], tile[0, :, cols - n :], tile[1, :, cols - n :])
    for out, value in ((cols_1, first), (cols_2, second)):
        out[:rows] = value
        out[rows:] = coded


def corner_kernel(cols_1, cols_2, out_1, out_2):
    n = cols_1.shape[1]
    half = n // 2
    rows = cols_1.shape[0] - 8
    for out, at in zip((out_1, out_2), ends("row", rows, half)):
        for k, ref in enumerate((cols_1, cols_2)):
            out[k, :half] = ref[pl.ds(at, half)]
            out[k, half:] = ref[rows:]


def put_halo(ext, tile, rows_1, rows_2, cols_1, cols_2, corner_1, corner_2):
    _, rows, cols = tile.shape
    n = cols_1.shape[1]
    half = n // 2
    keep = lower(n)
    even = parity("row") == 0
    above = jnp.where(even, rows_2[:, :half], rows_1[:, :half])
    below = jnp.where(even, rows_1[:, :half], rows_2[:, :half])
    strips = []
    for k, ref in enumerate((cols_1, cols_2)):
        c1, c2 = corner_1[k, :half], corner_2[k, :half]
        strips.append(jnp.concatenate([jnp.where(even, c2, c1), ref[:rows], jnp.where(even, c1, c2)], axis=0))
    left, right = by_side(*strips)
    for ch in range(2):
        body = jnp.concatenate([above[ch], tile[ch], below[ch]], axis=0)
        lf = left if ch == 0 else pltpu.roll(left, half, 1)
        rt = right if ch == 1 else pltpu.roll(right, half, 1)
        turned = [lf] + [pltpu.roll(body[:, k : k + n], half, 1) for k in range(0, cols, n)] + [rt]
        for k in range(len(turned) - 1):
            ext[ch, :, k * n : (k + 1) * n] = jnp.where(keep, turned[k], turned[k + 1])


def give(n, terms, cols_1, cols_2, mid_1, mid_2):
    _, rows, cols = terms.shape
    for out, at in zip((cols_1, cols_2), ends("col", cols, n)):
        out[...] = terms[:, :, pl.ds(at, n)]
    for out, at in zip((mid_1, mid_2), ends("row", rows, n)):
        out[...] = terms[:, pl.ds(at, n), n : cols - n]


def first_kernel(offs, tile, rows_1, rows_2, cols_1, cols_2, corner_1, corner_2, probe, amps, tab,
                 ext, terms, grads, *sends):
    put_halo(ext, tile, rows_1, rows_2, cols_1, cols_2, corner_1, corner_2)
    positions(0, offs, ext, probe, amps, tab, terms, grads, True)
    give(probe.shape[2], terms, *sends)


def side_kernel(terms, got_1, got_2, side_1, side_2, send_1, send_2):
    n = got_1.shape[2]
    _, rows, cols = terms.shape
    for side, got, at in zip((side_1, side_2), (got_1, got_2), ends("col", cols, n)):
        side[...] = terms[:, :, pl.ds(at, n)] + got[...]
    for out, at in zip((send_1, send_2), ends("row", rows, n)):
        for k, side in enumerate((side_1, side_2)):
            out[k] = side[:, pl.ds(at, n)]


def update(ext, old, weight, terms, side_1, side_2, mid_1, mid_2, ends_1, ends_2):
    n = side_1.shape[2]
    _, rows, cols = old.shape
    at_rows = ends("row", rows, n)
    inner = slice(n, cols - n)
    for ch in range(2):
        for k, (side, at) in enumerate(zip((side_1, side_2), ends("col", cols, n))):
            here = pl.ds(at, n)
            ext[ch, :, here] = old[ch, :, here] + side[ch] * weight[:, here]
            for got, top in zip((ends_1, ends_2), at_rows):
                there = pl.ds(top, n)
                ext[ch, there, here] = ext[ch, there, here] + got[k, ch] * weight[there, here]
        ext[ch, :, inner] = old[ch, :, inner] + terms[ch, :, inner] * weight[:, inner]
        for got, top in zip((mid_1, mid_2), at_rows):
            there = pl.ds(top, n)
            ext[ch, there, inner] = ext[ch, there, inner] + got[ch] * weight[there, inner]


def next_kernel(batch, offs, old, weight, old_terms, side_1, side_2, mid_1, mid_2, ends_1, ends_2, probe, amps, tab,
                grads_in, ext, terms, grads, *sends):
    update(ext, old, weight, old_terms, side_1, side_2, mid_1, mid_2, ends_1, ends_2)
    grads[...] = grads_in[...]
    positions(batch, offs, ext, probe, amps, tab, terms, grads, False)
    give(probe.shape[2], terms, *sends)


def last_kernel(batch, offs, old, weight, old_terms, side_1, side_2, mid_1, mid_2, ends_1, ends_2, probe, amps, tab,
                grads_in, ext, terms, keep, send, cols_1, cols_2, mids_1, mids_2, grads):
    n = probe.shape[2]
    half = n // 2
    update(ext, old, weight, old_terms, side_1, side_2, mid_1, mid_2, ends_1, ends_2)
    grads[...] = grads_in[...]
    positions(batch, offs, ext, probe, amps, tab, terms, grads, False)
    mine = pl.multiple_of(parity("col") * half, half)
    keep[...] = grads[:, pl.ds(mine, half)]
    send[...] = grads[:, pl.ds(pl.multiple_of(half - mine, half), half)]
    _, rows, cols = terms.shape
    first, second = pack_sides(terms[0, :, :n], terms[1, :, :n], terms[0, :, cols - n :], terms[1, :, cols - n :])
    cols_1[...] = first
    cols_2[...] = second
    for out, at in zip((mids_1, mids_2), ends("row", rows, half)):
        out[...] = terms[:, pl.ds(at, half), n : cols - n]


def last_side_kernel(terms, got_1, got_2, side, send_1, send_2):
    _, rows, cols = terms.shape
    n = got_1.shape[1]
    half = n // 2
    keep = lower(n)
    left, right = by_side(got_1[...], got_2[...])
    for ch in range(2):
        lf = pltpu.roll(left, half, 1) if ch == 0 else left
        rt = right if ch == 0 else pltpu.roll(right, half, 1)
        side[ch] = jnp.where(keep, terms[ch, :, cols - n :] + rt, terms[ch, :, :n] + lf)
    for out, at in zip((send_1, send_2), ends("row", rows, half)):
        out[...] = side[:, pl.ds(at, half)]


def object_kernel(old, weight, terms, side, mid_1, mid_2, ends_1, ends_2, out):
    _, rows, cols = old.shape
    n = side.shape[2]
    half = n // 2
    keep = lower(n)
    even = parity("row") == 0
    inner = slice(n, cols - n)
    own = slice(half, rows - half)
    tall = rows - n - 2 * half

    def tops(value, first, second):
        above, below = jnp.where(even, second, first), jnp.where(even, first, second)
        gap = jnp.zeros((tall, value.shape[1]), F32)
        return value + jnp.concatenate([above, gap, below], axis=0)

    for ch in range(2):
        edge = tops(side[ch, own], ends_1[ch], ends_2[ch])
        edge = jnp.where(keep, old[ch, own, cols - n :], old[ch, own, :n]) + edge * jnp.where(
            keep, weight[own, cols - n :], weight[own, :n])
        body = old[ch, own, inner] + tops(terms[ch, own, inner], mid_1[ch], mid_2[ch]) * weight[own, inner]
        edge = pltpu.roll(edge, half, 1)
        turned = [edge] + [pltpu.roll(body[:, k : k + n], half, 1) for k in range(0, cols - 2 * n, n)] + [edge]
        for k in range(len(turned) - 1):
            out[ch, :, k * n : (k + 1) * n] = jnp.where(keep, turned[k], turned[k + 1])


def light_kernel(batch, around, probe, weight, light):
    _, modes, n, _ = probe.shape
    half = n // 2
    rows, cols = weight.shape
    tile_r, tile_c = rows - n, cols - n
    pos = around.shape[2]
    lit = None
    for m in range(modes):
        s = probe[0, m] * probe[0, m] + probe[1, m] * probe[1, m]
        lit = s if lit is None else lit + s
    light[...] = jnp.zeros_like(light)
    big = int(MARK)

    def side(which, axis):
        step = 1 - 2 * parity(axis)
        return jnp.where(which == 0, 0, jnp.where(which == 1, step, -step))

    def one(i, carry):
        k, p = i // pos, i % pos
        there = around[k, batch, p, 0] > 0
        row = around[k, batch, p, 0] - big + half + side(k // 3, "row") * tile_r
        col = around[k, batch, p, 1] - big + half + side(k % 3, "col") * tile_c
        hit = there & (row > -n) & (row < rows) & (col > -n) & (col < cols)

        @pl.when(hit)
        def _():
            put(light, (), row + n, col + n, lit)

        return carry

    lax.fori_loop(0, 9 * pos, one, 0)
    r = lax.broadcasted_iota(jnp.int32, (rows, cols), 0)
    c = lax.broadcasted_iota(jnp.int32, (rows, cols), 1)
    odd_r, odd_c = parity("row"), parity("col")
    low_r = jnp.where(around[6 - 3 * odd_r, 0, 0, 0] > 0, 0, half)
    high_r = jnp.where(around[3 + 3 * odd_r, 0, 0, 0] > 0, rows, rows - half)
    low_c = jnp.where(around[2 - odd_c, 0, 0, 0] > 0, 0, half)
    high_c = jnp.where(around[1 + odd_c, 0, 0, 0] > 0, cols, cols - half)
    inside = (r >= low_r) & (r < high_r) & (c >= low_c) & (c < high_c)
    total = light[n : n + rows, n : n + cols]
    weight[...] = jnp.where(inside, 1.0 / (total + OBJECT_REG), 0.0)


def parts_kernel(keep, got, parts):
    maps = keep.shape[0]
    each = parts.shape[1] // maps
    for m in range(maps):
        total = keep[m] + got[m]
        for i in range(parts.shape[0]):
            parts[i, m * each : (m + 1) * each] = total[i * each : (i + 1) * each]


def step_kernel(parts, out):
    total = parts[0]
    for i in range(1, parts.shape[0]):
        total = total + parts[i]
    each = total.shape[0] - out.shape[1]
    maps = total.shape[0] // each
    scale = 1.0 / jnp.sqrt(total[(maps - 1) * each :] + PROBE_REG)
    step = jnp.concatenate([total[m * each : (m + 1) * each] * scale for m in range(maps - 1)], axis=0)
    for i in range(out.shape[0]):
        out[i] = step


def join_kernel(mine, other, out):
    maps, n, _ = out.shape
    half = n // 2
    each = mine.shape[1] // maps
    at = pl.multiple_of(parity("col") * half, half)
    for ref, top in ((mine, at), (other, pl.multiple_of(half - at, half))):
        for m in range(maps):
            out[m, pl.ds(top, half)] = jnp.concatenate(
                [ref[i, m * each : (m + 1) * each] for i in range(ref.shape[0])], axis=0)


def swap(value, axis, phase):
    size = lax.axis_size(axis)
    pairs = [(i, i + 1) for i in range(phase, size - 1, 2)]
    return lax.ppermute(value, axis, pairs + [(j, i) for i, j in pairs])


def both(first, second, axis):
    return swap(first, axis, 0), swap(second, axis, 1)


def on_device(tile, probe, amplitudes, offsets):
    _, modes, n, _ = probe.shape
    half = n // 2
    _, rows, cols = tile.shape
    tall, wide = rows + n, cols + n
    amps = amplitudes[0, 0]
    offs = offsets[0, 0]
    batches, pos = offs.shape[:2]
    count = batches * pos * 2
    maps = 2 * modes + 1
    tab = tables(n)
    flops = pos * modes * 2 * 2 * 4 * 2 * n**3 * 3

    sends = call(send_kernel, [shape(2, half + 8, cols)] * 2 + [shape(rows + 8, n)] * 2, offs, tile, smem=1)
    c1, c2 = both(*sends[2:], "col")
    r1, r2 = both(*sends[:2], "row")
    k1, k2 = both(*call(corner_kernel, [shape(2, half + 8, n)] * 2, c1, c2), "row")

    plain = [shape(2, tall, wide), shape(2, tall, wide), shape(maps, n, n)]
    messages = [shape(2, tall, n)] * 2 + [shape(2, n, cols - n)] * 2
    ext, terms, grads, *sends = call(
        first_kernel, plain + messages, offs, tile, r1, r2, c1, c2, k1, k2, probe, amps, tab, smem=1, flops=flops)

    around_offs, r1, r2, c1, c2, k1, k2, sends = lax.optimization_barrier((offs, r1, r2, c1, c2, k1, k2, sends))
    around = jnp.stack([
        around_offs.astype(F32).reshape(count) + MARK, c1[rows, :count], c2[rows, :count],
        r1[0, half, :count], k1[0, half, :count], k1[1, half, :count],
        r2[0, half, :count], k2[0, half, :count], k2[1, half, :count],
    ]).astype(jnp.int32).reshape(9, batches, pos, 2)

    def light(batch, around):
        return call(
            functools.partial(light_kernel, batch), [shape(tall, wide)], around, probe, smem=1,
            scratch=[pltpu.VMEM((tall + 2 * n, wide + 2 * n), F32)], flops=10**9)[0]

    weights = [light(batch, around) for batch in range(min(2, batches))]
    for batch in range(batches):
        c1, c2 = both(*sends[:2], "col")
        m1, m2 = both(*sends[2:4], "row")
        if batch + 1 == batches:
            break
        c1, c2, m1, m2 = lax.optimization_barrier((c1, c2, m1, m2))
        s1, s2, *sends = call(
            side_kernel, [shape(2, tall, n)] * 2 + [shape(2, 2, n, n)] * 2, terms, c1, c2)
        e1, e2 = both(*sends, "row")
        if len(weights) < batches and batch > 0:
            around, c1 = lax.optimization_barrier((around, c1))
            weights.append(light(batch + 1, around))
        terms, weights = lax.optimization_barrier((terms, weights))
        args = (offs, ext, weights[batch], terms, s1, s2, m1, m2, e1, e2, probe, amps, tab, grads)
        if batch + 2 < batches:
            ext, terms, grads, *sends = call(
                functools.partial(next_kernel, batch + 1), plain + messages, *args, smem=1, flops=flops)
        else:
            ext, terms, keep, send, *sends = call(
                functools.partial(last_kernel, batch + 1),
                plain[:2] + [shape(maps, half, n)] * 2 + [shape(tall, n)] * 2 + [shape(2, half, cols - n)] * 2,
                *args, smem=1, flops=flops, scratch=[pltpu.VMEM((maps, n, n), F32)])
            got = swap(send, "col", 0)
            got, sends = lax.optimization_barrier((got, sends))

    def rest(c1, c2, m1, m2):
        side, *sends = call(last_side_kernel, [shape(2, tall, n)] + [shape(2, half, n)] * 2, terms, c1, c2)
        e1, e2 = both(*sends, "row")
        return call(object_kernel, [shape(2, rows, cols)], ext, weights[-1], terms, side, m1, m2, e1, e2)[0]

    probe_step, object_new = all_sum(keep, send, got, (c1, c2, m1, m2), rest)
    return object_new, probe_step.reshape(2, modes, n, n)


def all_sum(keep, send, got, beside, rest):
    maps, half, n = keep.shape
    axes = ("row", "col")
    across = lax.axis_size("col")
    devices = lax.axis_size("row") * across
    if across % 2 or half % (devices // 2):
        first = jnp.where(parity("col") == 0, keep, send)
        second = jnp.where(parity("col") == 0, send, keep)
        total = lax.psum(jnp.concatenate([first, second], axis=1), axes)
        return total[:-1] / jnp.sqrt(total[-1] + PROBE_REG), rest(*beside)
    groups = [list(range(k, devices, 2)) for k in range(2)]
    each = 2 * half // devices
    (parts,) = call(parts_kernel, [shape(devices // 2, maps * each, n)], keep, got)
    parts = lax.all_to_all(parts, axes, 0, 0, axis_index_groups=groups, tiled=True)
    parts, beside = lax.optimization_barrier((parts, beside))
    (steps,) = call(step_kernel, [shape(devices // 2, (maps - 1) * each, n)], parts)
    steps, beside = lax.optimization_barrier((steps, beside))
    steps = lax.all_to_all(steps, axes, 0, 0, axis_index_groups=groups, tiled=True)
    object_new = rest(*beside)
    steps, object_new = lax.optimization_barrier((steps, object_new))
    (out,) = call(join_kernel, [shape(maps - 1, n, n)], steps, swap(steps, "col", 0))
    return out, object_new


def solution(mesh):
    placed = (
        P(None, "row", "col"),
        P(),
        P("row", "col", None, None, None, None),
        P("row", "col", None, None, None),
    )
    return jax.shard_map(
        on_device,
        mesh=mesh,
        in_specs=placed,
        out_specs=(P(None, "row", "col"), P()),
        check_vma=False,
    )
```

```python
import functools
import math

import jax
import jax.numpy as jnp
import numpy as np
from jax import lax
from jax.experimental import pallas as pl
from jax.experimental.pallas import tpu as pltpu
from jax.sharding import PartitionSpec as P

AMP_FLOOR = 0.25
OBJECT_REG = 0.5
PROBE_REG = 1.0
MARK = 4096.0
F32 = jnp.float32
BF16 = jnp.bfloat16
LIMIT = 20 * 1024 * 1024


def tables(n):
    k = np.arange(n)
    angle = (np.outer(k, k) % n) * (2.0 * math.pi / n)
    re, im = np.cos(angle) / math.sqrt(n), -np.sin(angle) / math.sqrt(n)
    right = np.block([[re, im], [-im, re]]).astype(np.float32)
    left = np.block([[re, -im], [im, re]]).astype(np.float32)
    both = np.stack([right, left])
    high = both.astype(jnp.bfloat16)
    low = (both - high.astype(np.float32)).astype(jnp.bfloat16)
    return jnp.asarray(np.stack([high, low]))


def call(kernel, out, *args, smem=0, hbm=0, scratch=(), flops=0):
    vmem = pl.BlockSpec(memory_space=pltpu.VMEM)
    specs = [pl.BlockSpec(memory_space=pltpu.SMEM)] * smem + [pl.BlockSpec(memory_space=pltpu.HBM)] * hbm
    specs = specs + [vmem] * (len(args) - smem - hbm)
    nbytes = sum(math.prod(o.shape) * 4 for o in out) + sum(a.size * 4 for a in args)
    return pl.pallas_call(
        kernel,
        out_shape=tuple(out),
        in_specs=specs,
        out_specs=tuple([vmem] * len(out)),
        scratch_shapes=list(scratch),
        compiler_params=pltpu.CompilerParams(vmem_limit_bytes=LIMIT),
        cost_estimate=pl.CostEstimate(flops=flops, bytes_accessed=nbytes, transcendentals=0),
    )(*args)


def shape(*dims):
    return jax.ShapeDtypeStruct(dims, F32)


def split(x):
    high = x.astype(BF16)
    return high, (x - high.astype(F32)).astype(BF16)


def mm(a, b):
    return jnp.dot(a, b, preferred_element_type=F32)


def by_right(x, tab, which):
    high, low = split(x)
    t, u = tab[0, which], tab[1, which]
    return mm(high, t) + (mm(low, t) + mm(high, u))


def by_left(x, tab, which):
    high, low = split(x)
    t, u = tab[0, which], tab[1, which]
    return mm(t, high) + (mm(t, low) + mm(u, high))


def put(ref, lead, row, col, value):
    n = value.shape[0]
    tall, wide = ref.shape[len(lead) :]
    top = pl.multiple_of(jnp.minimum(row // 8, (tall - n) // 8 - 1) * 8, 8)
    base = pl.multiple_of(jnp.minimum(col // n, wide // n - 2) * n, n)
    down, right = row - top, col - base
    tiles = pltpu.roll(value.reshape(n // 8, 8, n), down & 7, 1)
    none = jnp.zeros((1, 8, n), F32)
    sub = lax.broadcasted_iota(jnp.int32, (1, 8, 1), 1)
    tiles = jnp.where(sub < down, jnp.concatenate([none, tiles], axis=0), jnp.concatenate([tiles, none], axis=0))
    moved = pltpu.roll(tiles.reshape(n + 8, n), right & (n - 1), 1)
    lane = lax.broadcasted_iota(jnp.int32, (1, n), 1)
    for at, here in ((base, lane >= right), (base + n, lane < right)):
        block = (*lead, pl.ds(top, n + 8), pl.ds(pl.multiple_of(at, n), n))
        ref[block] = ref[block] + jnp.where(here, moved, 0.0)


def cut(ref, lead, row, col, n):
    tall, wide = ref.shape[len(lead) :]
    top = pl.multiple_of(jnp.minimum(row // 8, (tall - n) // 8 - 1) * 8, 8)
    base = pl.multiple_of(jnp.minimum(col // n, wide // n - 2) * n, n)
    down, right = row - top, col - base
    lane = lax.broadcasted_iota(jnp.int32, (1, n), 1)
    left, after = (
        pltpu.roll(ref[(*lead, pl.ds(top, n + 8), pl.ds(pl.multiple_of(at, n), n))], (n - right) & (n - 1), 1)
        for at in (base, base + n)
    )
    tiles = jnp.where(lane < n - right, left, after).reshape(n // 8 + 1, 8, n)
    tiles = pltpu.roll(tiles, (8 - down) & 7, 1)
    sub = lax.broadcasted_iota(jnp.int32, (1, 8, 1), 1)
    return jnp.where(sub < 8 - down, tiles[:-1], tiles[1:]).reshape(n, n)


def positions(batch, offs, ext, probe, amps, tab, terms, grads, first):
    _, modes, n, _ = probe.shape
    half = n // 2
    terms[...] = jnp.zeros_like(terms)
    if first:
        grads[...] = jnp.zeros_like(grads)

    def one(p):
        row = offs[0, 0, batch, p, 0] + half
        col = offs[0, 0, batch, p, 1] + half
        pr, pi = cut(ext, (0,), row, col, n), cut(ext, (1,), row, col, n)
        waves = []
        for m in range(modes):
            qr, qi = probe[0, m], probe[1, m]
            waves.append(jnp.concatenate([qr * pr - qi * pi, qr * pi + qi * pr], axis=1))
        y = by_right(jnp.concatenate(waves, axis=0), tab, 0)
        z = jnp.concatenate(
            [
                jnp.concatenate([y[m * n : (m + 1) * n, :n] for m in range(modes)], axis=1),
                jnp.concatenate([y[m * n : (m + 1) * n, n:] for m in range(modes)], axis=1),
            ],
            axis=0,
        )
        far = by_left(z, tab, 1)
        square = far * far
        square = square[:n] + square[n:]
        intensity = square[:, :n]
        for m in range(1, modes):
            intensity = intensity + square[:, m * n : (m + 1) * n]
        factor = amps[batch, p] / jnp.maximum(jnp.sqrt(intensity), AMP_FLOOR) - 1.0
        wide = jnp.concatenate([factor] * modes, axis=1)
        h = by_left(far * jnp.concatenate([wide, wide], axis=0), tab, 0)
        h = jnp.concatenate(
            [
                jnp.concatenate([h[:n, m * n : (m + 1) * n], h[n:, m * n : (m + 1) * n]], axis=1)
                for m in range(modes)
            ],
            axis=0,
        )
        change = by_right(h, tab, 1)
        tr = ti = None
        for m in range(modes):
            cr, ci = change[m * n : (m + 1) * n, :n], change[m * n : (m + 1) * n, n:]
            qr, qi = probe[0, m], probe[1, m]
            ar, ai = qr * cr + qi * ci, qr * ci - qi * cr
            tr, ti = (ar, ai) if tr is None else (tr + ar, ti + ai)
            grads[m] = grads[m] + (pr * cr + pi * ci)
            grads[modes + m] = grads[modes + m] + (pr * ci - pi * cr)
        grads[2 * modes] = grads[2 * modes] + (pr * pr + pi * pi)
        put(terms, (0,), row, col, tr)
        put(terms, (1,), row, col, ti)

    for p in range(amps.shape[1]):
        one(p)


def parity(axis):
    return lax.axis_index(axis) % 2


def ends(axis, length, width):
    near = (1 - parity(axis)) * (length - width)
    return pl.multiple_of(near, width), pl.multiple_of(length - width - near, width)


def lower(n):
    return lax.broadcasted_iota(jnp.int32, (1, n), 1) < n // 2


def pack_sides(re_low, im_low, re_high, im_high):
    half = re_low.shape[1] // 2
    keep = lower(2 * half)
    left = jnp.where(keep, re_low, pltpu.roll(im_low, half, 1))
    right = jnp.where(keep, pltpu.roll(re_high, half, 1), im_high)
    even = parity("col") == 0
    return jnp.where(even, right, left), jnp.where(even, left, right)


def by_side(first, second):
    even = parity("col") == 0
    return jnp.where(even, second, first), jnp.where(even, first, second)


def code(offs, n):
    lane = lax.broadcasted_iota(jnp.int32, (8, n), 1)
    coded = jnp.zeros((8, n), jnp.int32)
    for i, index in enumerate(np.ndindex(offs.shape)):
        coded = jnp.where(lane == i, offs[index] + int(MARK), coded)
    return coded


def send_kernel(offs, tile, rows_1, rows_2, cols_1, cols_2):
    _, rows, cols = tile.shape
    n = cols_1.shape[1]
    half = n // 2
    coded = code(offs, n).astype(F32)
    for out, at in zip((rows_1, rows_2), ends("row", rows, half)):
        out[:, :half] = tile[:, pl.ds(at, half)]
        out[:, half:] = jnp.zeros((2, 8, cols), F32)
        out[0, half:, :n] = coded
    first, second = pack_sides(tile[0, :, :n], tile[1, :, :n], tile[0, :, cols - n :], tile[1, :, cols - n :])
    for out, value in ((cols_1, first), (cols_2, second)):
        out[:rows] = value
        out[rows:] = coded


def corner_kernel(cols_1, cols_2, out_1, out_2):
    n = cols_1.shape[1]
    half = n // 2
    rows = cols_1.shape[0] - 8
    for out, at in zip((out_1, out_2), ends("row", rows, half)):
        for k, ref in enumerate((cols_1, cols_2)):
            out[k, :half] = ref[pl.ds(at, half)]
            out[k, half:] = ref[rows:]


def put_halo(ext, tile, rows_1, rows_2, cols_1, cols_2, corner_1, corner_2):
    _, rows, cols = tile.shape
    n = cols_1.shape[1]
    half = n // 2
    keep = lower(n)
    even = parity("row") == 0
    above = jnp.where(even, rows_2[:, :half], rows_1[:, :half])
    below = jnp.where(even, rows_1[:, :half], rows_2[:, :half])
    strips = []
    for k, ref in enumerate((cols_1, cols_2)):
        c1, c2 = corner_1[k, :half], corner_2[k, :half]
        strips.append(jnp.concatenate([jnp.where(even, c2, c1), ref[:rows], jnp.where(even, c1, c2)], axis=0))
    left, right = by_side(*strips)
    for ch in range(2):
        body = jnp.concatenate([above[ch], tile[ch], below[ch]], axis=0)
        lf = left if ch == 0 else pltpu.roll(left, half, 1)
        rt = right if ch == 1 else pltpu.roll(right, half, 1)
        turned = [lf] + [pltpu.roll(body[:, k : k + n], half, 1) for k in range(0, cols, n)] + [rt]
        for k in range(len(turned) - 1):
            ext[ch, :, k * n : (k + 1) * n] = jnp.where(keep, turned[k], turned[k + 1])


def give(n, terms, cols_1, cols_2, mid_1, mid_2):
    _, rows, cols = terms.shape
    for out, at in zip((cols_1, cols_2), ends("col", cols, n)):
        out[...] = terms[:, :, pl.ds(at, n)]
    for out, at in zip((mid_1, mid_2), ends("row", rows, n)):
        out[...] = terms[:, pl.ds(at, n), n : cols - n]


def first_kernel(offs, tile_hbm, probe_hbm, amps_hbm, tab_hbm, rows_1, rows_2, cols_1, cols_2, corner_1, corner_2,
                 ext, terms, grads, around, cols_out_1, cols_out_2, mid_out_1, mid_out_2,
                 tile, probe, amps, tab, sems):
    copies = [
        pltpu.make_async_copy(src, dst, sems.at[i])
        for i, (src, dst) in enumerate((
            (tile_hbm, tile), (probe_hbm, probe), (tab_hbm, tab), (amps_hbm.at[pl.ds(0, 1)], amps)))
    ]
    for copy in copies:
        copy.start()
    n = cols_1.shape[1]
    rows = cols_1.shape[0] - 8
    half = n // 2
    lines = [code(offs, n)[:1]]
    lines += [ref[rows : rows + 1].astype(jnp.int32) for ref in (cols_1, cols_2)]
    for ref, corner in ((rows_1, corner_1), (rows_2, corner_2)):
        lines += [ref[0, half : half + 1, :n].astype(jnp.int32)]
        lines += [corner[k, half : half + 1].astype(jnp.int32) for k in range(2)]
    around[...] = jnp.zeros_like(around)
    for k, line in enumerate(lines):
        around[k : k + 1] = line
    copies[0].wait()
    put_halo(ext, tile, rows_1, rows_2, cols_1, cols_2, corner_1, corner_2)
    for copy in copies[1:]:
        copy.wait()
    positions(0, offs, ext, probe, amps, tab, terms, grads, True)
    give(n, terms, cols_out_1, cols_out_2, mid_out_1, mid_out_2)


def side_kernel(terms, got_1, got_2, side_1, side_2, send_1, send_2):
    n = got_1.shape[2]
    _, rows, cols = terms.shape
    for side, got, at in zip((side_1, side_2), (got_1, got_2), ends("col", cols, n)):
        side[...] = terms[:, :, pl.ds(at, n)] + got[...]
    for out, at in zip((send_1, send_2), ends("row", rows, n)):
        for k, side in enumerate((side_1, side_2)):
            out[k] = side[:, pl.ds(at, n)]


def update(ext, old, weight, terms, side_1, side_2, mid_1, mid_2, ends_1, ends_2):
    n = side_1.shape[2]
    _, rows, cols = old.shape
    at_rows = ends("row", rows, n)
    inner = slice(n, cols - n)
    for ch in range(2):
        for k, (side, at) in enumerate(zip((side_1, side_2), ends("col", cols, n))):
            here = pl.ds(at, n)
            ext[ch, :, here] = old[ch, :, here] + side[ch] * weight[:, here]
            for got, top in zip((ends_1, ends_2), at_rows):
                there = pl.ds(top, n)
                ext[ch, there, here] = ext[ch, there, here] + got[k, ch] * weight[there, here]
        ext[ch, :, inner] = old[ch, :, inner] + terms[ch, :, inner] * weight[:, inner]
        for got, top in zip((mid_1, mid_2), at_rows):
            there = pl.ds(top, n)
            ext[ch, there, inner] = ext[ch, there, inner] + got[ch] * weight[there, inner]


def next_kernel(batch, offs, old, weight, old_terms, side_1, side_2, mid_1, mid_2, ends_1, ends_2, probe, amps, tab,
                grads_in, ext, terms, grads, *sends):
    update(ext, old, weight, old_terms, side_1, side_2, mid_1, mid_2, ends_1, ends_2)
    grads[...] = grads_in[...]
    positions(batch, offs, ext, probe, amps, tab, terms, grads, False)
    give(probe.shape[2], terms, *sends)


def last_kernel(batch, offs, old, weight, old_terms, side_1, side_2, mid_1, mid_2, ends_1, ends_2, probe, amps, tab,
                grads_in, ext, terms, keep, send, cols_1, cols_2, mids_1, mids_2, grads):
    n = probe.shape[2]
    half = n // 2
    update(ext, old, weight, old_terms, side_1, side_2, mid_1, mid_2, ends_1, ends_2)
    grads[...] = grads_in[...]
    positions(batch, offs, ext, probe, amps, tab, terms, grads, False)
    mine = pl.multiple_of(parity("col") * half, half)
    keep[...] = grads[:, pl.ds(mine, half)]
    send[...] = grads[:, pl.ds(pl.multiple_of(half - mine, half), half)]
    _, rows, cols = terms.shape
    first, second = pack_sides(terms[0, :, :n], terms[1, :, :n], terms[0, :, cols - n :], terms[1, :, cols - n :])
    cols_1[...] = first
    cols_2[...] = second
    for out, at in zip((mids_1, mids_2), ends("row", rows, half)):
        out[...] = terms[:, pl.ds(at, half), n : cols - n]


def last_side_kernel(terms, got_1, got_2, side, send_1, send_2):
    _, rows, cols = terms.shape
    n = got_1.shape[1]
    half = n // 2
    keep = lower(n)
    left, right = by_side(got_1[...], got_2[...])
    for ch in range(2):
        lf = pltpu.roll(left, half, 1) if ch == 0 else left
        rt = right if ch == 0 else pltpu.roll(right, half, 1)
        side[ch] = jnp.where(keep, terms[ch, :, cols - n :] + rt, terms[ch, :, :n] + lf)
    for out, at in zip((send_1, send_2), ends("row", rows, half)):
        out[...] = side[:, pl.ds(at, half)]


def object_kernel(old, weight, terms, side, mid_1, mid_2, ends_1, ends_2, out):
    _, rows, cols = old.shape
    n = side.shape[2]
    half = n // 2
    keep = lower(n)
    even = parity("row") == 0
    inner = slice(n, cols - n)
    own = slice(half, rows - half)
    tall = rows - n - 2 * half

    def tops(value, first, second):
        above, below = jnp.where(even, second, first), jnp.where(even, first, second)
        gap = jnp.zeros((tall, value.shape[1]), F32)
        return value + jnp.concatenate([above, gap, below], axis=0)

    for ch in range(2):
        edge = tops(side[ch, own], ends_1[ch], ends_2[ch])
        edge = jnp.where(keep, old[ch, own, cols - n :], old[ch, own, :n]) + edge * jnp.where(
            keep, weight[own, cols - n :], weight[own, :n])
        body = old[ch, own, inner] + tops(terms[ch, own, inner], mid_1[ch], mid_2[ch]) * weight[own, inner]
        edge = pltpu.roll(edge, half, 1)
        turned = [edge] + [pltpu.roll(body[:, k : k + n], half, 1) for k in range(0, cols - 2 * n, n)] + [edge]
        for k in range(len(turned) - 1):
            out[ch, :, k * n : (k + 1) * n] = jnp.where(keep, turned[k], turned[k + 1])


def light_kernel(batch, pos, around, probe, weight, light):
    _, modes, n, _ = probe.shape
    half = n // 2
    rows, cols = weight.shape
    tile_r, tile_c = rows - n, cols - n
    lit = None
    for m in range(modes):
        s = probe[0, m] * probe[0, m] + probe[1, m] * probe[1, m]
        lit = s if lit is None else lit + s
    light[...] = jnp.zeros_like(light)
    big = int(MARK)

    def side(which, axis):
        step = 1 - 2 * parity(axis)
        return jnp.where(which == 0, 0, jnp.where(which == 1, step, -step))

    def one(i, carry):
        k, p = i // pos, i % pos
        at = (batch * pos + p) * 2
        there = around[k, at] > 0
        row = around[k, at] - big + half + side(k // 3, "row") * tile_r
        col = around[k, at + 1] - big + half + side(k % 3, "col") * tile_c
        hit = there & (row > -n) & (row < rows) & (col > -n) & (col < cols)

        @pl.when(hit)
        def _():
            put(light, (), row + n, col + n, lit)

        return carry

    lax.fori_loop(0, 9 * pos, one, 0)
    r = lax.broadcasted_iota(jnp.int32, (rows, cols), 0)
    c = lax.broadcasted_iota(jnp.int32, (rows, cols), 1)
    odd_r, odd_c = parity("row"), parity("col")
    low_r = jnp.where(around[6 - 3 * odd_r, 0] > 0, 0, half)
    high_r = jnp.where(around[3 + 3 * odd_r, 0] > 0, rows, rows - half)
    low_c = jnp.where(around[2 - odd_c, 0] > 0, 0, half)
    high_c = jnp.where(around[1 + odd_c, 0] > 0, cols, cols - half)
    inside = (r >= low_r) & (r < high_r) & (c >= low_c) & (c < high_c)
    total = light[n : n + rows, n : n + cols]
    weight[...] = jnp.where(inside, 1.0 / (total + OBJECT_REG), 0.0)


def parts_kernel(keep, got, parts):
    maps = keep.shape[0]
    each = parts.shape[1] // maps
    for m in range(maps):
        total = keep[m] + got[m]
        for i in range(parts.shape[0]):
            parts[i, m * each : (m + 1) * each] = total[i * each : (i + 1) * each]


def step_kernel(parts, out):
    total = parts[0]
    for i in range(1, parts.shape[0]):
        total = total + parts[i]
    each = total.shape[0] - out.shape[1]
    maps = total.shape[0] // each
    scale = 1.0 / jnp.sqrt(total[(maps - 1) * each :] + PROBE_REG)
    step = jnp.concatenate([total[m * each : (m + 1) * each] * scale for m in range(maps - 1)], axis=0)
    for i in range(out.shape[0]):
        out[i] = step


def join_kernel(mine, other, out):
    maps, n, _ = out.shape
    half = n // 2
    each = mine.shape[1] // maps
    at = pl.multiple_of(parity("col") * half, half)
    for ref, top in ((mine, at), (other, pl.multiple_of(half - at, half))):
        for m in range(maps):
            out[m, pl.ds(top, half)] = jnp.concatenate(
                [ref[i, m * each : (m + 1) * each] for i in range(ref.shape[0])], axis=0)


def swap(value, axis, phase):
    size = lax.axis_size(axis)
    pairs = [(i, i + 1) for i in range(phase, size - 1, 2)]
    return lax.ppermute(value, axis, pairs + [(j, i) for i, j in pairs])


def both(first, second, axis):
    return swap(first, axis, 0), swap(second, axis, 1)


def on_device(tile, probe, amplitudes, offsets):
    _, modes, n, _ = probe.shape
    half = n // 2
    _, rows, cols = tile.shape
    tall, wide = rows + n, cols + n
    amps = amplitudes[0, 0]
    batches, pos = offsets.shape[2:4]
    maps = 2 * modes + 1
    tab = tables(n)
    flops = pos * modes * 2 * 2 * 4 * 2 * n**3 * 3

    sends = call(send_kernel, [shape(2, half + 8, cols)] * 2 + [shape(rows + 8, n)] * 2, offsets, tile, smem=1)
    c1, c2 = both(*sends[2:], "col")
    r1, r2 = both(*sends[:2], "row")
    k1, k2 = both(*call(corner_kernel, [shape(2, half + 8, n)] * 2, c1, c2), "row")

    plain = [shape(2, tall, wide), shape(2, tall, wide), shape(maps, n, n)]
    messages = [shape(2, tall, n)] * 2 + [shape(2, n, cols - n)] * 2
    ext, terms, grads, around, *sends = call(
        first_kernel, plain + [jax.ShapeDtypeStruct((16, n), jnp.int32)] + messages,
        offsets, tile, probe, amps, tab, r1, r2, c1, c2, k1, k2, smem=1, hbm=4, flops=flops,
        scratch=[pltpu.VMEM(tile.shape, F32), pltpu.VMEM(probe.shape, F32), pltpu.VMEM((1, *amps.shape[1:]), F32),
                 pltpu.VMEM(tab.shape, BF16), pltpu.SemaphoreType.DMA((4,))])

    def light(batch, around):
        return call(
            functools.partial(light_kernel, batch, pos), [shape(tall, wide)], around, probe, smem=1,
            scratch=[pltpu.VMEM((tall + 2 * n, wide + 2 * n), F32)], flops=10**9)[0]

    weights = [light(batch, around) for batch in range(min(2, batches))]
    for batch in range(batches):
        c1, c2 = both(*sends[:2], "col")
        m1, m2 = both(*sends[2:4], "row")
        if batch + 1 == batches:
            break
        s1, s2, *sends = call(
            side_kernel, [shape(2, tall, n)] * 2 + [shape(2, 2, n, n)] * 2, terms, c1, c2)
        e1, e2 = both(*sends, "row")
        if len(weights) < batches and batch > 0:
            around, c1 = lax.optimization_barrier((around, c1))
            weights.append(light(batch + 1, around))
        terms, weights = lax.optimization_barrier((terms, weights))
        args = (offsets, ext, weights[batch], terms, s1, s2, m1, m2, e1, e2, probe, amps, tab, grads)
        if batch + 2 < batches:
            ext, terms, grads, *sends = call(
                functools.partial(next_kernel, batch + 1), plain + messages, *args, smem=1, flops=flops)
        else:
            ext, terms, keep, send, *sends = call(
                functools.partial(last_kernel, batch + 1),
                plain[:2] + [shape(maps, half, n)] * 2 + [shape(tall, n)] * 2 + [shape(2, half, cols - n)] * 2,
                *args, smem=1, flops=flops, scratch=[pltpu.VMEM((maps, n, n), F32)])
            got = swap(send, "col", 0)
            got, sends = lax.optimization_barrier((got, sends))

    def rest(c1, c2, m1, m2):
        side, *sends = call(last_side_kernel, [shape(2, tall, n)] + [shape(2, half, n)] * 2, terms, c1, c2)
        e1, e2 = both(*sends, "row")
        return call(object_kernel, [shape(2, rows, cols)], ext, weights[-1], terms, side, m1, m2, e1, e2)[0]

    probe_step, object_new = all_sum(keep, send, got, (c1, c2, m1, m2), rest)
    return object_new, probe_step.reshape(2, modes, n, n)


def all_sum(keep, send, got, beside, rest):
    maps, half, n = keep.shape
    axes = ("row", "col")
    across = lax.axis_size("col")
    devices = lax.axis_size("row") * across
    if across % 2 or half % (devices // 2):
        first = jnp.where(parity("col") == 0, keep, send)
        second = jnp.where(parity("col") == 0, send, keep)
        total = lax.psum(jnp.concatenate([first, second], axis=1), axes)
        return total[:-1] / jnp.sqrt(total[-1] + PROBE_REG), rest(*beside)
    groups = [list(range(k, devices, 2)) for k in range(2)]
    each = 2 * half // devices
    (parts,) = call(parts_kernel, [shape(devices // 2, maps * each, n)], keep, got)
    parts = lax.all_to_all(parts, axes, 0, 0, axis_index_groups=groups, tiled=True)
    parts, beside = lax.optimization_barrier((parts, beside))
    (steps,) = call(step_kernel, [shape(devices // 2, (maps - 1) * each, n)], parts)
    steps, beside = lax.optimization_barrier((steps, beside))
    steps = lax.all_to_all(steps, axes, 0, 0, axis_index_groups=groups, tiled=True)
    object_new = rest(*beside)
    steps, object_new = lax.optimization_barrier((steps, object_new))
    (out,) = call(join_kernel, [shape(maps - 1, n, n)], steps, swap(steps, "col", 0))
    return out, object_new


def solution(mesh):
    placed = (
        P(None, "row", "col"),
        P(),
        P("row", "col", None, None, None, None),
        P("row", "col", None, None, None),
    )
    return jax.shard_map(
        on_device,
        mesh=mesh,
        in_specs=placed,
        out_specs=(P(None, "row", "col"), P()),
        check_vma=False,
    )
```

```python
import functools
import math

import jax
import jax.numpy as jnp
import numpy as np
from jax import lax
from jax.experimental import pallas as pl
from jax.experimental.pallas import tpu as pltpu
from jax.sharding import PartitionSpec as P

AMP_FLOOR = 0.25
OBJECT_REG = 0.5
PROBE_REG = 1.0
MARK = 4096.0
F32 = jnp.float32
BF16 = jnp.bfloat16
LIMIT = 20 * 1024 * 1024


def tables(n):
    k = np.arange(n)
    angle = (np.outer(k, k) % n) * (2.0 * math.pi / n)
    re, im = np.cos(angle) / math.sqrt(n), -np.sin(angle) / math.sqrt(n)
    right = np.block([[re, im], [-im, re]]).astype(np.float32)
    left = np.block([[re, -im], [im, re]]).astype(np.float32)
    both = np.stack([right, left])
    high = both.astype(jnp.bfloat16)
    low = (both - high.astype(np.float32)).astype(jnp.bfloat16)
    return jnp.asarray(np.stack([high, low]))


def call(kernel, out, *args, smem=0, hbm=0, scratch=(), flops=0):
    vmem = pl.BlockSpec(memory_space=pltpu.VMEM)
    specs = [pl.BlockSpec(memory_space=pltpu.SMEM)] * smem + [pl.BlockSpec(memory_space=pltpu.HBM)] * hbm
    specs = specs + [vmem] * (len(args) - smem - hbm)
    nbytes = sum(math.prod(o.shape) * 4 for o in out) + sum(a.size * 4 for a in args)
    return pl.pallas_call(
        kernel,
        out_shape=tuple(out),
        in_specs=specs,
        out_specs=tuple([vmem] * len(out)),
        scratch_shapes=list(scratch),
        compiler_params=pltpu.CompilerParams(vmem_limit_bytes=LIMIT),
        cost_estimate=pl.CostEstimate(flops=flops, bytes_accessed=nbytes, transcendentals=0),
    )(*args)


def shape(*dims):
    return jax.ShapeDtypeStruct(dims, F32)


def split(x):
    high = x.astype(BF16)
    return high, (x - high.astype(F32)).astype(BF16)


def mm(a, b):
    return jnp.dot(a, b, preferred_element_type=F32)


def by_right(x, tab, which):
    high, low = split(x)
    t, u = tab[0, which], tab[1, which]
    return mm(high, t) + (mm(low, t) + mm(high, u))


def by_left(x, tab, which):
    high, low = split(x)
    t, u = tab[0, which], tab[1, which]
    return mm(t, high) + (mm(t, low) + mm(u, high))


def put(ref, lead, row, col, value):
    n = value.shape[0]
    tall, wide = ref.shape[len(lead) :]
    top = pl.multiple_of(jnp.minimum(row // 8, (tall - n) // 8 - 1) * 8, 8)
    base = pl.multiple_of(jnp.minimum(col // n, wide // n - 2) * n, n)
    down, right = row - top, col - base
    tiles = pltpu.roll(value.reshape(n // 8, 8, n), down & 7, 1)
    none = jnp.zeros((1, 8, n), F32)
    sub = lax.broadcasted_iota(jnp.int32, (1, 8, 1), 1)
    tiles = jnp.where(sub < down, jnp.concatenate([none, tiles], axis=0), jnp.concatenate([tiles, none], axis=0))
    moved = pltpu.roll(tiles.reshape(n + 8, n), right & (n - 1), 1)
    lane = lax.broadcasted_iota(jnp.int32, (1, n), 1)
    for at, here in ((base, lane >= right), (base + n, lane < right)):
        block = (*lead, pl.ds(top, n + 8), pl.ds(pl.multiple_of(at, n), n))
        ref[block] = ref[block] + jnp.where(here, moved, 0.0)


def cut(ref, lead, row, col, n):
    tall, wide = ref.shape[len(lead) :]
    top = pl.multiple_of(jnp.minimum(row // 8, (tall - n) // 8 - 1) * 8, 8)
    base = pl.multiple_of(jnp.minimum(col // n, wide // n - 2) * n, n)
    down, right = row - top, col - base
    lane = lax.broadcasted_iota(jnp.int32, (1, n), 1)
    left, after = (
        pltpu.roll(ref[(*lead, pl.ds(top, n + 8), pl.ds(pl.multiple_of(at, n), n))], (n - right) & (n - 1), 1)
        for at in (base, base + n)
    )
    tiles = jnp.where(lane < n - right, left, after).reshape(n // 8 + 1, 8, n)
    tiles = pltpu.roll(tiles, (8 - down) & 7, 1)
    sub = lax.broadcasted_iota(jnp.int32, (1, 8, 1), 1)
    return jnp.where(sub < 8 - down, tiles[:-1], tiles[1:]).reshape(n, n)


def positions(batch, offs, ext, probe, amps, tab, terms, grads, first):
    _, modes, n, _ = probe.shape
    half = n // 2
    terms[...] = jnp.zeros_like(terms)
    if first:
        grads[...] = jnp.zeros_like(grads)

    def one(p):
        row = offs[0, 0, batch, p, 0] + half
        col = offs[0, 0, batch, p, 1] + half
        pr, pi = cut(ext, (0,), row, col, n), cut(ext, (1,), row, col, n)
        waves = []
        for m in range(modes):
            qr, qi = probe[0, m], probe[1, m]
            waves.append(jnp.concatenate([qr * pr - qi * pi, qr * pi + qi * pr], axis=1))
        y = by_right(jnp.concatenate(waves, axis=0), tab, 0)
        z = jnp.concatenate(
            [
                jnp.concatenate([y[m * n : (m + 1) * n, :n] for m in range(modes)], axis=1),
                jnp.concatenate([y[m * n : (m + 1) * n, n:] for m in range(modes)], axis=1),
            ],
            axis=0,
        )
        far = by_left(z, tab, 1)
        square = far * far
        square = square[:n] + square[n:]
        intensity = square[:, :n]
        for m in range(1, modes):
            intensity = intensity + square[:, m * n : (m + 1) * n]
        factor = amps[batch, p] / jnp.maximum(jnp.sqrt(intensity), AMP_FLOOR) - 1.0
        wide = jnp.concatenate([factor] * modes, axis=1)
        h = by_left(far * jnp.concatenate([wide, wide], axis=0), tab, 0)
        h = jnp.concatenate(
            [
                jnp.concatenate([h[:n, m * n : (m + 1) * n], h[n:, m * n : (m + 1) * n]], axis=1)
                for m in range(modes)
            ],
            axis=0,
        )
        change = by_right(h, tab, 1)
        tr = ti = None
        for m in range(modes):
            cr, ci = change[m * n : (m + 1) * n, :n], change[m * n : (m + 1) * n, n:]
            qr, qi = probe[0, m], probe[1, m]
            ar, ai = qr * cr + qi * ci, qr * ci - qi * cr
            tr, ti = (ar, ai) if tr is None else (tr + ar, ti + ai)
            grads[m] = grads[m] + (pr * cr + pi * ci)
            grads[modes + m] = grads[modes + m] + (pr * ci - pi * cr)
        grads[2 * modes] = grads[2 * modes] + (pr * pr + pi * pi)
        put(terms, (0,), row, col, tr)
        put(terms, (1,), row, col, ti)

    for p in range(amps.shape[1]):
        one(p)


def parity(axis):
    return lax.axis_index(axis) % 2


def ends(axis, length, width):
    near = (1 - parity(axis)) * (length - width)
    return pl.multiple_of(near, width), pl.multiple_of(length - width - near, width)


def lower(n):
    return lax.broadcasted_iota(jnp.int32, (1, n), 1) < n // 2


def pack_sides(re_low, im_low, re_high, im_high):
    half = re_low.shape[1] // 2
    keep = lower(2 * half)
    left = jnp.where(keep, re_low, pltpu.roll(im_low, half, 1))
    right = jnp.where(keep, pltpu.roll(re_high, half, 1), im_high)
    even = parity("col") == 0
    return jnp.where(even, right, left), jnp.where(even, left, right)


def by_side(first, second):
    even = parity("col") == 0
    return jnp.where(even, second, first), jnp.where(even, first, second)


def lines(offs):
    return -(-offs.shape[2] * offs.shape[3] // 8) * 8


def code(offs):
    _, _, batches, pos, dims = offs.shape
    rows = [offs[0, 0, b] + int(MARK) for b in range(batches)]
    spare = lines(offs) - batches * pos
    if spare:
        rows.append(jnp.zeros((spare, dims), jnp.int32))
    return jnp.concatenate(rows, axis=0)


def send_kernel(offs, tile, rows_1, rows_2, cols_1, cols_2):
    _, rows, cols = tile.shape
    n = cols_1.shape[1]
    half = n // 2
    coded = code(offs).astype(F32)
    for out, at in zip((rows_1, rows_2), ends("row", rows, half)):
        out[:, :half] = tile[:, pl.ds(at, half)]
        out[:, half:] = jnp.zeros((2, lines(offs), cols), F32)
        out[0, half:, : coded.shape[1]] = coded
    first, second = pack_sides(tile[0, :, :n], tile[1, :, :n], tile[0, :, cols - n :], tile[1, :, cols - n :])
    for out, value in ((cols_1, first), (cols_2, second)):
        out[:rows] = value
        out[rows:] = jnp.zeros((lines(offs), n), F32)
        out[rows:, : coded.shape[1]] = coded


def corner_kernel(cols_1, cols_2, out_1, out_2):
    n = cols_1.shape[1]
    half = n // 2
    rows = cols_1.shape[0] - (out_1.shape[1] - half)
    for out, at in zip((out_1, out_2), ends("row", rows, half)):
        for k, ref in enumerate((cols_1, cols_2)):
            out[k, :half] = ref[pl.ds(at, half)]
            out[k, half:] = ref[rows:]


def put_halo(ext, tile, rows_1, rows_2, cols_1, cols_2, corner_1, corner_2):
    _, rows, cols = tile.shape
    n = cols_1.shape[1]
    half = n // 2
    keep = lower(n)
    even = parity("row") == 0
    above = jnp.where(even, rows_2[:, :half], rows_1[:, :half])
    below = jnp.where(even, rows_1[:, :half], rows_2[:, :half])
    strips = []
    for k, ref in enumerate((cols_1, cols_2)):
        c1, c2 = corner_1[k, :half], corner_2[k, :half]
        strips.append(jnp.concatenate([jnp.where(even, c2, c1), ref[:rows], jnp.where(even, c1, c2)], axis=0))
    left, right = by_side(*strips)
    for ch in range(2):
        body = jnp.concatenate([above[ch], tile[ch], below[ch]], axis=0)
        lf = left if ch == 0 else pltpu.roll(left, half, 1)
        rt = right if ch == 1 else pltpu.roll(right, half, 1)
        turned = [lf] + [pltpu.roll(body[:, k : k + n], half, 1) for k in range(0, cols, n)] + [rt]
        for k in range(len(turned) - 1):
            ext[ch, :, k * n : (k + 1) * n] = jnp.where(keep, turned[k], turned[k + 1])


def give(n, terms, cols_1, cols_2, mid_1, mid_2):
    _, rows, cols = terms.shape
    for out, at in zip((cols_1, cols_2), ends("col", cols, n)):
        out[...] = terms[:, :, pl.ds(at, n)]
    for out, at in zip((mid_1, mid_2), ends("row", rows, n)):
        out[...] = terms[:, pl.ds(at, n), n : cols - n]


def stage_kernel(*refs):
    count = len(refs) // 2
    for src, dst in zip(refs[:count], refs[count:]):
        dst[...] = src[: dst.shape[0]]


def first_kernel(offs, own, tile, probe, amps, tab, rows_1, rows_2, cols_1, cols_2, corner_1, corner_2,
                 ext, terms, grads, around, *sends):
    n = cols_1.shape[1]
    half = n // 2
    rows = tile.shape[1]
    size = lines(own)
    coded = code(own)
    around[:size] = jnp.zeros((size, n), jnp.int32)
    around[:size, : coded.shape[1]] = coded
    blocks = [ref[rows:] for ref in (cols_1, cols_2)]
    for ref, corner in ((rows_1, corner_1), (rows_2, corner_2)):
        blocks += [ref[0, half:, :n], corner[0, half:], corner[1, half:]]
    for k, block in enumerate(blocks):
        around[(k + 1) * size : (k + 2) * size] = block.astype(jnp.int32)
    put_halo(ext, tile, rows_1, rows_2, cols_1, cols_2, corner_1, corner_2)
    positions(0, offs, ext, probe, amps, tab, terms, grads, True)
    give(n, terms, *sends)


def side_kernel(terms, got_1, got_2, side_1, side_2, send_1, send_2):
    n = got_1.shape[2]
    _, rows, cols = terms.shape
    for side, got, at in zip((side_1, side_2), (got_1, got_2), ends("col", cols, n)):
        side[...] = terms[:, :, pl.ds(at, n)] + got[...]
    for out, at in zip((send_1, send_2), ends("row", rows, n)):
        for k, side in enumerate((side_1, side_2)):
            out[k] = side[:, pl.ds(at, n)]


def update(ext, old, weight, terms, side_1, side_2, mid_1, mid_2, ends_1, ends_2):
    n = side_1.shape[2]
    _, rows, cols = old.shape
    at_rows = ends("row", rows, n)
    inner = slice(n, cols - n)
    for ch in range(2):
        for k, (side, at) in enumerate(zip((side_1, side_2), ends("col", cols, n))):
            here = pl.ds(at, n)
            ext[ch, :, here] = old[ch, :, here] + side[ch] * weight[:, here]
            for got, top in zip((ends_1, ends_2), at_rows):
                there = pl.ds(top, n)
                ext[ch, there, here] = ext[ch, there, here] + got[k, ch] * weight[there, here]
        ext[ch, :, inner] = old[ch, :, inner] + terms[ch, :, inner] * weight[:, inner]
        for got, top in zip((mid_1, mid_2), at_rows):
            there = pl.ds(top, n)
            ext[ch, there, inner] = ext[ch, there, inner] + got[ch] * weight[there, inner]


def next_kernel(batch, offs, old, weight, old_terms, side_1, side_2, mid_1, mid_2, ends_1, ends_2, probe, amps, tab,
                grads_in, ext, terms, grads, *sends):
    update(ext, old, weight, old_terms, side_1, side_2, mid_1, mid_2, ends_1, ends_2)
    grads[...] = grads_in[...]
    positions(batch, offs, ext, probe, amps, tab, terms, grads, False)
    give(probe.shape[2], terms, *sends)


def last_kernel(batch, offs, old, weight, old_terms, side_1, side_2, mid_1, mid_2, ends_1, ends_2, probe, amps, tab,
                grads_in, ext, terms, keep, send, rows_1, rows_2, grads):
    n = probe.shape[2]
    half = n // 2
    update(ext, old, weight, old_terms, side_1, side_2, mid_1, mid_2, ends_1, ends_2)
    grads[...] = grads_in[...]
    positions(batch, offs, ext, probe, amps, tab, terms, grads, False)
    mine = pl.multiple_of(parity("col") * half, half)
    keep[...] = grads[:, pl.ds(mine, half)]
    send[...] = grads[:, pl.ds(pl.multiple_of(half - mine, half), half)]
    for out, at in zip((rows_1, rows_2), ends("row", terms.shape[1], half)):
        out[...] = terms[:, pl.ds(at, half)]


def own_rows(terms, ch, got_1, got_2, at):
    rows = terms.shape[1]
    half = got_1.shape[1]
    even = parity("row") == 0
    first, second = got_1[ch, :, at], got_2[ch, :, at]
    value = terms[ch, half : rows - half, at]
    gap = jnp.zeros((value.shape[0] - 2 * half, value.shape[1]), F32)
    return value + jnp.concatenate(
        [jnp.where(even, second, first), gap, jnp.where(even, first, second)], axis=0)


def last_side_kernel(terms, got_1, got_2, cols_1, cols_2):
    n = cols_1.shape[1]
    cols = terms.shape[2]
    left, right = slice(0, n), slice(cols - n, cols)
    cols_1[...], cols_2[...] = pack_sides(
        *(own_rows(terms, ch, got_1, got_2, at) for at in (left, right) for ch in range(2)))


def object_kernel(old, weight, terms, got_1, got_2, cols_1, cols_2, out):
    _, rows, cols = old.shape
    n = cols_1.shape[1]
    half = n // 2
    keep = lower(n)
    own = slice(half, rows - half)
    left, right = by_side(cols_1[...], cols_2[...])
    for ch in range(2):
        lf = pltpu.roll(left, half, 1) if ch == 0 else left
        rt = right if ch == 0 else pltpu.roll(right, half, 1)
        turned = []
        for k in range(0, cols, n):
            at = slice(k, k + n)
            total = own_rows(terms, ch, got_1, got_2, at)
            if k == 0:
                total = jnp.where(keep, total, total + lf)
            if k == cols - n:
                total = jnp.where(keep, total + rt, total)
            turned.append(pltpu.roll(old[ch, own, at] + total * weight[own, at], half, 1))
        for k in range(len(turned) - 1):
            out[ch, :, k * n : (k + 1) * n] = jnp.where(keep, turned[k], turned[k + 1])


def light_kernel(batch, pos, around, probe, weight, light):
    _, modes, n, _ = probe.shape
    half = n // 2
    rows, cols = weight.shape
    tile_r, tile_c = rows - n, cols - n
    lit = None
    for m in range(modes):
        s = probe[0, m] * probe[0, m] + probe[1, m] * probe[1, m]
        lit = s if lit is None else lit + s
    light[...] = jnp.zeros_like(light)
    big = int(MARK)
    size = around.shape[0] // 9

    def side(which, axis):
        step = 1 - 2 * parity(axis)
        return jnp.where(which == 0, 0, jnp.where(which == 1, step, -step))

    def one(i, carry):
        k, p = i // pos, i % pos
        at = k * size + batch * pos + p
        there = around[at, 0] > 0
        row = around[at, 0] - big + half + side(k // 3, "row") * tile_r
        col = around[at, 1] - big + half + side(k % 3, "col") * tile_c
        hit = there & (row > -n) & (row < rows) & (col > -n) & (col < cols)

        @pl.when(hit)
        def _():
            put(light, (), row + n, col + n, lit)

        return carry

    lax.fori_loop(0, 9 * pos, one, 0)
    r = lax.broadcasted_iota(jnp.int32, (rows, cols), 0)
    c = lax.broadcasted_iota(jnp.int32, (rows, cols), 1)
    odd_r, odd_c = parity("row"), parity("col")
    low_r = jnp.where(around[(6 - 3 * odd_r) * size, 0] > 0, 0, half)
    high_r = jnp.where(around[(3 + 3 * odd_r) * size, 0] > 0, rows, rows - half)
    low_c = jnp.where(around[(2 - odd_c) * size, 0] > 0, 0, half)
    high_c = jnp.where(around[(1 + odd_c) * size, 0] > 0, cols, cols - half)
    inside = (r >= low_r) & (r < high_r) & (c >= low_c) & (c < high_c)
    total = light[n : n + rows, n : n + cols]
    weight[...] = jnp.where(inside, 1.0 / (total + OBJECT_REG), 0.0)


def parts_kernel(keep, got, parts):
    maps = keep.shape[0]
    each = parts.shape[1] // maps
    for m in range(maps):
        total = keep[m] + got[m]
        for i in range(parts.shape[0]):
            parts[i, m * each : (m + 1) * each] = total[i * each : (i + 1) * each]


def step_kernel(parts, out):
    total = parts[0]
    for i in range(1, parts.shape[0]):
        total = total + parts[i]
    each = total.shape[0] - out.shape[1]
    maps = total.shape[0] // each
    scale = 1.0 / jnp.sqrt(total[(maps - 1) * each :] + PROBE_REG)
    step = jnp.concatenate([total[m * each : (m + 1) * each] * scale for m in range(maps - 1)], axis=0)
    for i in range(out.shape[0]):
        out[i] = step


def join_kernel(mine, other, out):
    maps, n, _ = out.shape
    half = n // 2
    each = mine.shape[1] // maps
    at = pl.multiple_of(parity("col") * half, half)
    for ref, top in ((mine, at), (other, pl.multiple_of(half - at, half))):
        for m in range(maps):
            out[m, pl.ds(top, half)] = jnp.concatenate(
                [ref[i, m * each : (m + 1) * each] for i in range(ref.shape[0])], axis=0)


def swap(value, axis, phase):
    size = lax.axis_size(axis)
    pairs = [(i, i + 1) for i in range(phase, size - 1, 2)]
    return lax.ppermute(value, axis, pairs + [(j, i) for i, j in pairs])


def both(first, second, axis):
    return swap(first, axis, 0), swap(second, axis, 1)


def on_device(tile, probe, amplitudes, offsets):
    _, modes, n, _ = probe.shape
    half = n // 2
    _, rows, cols = tile.shape
    tall, wide = rows + n, cols + n
    amps = amplitudes[0, 0]
    batches, pos = offsets.shape[2:4]
    maps = 2 * modes + 1
    tab = tables(n)
    flops = pos * modes * 2 * 2 * 4 * 2 * n**3 * 3

    size = lines(offsets)
    sends = call(send_kernel, [shape(2, half + size, cols)] * 2 + [shape(rows + size, n)] * 2, offsets, tile)
    c1, c2 = both(*sends[2:], "col")
    r1, r2 = both(*sends[:2], "row")
    corners = call(corner_kernel, [shape(2, half + size, n)] * 2, c1, c2)
    corners, tile, probe, amps_now, tab = lax.optimization_barrier((corners, tile, probe, amps, tab))
    k1, k2 = both(*corners, "row")
    tile, probe, amps_now, tab = call(
        stage_kernel,
        [shape(*tile.shape), shape(*probe.shape), shape(1, *amps.shape[1:]), jax.ShapeDtypeStruct(tab.shape, BF16)],
        tile, probe, amps_now, tab, flops=10**9)

    plain = [shape(2, tall, wide), shape(2, tall, wide), shape(maps, n, n)]
    messages = [shape(2, tall, n)] * 2 + [shape(2, n, cols - n)] * 2
    ext, terms, grads, around, *sends = call(
        first_kernel, plain + [jax.ShapeDtypeStruct((9 * size, n), jnp.int32)] + messages,
        offsets, offsets, tile, probe, amps_now, tab, r1, r2, c1, c2, k1, k2, smem=1, flops=flops)

    def light(batch, around):
        return call(
            functools.partial(light_kernel, batch, pos), [shape(tall, wide)], around, probe, smem=1,
            scratch=[pltpu.VMEM((tall + 2 * n, wide + 2 * n), F32)], flops=10**9)[0]

    for batch in range(batches - 1):
        c1, c2 = both(*sends[:2], "col")
        m1, m2 = both(*sends[2:4], "row")
        if batch == 0:
            weights = [light(0, around)]
        else:
            weights.append(light(batch + 1, around))
        c1, c2, weights = lax.optimization_barrier((c1, c2, weights))
        s1, s2, *sends = call(
            side_kernel, [shape(2, tall, n)] * 2 + [shape(2, 2, n, n)] * 2, terms, c1, c2)
        e1, e2 = both(*sends, "row")
        if batch == 0:
            around, sends = lax.optimization_barrier((around, sends))
            weights.append(light(1, around))
        terms, weights = lax.optimization_barrier((terms, weights))
        args = (offsets, ext, weights[batch], terms, s1, s2, m1, m2, e1, e2, probe, amps, tab, grads)
        if batch + 2 < batches:
            ext, terms, grads, *sends = call(
                functools.partial(next_kernel, batch + 1), plain + messages, *args, smem=1, flops=flops)
        else:
            ext, terms, keep, send, *sends = call(
                functools.partial(last_kernel, batch + 1),
                plain[:2] + [shape(maps, half, n)] * 2 + [shape(2, half, wide)] * 2,
                *args, smem=1, flops=flops, scratch=[pltpu.VMEM((maps, n, n), F32)])
    got = swap(send, "col", 0)
    got, sends = lax.optimization_barrier((got, sends))
    r1, r2 = both(*sends, "row")

    def rest(r1, r2):
        c1, c2 = both(*call(last_side_kernel, [shape(rows, n)] * 2, terms, r1, r2), "col")
        return call(object_kernel, [shape(2, rows, cols)], ext, weights[-1], terms, r1, r2, c1, c2)[0]

    probe_step, object_new = all_sum(keep, send, got, (r1, r2), rest)
    return object_new, probe_step.reshape(2, modes, n, n)


def all_sum(keep, send, got, beside, rest):
    maps, half, n = keep.shape
    axes = ("row", "col")
    across = lax.axis_size("col")
    devices = lax.axis_size("row") * across
    if across % 2 or half % (devices // 2):
        first = jnp.where(parity("col") == 0, keep, send)
        second = jnp.where(parity("col") == 0, send, keep)
        total = lax.psum(jnp.concatenate([first, second], axis=1), axes)
        return total[:-1] / jnp.sqrt(total[-1] + PROBE_REG), rest(*beside)
    groups = [list(range(k, devices, 2)) for k in range(2)]
    each = 2 * half // devices
    (parts,) = call(parts_kernel, [shape(devices // 2, maps * each, n)], keep, got)
    parts = lax.all_to_all(parts, axes, 0, 0, axis_index_groups=groups, tiled=True)
    parts, beside = lax.optimization_barrier((parts, beside))
    (steps,) = call(step_kernel, [shape(devices // 2, (maps - 1) * each, n)], parts)
    steps, beside = lax.optimization_barrier((steps, beside))
    steps = lax.all_to_all(steps, axes, 0, 0, axis_index_groups=groups, tiled=True)
    object_new = rest(*beside)
    steps, object_new = lax.optimization_barrier((steps, object_new))
    (out,) = call(join_kernel, [shape(maps - 1, n, n)], steps, swap(steps, "col", 0))
    return out, object_new


def solution(mesh):
    placed = (
        P(None, "row", "col"),
        P(),
        P("row", "col", None, None, None, None),
        P("row", "col", None, None, None),
    )
    return jax.shard_map(
        on_device,
        mesh=mesh,
        in_specs=placed,
        out_specs=(P(None, "row", "col"), P()),
        check_vma=False,
    )
```

```python
import functools
import math

import jax
import jax.numpy as jnp
import numpy as np
from jax import lax
from jax.experimental import pallas as pl
from jax.experimental.pallas import tpu as pltpu
from jax.sharding import PartitionSpec as P

AMP_FLOOR = 0.25
OBJECT_REG = 0.5
PROBE_REG = 1.0
MARK = 4096.0
F32 = jnp.float32
BF16 = jnp.bfloat16
LIMIT = 20 * 1024 * 1024


def tables(n):
    k = np.arange(n)
    angle = (np.outer(k, k) % n) * (2.0 * math.pi / n)
    re, im = np.cos(angle) / math.sqrt(n), -np.sin(angle) / math.sqrt(n)
    right = np.block([[re, im], [-im, re]]).astype(np.float32)
    left = np.block([[re, -im], [im, re]]).astype(np.float32)
    both = np.stack([right, left])
    high = both.astype(jnp.bfloat16)
    low = (both - high.astype(np.float32)).astype(jnp.bfloat16)
    return jnp.asarray(np.stack([high, low]))


def call(kernel, out, *args, smem=0, hbm=0, scratch=(), flops=0):
    vmem = pl.BlockSpec(memory_space=pltpu.VMEM)
    specs = [pl.BlockSpec(memory_space=pltpu.SMEM)] * smem + [pl.BlockSpec(memory_space=pltpu.HBM)] * hbm
    specs = specs + [vmem] * (len(args) - smem - hbm)
    nbytes = sum(math.prod(o.shape) * 4 for o in out) + sum(a.size * 4 for a in args)
    return pl.pallas_call(
        kernel,
        out_shape=tuple(out),
        in_specs=specs,
        out_specs=tuple([vmem] * len(out)),
        scratch_shapes=list(scratch),
        compiler_params=pltpu.CompilerParams(vmem_limit_bytes=LIMIT),
        cost_estimate=pl.CostEstimate(flops=flops, bytes_accessed=nbytes, transcendentals=0),
    )(*args)


def shape(*dims):
    return jax.ShapeDtypeStruct(dims, F32)


def split(x):
    high = x.astype(BF16)
    return high, (x - high.astype(F32)).astype(BF16)


def mm(a, b):
    return jnp.dot(a, b, preferred_element_type=F32)


def by_right(x, tab, which):
    high, low = split(x)
    t, u = tab[0, which], tab[1, which]
    return mm(high, t) + (mm(low, t) + mm(high, u))


def by_left(x, tab, which):
    high, low = split(x)
    t, u = tab[0, which], tab[1, which]
    return mm(t, high) + (mm(t, low) + mm(u, high))


def put(ref, lead, row, col, value):
    n = value.shape[0]
    tall, wide = ref.shape[len(lead) :]
    top = pl.multiple_of(jnp.minimum(row // 8, (tall - n) // 8 - 1) * 8, 8)
    base = pl.multiple_of(jnp.minimum(col // n, wide // n - 2) * n, n)
    down, right = row - top, col - base
    tiles = pltpu.roll(value.reshape(n // 8, 8, n), down & 7, 1)
    none = jnp.zeros((1, 8, n), F32)
    sub = lax.broadcasted_iota(jnp.int32, (1, 8, 1), 1)
    tiles = jnp.where(sub < down, jnp.concatenate([none, tiles], axis=0), jnp.concatenate([tiles, none], axis=0))
    moved = pltpu.roll(tiles.reshape(n + 8, n), right & (n - 1), 1)
    lane = lax.broadcasted_iota(jnp.int32, (1, n), 1)
    for at, here in ((base, lane >= right), (base + n, lane < right)):
        block = (*lead, pl.ds(top, n + 8), pl.ds(pl.multiple_of(at, n), n))
        ref[block] = ref[block] + jnp.where(here, moved, 0.0)


def cut(ref, lead, row, col, n):
    tall, wide = ref.shape[len(lead) :]
    top = pl.multiple_of(jnp.minimum(row // 8, (tall - n) // 8 - 1) * 8, 8)
    base = pl.multiple_of(jnp.minimum(col // n, wide // n - 2) * n, n)
    down, right = row - top, col - base
    lane = lax.broadcasted_iota(jnp.int32, (1, n), 1)
    left, after = (
        pltpu.roll(ref[(*lead, pl.ds(top, n + 8), pl.ds(pl.multiple_of(at, n), n))], (n - right) & (n - 1), 1)
        for at in (base, base + n)
    )
    tiles = jnp.where(lane < n - right, left, after).reshape(n // 8 + 1, 8, n)
    tiles = pltpu.roll(tiles, (8 - down) & 7, 1)
    sub = lax.broadcasted_iota(jnp.int32, (1, 8, 1), 1)
    return jnp.where(sub < 8 - down, tiles[:-1], tiles[1:]).reshape(n, n)


def positions(batch, offs, ext, probe, amps, tab, terms, grads, first):
    _, modes, n, _ = probe.shape
    half = n // 2
    terms[...] = jnp.zeros_like(terms)
    if first:
        grads[...] = jnp.zeros_like(grads)

    def one(p):
        row = offs[0, 0, batch, p, 0] + half
        col = offs[0, 0, batch, p, 1] + half
        pr, pi = cut(ext, (0,), row, col, n), cut(ext, (1,), row, col, n)
        waves = []
        for m in range(modes):
            qr, qi = probe[0, m], probe[1, m]
            waves.append(jnp.concatenate([qr * pr - qi * pi, qr * pi + qi * pr], axis=1))
        y = by_right(jnp.concatenate(waves, axis=0), tab, 0)
        z = jnp.concatenate(
            [
                jnp.concatenate([y[m * n : (m + 1) * n, :n] for m in range(modes)], axis=1),
                jnp.concatenate([y[m * n : (m + 1) * n, n:] for m in range(modes)], axis=1),
            ],
            axis=0,
        )
        far = by_left(z, tab, 1)
        square = far * far
        square = square[:n] + square[n:]
        intensity = square[:, :n]
        for m in range(1, modes):
            intensity = intensity + square[:, m * n : (m + 1) * n]
        factor = amps[batch, p] / jnp.maximum(jnp.sqrt(intensity), AMP_FLOOR) - 1.0
        wide = jnp.concatenate([factor] * modes, axis=1)
        h = by_left(far * jnp.concatenate([wide, wide], axis=0), tab, 0)
        h = jnp.concatenate(
            [
                jnp.concatenate([h[:n, m * n : (m + 1) * n], h[n:, m * n : (m + 1) * n]], axis=1)
                for m in range(modes)
            ],
            axis=0,
        )
        change = by_right(h, tab, 1)
        tr = ti = None
        for m in range(modes):
            cr, ci = change[m * n : (m + 1) * n, :n], change[m * n : (m + 1) * n, n:]
            qr, qi = probe[0, m], probe[1, m]
            ar, ai = qr * cr + qi * ci, qr * ci - qi * cr
            tr, ti = (ar, ai) if tr is None else (tr + ar, ti + ai)
            grads[m] = grads[m] + (pr * cr + pi * ci)
            grads[modes + m] = grads[modes + m] + (pr * ci - pi * cr)
        grads[2 * modes] = grads[2 * modes] + (pr * pr + pi * pi)
        put(terms, (0,), row, col, tr)
        put(terms, (1,), row, col, ti)

    for p in range(amps.shape[1]):
        one(p)


def parity(axis):
    return lax.axis_index(axis) % 2


def ends(axis, length, width):
    near = (1 - parity(axis)) * (length - width)
    return pl.multiple_of(near, width), pl.multiple_of(length - width - near, width)


def lower(n):
    return lax.broadcasted_iota(jnp.int32, (1, n), 1) < n // 2


def pack_sides(re_low, im_low, re_high, im_high):
    half = re_low.shape[1] // 2
    keep = lower(2 * half)
    left = jnp.where(keep, re_low, pltpu.roll(im_low, half, 1))
    right = jnp.where(keep, pltpu.roll(re_high, half, 1), im_high)
    even = parity("col") == 0
    return jnp.where(even, right, left), jnp.where(even, left, right)


def by_side(first, second):
    even = parity("col") == 0
    return jnp.where(even, second, first), jnp.where(even, first, second)


def lines(offs):
    return -(-offs.shape[2] * offs.shape[3] // 8) * 8


def code(offs):
    _, _, batches, pos, dims = offs.shape
    rows = [offs[0, 0, b] + int(MARK) for b in range(batches)]
    spare = lines(offs) - batches * pos
    if spare:
        rows.append(jnp.zeros((spare, dims), jnp.int32))
    return jnp.concatenate(rows, axis=0)


def send_kernel(offs, tile, rows_1, rows_2, cols_1, cols_2):
    _, rows, cols = tile.shape
    n = cols_1.shape[1]
    half = n // 2
    coded = code(offs).astype(F32)
    for out, at in zip((rows_1, rows_2), ends("row", rows, half)):
        out[:, :half] = tile[:, pl.ds(at, half)]
        out[:, half:] = jnp.zeros((2, lines(offs), cols), F32)
        out[0, half:, : coded.shape[1]] = coded
    first, second = pack_sides(tile[0, :, :n], tile[1, :, :n], tile[0, :, cols - n :], tile[1, :, cols - n :])
    for out, value in ((cols_1, first), (cols_2, second)):
        out[:rows] = value
        out[rows:] = jnp.zeros((lines(offs), n), F32)
        out[rows:, : coded.shape[1]] = coded


def corner_kernel(cols_1, cols_2, out_1, out_2):
    n = cols_1.shape[1]
    half = n // 2
    rows = cols_1.shape[0] - (out_1.shape[1] - half)
    for out, at in zip((out_1, out_2), ends("row", rows, half)):
        for k, ref in enumerate((cols_1, cols_2)):
            out[k, :half] = ref[pl.ds(at, half)]
            out[k, half:] = ref[rows:]


def put_halo(ext, tile, rows_1, rows_2, cols_1, cols_2, corner_1, corner_2):
    _, rows, cols = tile.shape
    n = cols_1.shape[1]
    half = n // 2
    keep = lower(n)
    even = parity("row") == 0
    above = jnp.where(even, rows_2[:, :half], rows_1[:, :half])
    below = jnp.where(even, rows_1[:, :half], rows_2[:, :half])
    strips = []
    for k, ref in enumerate((cols_1, cols_2)):
        c1, c2 = corner_1[k, :half], corner_2[k, :half]
        strips.append(jnp.concatenate([jnp.where(even, c2, c1), ref[:rows], jnp.where(even, c1, c2)], axis=0))
    left, right = by_side(*strips)
    for ch in range(2):
        body = jnp.concatenate([above[ch], tile[ch], below[ch]], axis=0)
        lf = left if ch == 0 else pltpu.roll(left, half, 1)
        rt = right if ch == 1 else pltpu.roll(right, half, 1)
        turned = [lf] + [pltpu.roll(body[:, k : k + n], half, 1) for k in range(0, cols, n)] + [rt]
        for k in range(len(turned) - 1):
            ext[ch, :, k * n : (k + 1) * n] = jnp.where(keep, turned[k], turned[k + 1])


def give(n, terms, cols_1, cols_2, mid_1, mid_2):
    _, rows, cols = terms.shape
    for out, at in zip((cols_1, cols_2), ends("col", cols, n)):
        out[...] = terms[:, :, pl.ds(at, n)]
    for out, at in zip((mid_1, mid_2), ends("row", rows, n)):
        out[...] = terms[:, pl.ds(at, n), n : cols - n]


def stage_kernel(*refs):
    count = len(refs) // 2
    for src, dst in zip(refs[:count], refs[count:]):
        dst[...] = src[: dst.shape[0]]


def first_kernel(offs, own, tile, probe, amps, tab, rows_1, rows_2, cols_1, cols_2, corner_1, corner_2,
                 ext, terms, grads, around, *sends):
    n = cols_1.shape[1]
    half = n // 2
    rows = tile.shape[1]
    size = lines(own)
    coded = code(own)
    around[:size] = jnp.zeros((size, n), jnp.int32)
    around[:size, : coded.shape[1]] = coded
    blocks = [ref[rows:] for ref in (cols_1, cols_2)]
    for ref, corner in ((rows_1, corner_1), (rows_2, corner_2)):
        blocks += [ref[0, half:, :n], corner[0, half:], corner[1, half:]]
    for k, block in enumerate(blocks):
        around[(k + 1) * size : (k + 2) * size] = block.astype(jnp.int32)
    put_halo(ext, tile, rows_1, rows_2, cols_1, cols_2, corner_1, corner_2)
    positions(0, offs, ext, probe, amps, tab, terms, grads, True)
    give(n, terms, *sends)


def side_kernel(terms, got_1, got_2, side_1, side_2, send_1, send_2):
    n = got_1.shape[2]
    _, rows, cols = terms.shape
    for side, got, at in zip((side_1, side_2), (got_1, got_2), ends("col", cols, n)):
        side[...] = terms[:, :, pl.ds(at, n)] + got[...]
    for out, at in zip((send_1, send_2), ends("row", rows, n)):
        for k, side in enumerate((side_1, side_2)):
            out[k] = side[:, pl.ds(at, n)]


def update(ext, old, weight, terms, side_1, side_2, mid_1, mid_2, ends_1, ends_2):
    n = side_1.shape[2]
    _, rows, cols = old.shape
    at_rows = ends("row", rows, n)
    inner = slice(n, cols - n)
    for ch in range(2):
        for k, (side, at) in enumerate(zip((side_1, side_2), ends("col", cols, n))):
            here = pl.ds(at, n)
            ext[ch, :, here] = old[ch, :, here] + side[ch] * weight[:, here]
            for got, top in zip((ends_1, ends_2), at_rows):
                there = pl.ds(top, n)
                ext[ch, there, here] = ext[ch, there, here] + got[k, ch] * weight[there, here]
        ext[ch, :, inner] = old[ch, :, inner] + terms[ch, :, inner] * weight[:, inner]
        for got, top in zip((mid_1, mid_2), at_rows):
            there = pl.ds(top, n)
            ext[ch, there, inner] = ext[ch, there, inner] + got[ch] * weight[there, inner]


def next_kernel(batch, offs, old, weight, old_terms, side_1, side_2, mid_1, mid_2, ends_1, ends_2, probe, amps, tab,
                grads_in, ext, terms, grads, *sends):
    update(ext, old, weight, old_terms, side_1, side_2, mid_1, mid_2, ends_1, ends_2)
    grads[...] = grads_in[...]
    positions(batch, offs, ext, probe, amps, tab, terms, grads, False)
    give(probe.shape[2], terms, *sends)


def last_kernel(batch, offs, old, weight, old_terms, side_1, side_2, mid_1, mid_2, ends_1, ends_2, probe, amps, tab,
                grads_in, ext, terms, keep, send, cols_1, cols_2, grads):
    n = probe.shape[2]
    half = n // 2
    update(ext, old, weight, old_terms, side_1, side_2, mid_1, mid_2, ends_1, ends_2)
    grads[...] = grads_in[...]
    positions(batch, offs, ext, probe, amps, tab, terms, grads, False)
    mine = pl.multiple_of(parity("col") * half, half)
    keep[...] = grads[:, pl.ds(mine, half)]
    send[...] = grads[:, pl.ds(pl.multiple_of(half - mine, half), half)]
    cols = terms.shape[2]
    cols_1[...], cols_2[...] = pack_sides(*(terms[ch, :, k : k + n] for k in (0, cols - n) for ch in range(2)))


def own_cols(terms, ch, cols_1, cols_2, at):
    n = cols_1.shape[1]
    cols = terms.shape[2]
    keep = lower(n)
    left, right = by_side(cols_1[at], cols_2[at])
    if ch == 0:
        left = pltpu.roll(left, n // 2, 1)
    else:
        right = pltpu.roll(right, n // 2, 1)
    blocks = [terms[ch, at, k : k + n] for k in range(0, cols, n)]
    blocks[0] = blocks[0] + jnp.where(keep, 0.0, left)
    blocks[-1] = blocks[-1] + jnp.where(keep, right, 0.0)
    return blocks


def turned(blocks):
    n = blocks[0].shape[1]
    keep = lower(n)
    moved = [pltpu.roll(block, n // 2, 1) for block in blocks]
    return [jnp.where(keep, moved[k], moved[k + 1]) for k in range(len(moved) - 1)]


def last_side_kernel(terms, cols_1, cols_2, rows_1, rows_2):
    n = cols_1.shape[1]
    half = n // 2
    for out, at in zip((rows_1, rows_2), ends("row", terms.shape[1], half)):
        for ch in range(2):
            for k, block in enumerate(turned(own_cols(terms, ch, cols_1, cols_2, pl.ds(at, half)))):
                out[ch, :, k * n : (k + 1) * n] = block


def object_kernel(old, weight, terms, cols_1, cols_2, rows_1, rows_2, out):
    _, rows, cols = old.shape
    n = cols_1.shape[1]
    half = n // 2
    tile = rows - n
    own = pl.ds(half, tile)
    gap = jnp.zeros((tile - n, n), F32)
    even = parity("row") == 0
    scales = turned([weight[own, k : k + n] for k in range(0, cols, n)])
    for ch in range(2):
        blocks = turned(own_cols(terms, ch, cols_1, cols_2, own))
        olds = turned([old[ch, own, k : k + n] for k in range(0, cols, n)])
        for k, block in enumerate(blocks):
            at = slice(k * n, (k + 1) * n)
            first, second = rows_1[ch, :, at], rows_2[ch, :, at]
            got = [jnp.where(even, second, first), gap, jnp.where(even, first, second)]
            out[ch, :, at] = olds[k] + (block + jnp.concatenate(got, axis=0)) * scales[k]


def light_kernel(batch, pos, around, probe, weight, light):
    _, modes, n, _ = probe.shape
    half = n // 2
    rows, cols = weight.shape
    tile_r, tile_c = rows - n, cols - n
    lit = None
    for m in range(modes):
        s = probe[0, m] * probe[0, m] + probe[1, m] * probe[1, m]
        lit = s if lit is None else lit + s
    light[...] = jnp.zeros_like(light)
    big = int(MARK)
    size = around.shape[0] // 9

    def side(which, axis):
        step = 1 - 2 * parity(axis)
        return jnp.where(which == 0, 0, jnp.where(which == 1, step, -step))

    def one(i, carry):
        k, p = i // pos, i % pos
        at = k * size + batch * pos + p
        there = around[at, 0] > 0
        row = around[at, 0] - big + half + side(k // 3, "row") * tile_r
        col = around[at, 1] - big + half + side(k % 3, "col") * tile_c
        hit = there & (row > -n) & (row < rows) & (col > -n) & (col < cols)

        @pl.when(hit)
        def _():
            put(light, (), row + n, col + n, lit)

        return carry

    lax.fori_loop(0, 9 * pos, one, 0)
    r = lax.broadcasted_iota(jnp.int32, (rows, cols), 0)
    c = lax.broadcasted_iota(jnp.int32, (rows, cols), 1)
    odd_r, odd_c = parity("row"), parity("col")
    low_r = jnp.where(around[(6 - 3 * odd_r) * size, 0] > 0, 0, half)
    high_r = jnp.where(around[(3 + 3 * odd_r) * size, 0] > 0, rows, rows - half)
    low_c = jnp.where(around[(2 - odd_c) * size, 0] > 0, 0, half)
    high_c = jnp.where(around[(1 + odd_c) * size, 0] > 0, cols, cols - half)
    inside = (r >= low_r) & (r < high_r) & (c >= low_c) & (c < high_c)
    total = light[n : n + rows, n : n + cols]
    weight[...] = jnp.where(inside, 1.0 / (total + OBJECT_REG), 0.0)


def parts_kernel(keep, got, parts):
    maps = keep.shape[0]
    each = parts.shape[1] // maps
    for m in range(maps):
        total = keep[m] + got[m]
        for i in range(parts.shape[0]):
            parts[i, m * each : (m + 1) * each] = total[i * each : (i + 1) * each]


def step_kernel(parts, out):
    total = parts[0]
    for i in range(1, parts.shape[0]):
        total = total + parts[i]
    each = total.shape[0] - out.shape[1]
    maps = total.shape[0] // each
    scale = 1.0 / jnp.sqrt(total[(maps - 1) * each :] + PROBE_REG)
    step = jnp.concatenate([total[m * each : (m + 1) * each] * scale for m in range(maps - 1)], axis=0)
    for i in range(out.shape[0]):
        out[i] = step


def join_kernel(mine, other, out):
    maps, n, _ = out.shape
    half = n // 2
    each = mine.shape[1] // maps
    at = pl.multiple_of(parity("col") * half, half)
    for ref, top in ((mine, at), (other, pl.multiple_of(half - at, half))):
        for m in range(maps):
            out[m, pl.ds(top, half)] = jnp.concatenate(
                [ref[i, m * each : (m + 1) * each] for i in range(ref.shape[0])], axis=0)


def swap(value, axis, phase):
    size = lax.axis_size(axis)
    pairs = [(i, i + 1) for i in range(phase, size - 1, 2)]
    return lax.ppermute(value, axis, pairs + [(j, i) for i, j in pairs])


def both(first, second, axis):
    return swap(first, axis, 0), swap(second, axis, 1)


def on_device(tile, probe, amplitudes, offsets):
    _, modes, n, _ = probe.shape
    half = n // 2
    _, rows, cols = tile.shape
    tall, wide = rows + n, cols + n
    amps = amplitudes[0, 0]
    batches, pos = offsets.shape[2:4]
    maps = 2 * modes + 1
    tab = tables(n)
    flops = pos * modes * 2 * 2 * 4 * 2 * n**3 * 3

    size = lines(offsets)
    sends = call(send_kernel, [shape(2, half + size, cols)] * 2 + [shape(rows + size, n)] * 2, offsets, tile)
    c1, c2 = both(*sends[2:], "col")
    r1, r2 = both(*sends[:2], "row")
    corners = call(corner_kernel, [shape(2, half + size, n)] * 2, c1, c2)
    corners, tile, probe, amps_now, tab = lax.optimization_barrier((corners, tile, probe, amps, tab))
    k1, k2 = both(*corners, "row")
    tile, probe, amps_now, tab = call(
        stage_kernel,
        [shape(*tile.shape), shape(*probe.shape), shape(1, *amps.shape[1:]), jax.ShapeDtypeStruct(tab.shape, BF16)],
        tile, probe, amps_now, tab, flops=10**9)

    plain = [shape(2, tall, wide), shape(2, tall, wide), shape(maps, n, n)]
    messages = [shape(2, tall, n)] * 2 + [shape(2, n, cols - n)] * 2
    ext, terms, grads, around, *sends = call(
        first_kernel, plain + [jax.ShapeDtypeStruct((9 * size, n), jnp.int32)] + messages,
        offsets, offsets, tile, probe, amps_now, tab, r1, r2, c1, c2, k1, k2, smem=1, flops=flops)

    def light(batch, around):
        return call(
            functools.partial(light_kernel, batch, pos), [shape(tall, wide)], around, probe, smem=1,
            scratch=[pltpu.VMEM((tall + 2 * n, wide + 2 * n), F32)], flops=10**9)[0]

    weights = [light(batch, around) for batch in range(min(2, batches))]
    for batch in range(batches - 1):
        c1, c2 = both(*sends[:2], "col")
        m1, m2 = both(*sends[2:4], "row")
        s1, s2, *sends = call(
            side_kernel, [shape(2, tall, n)] * 2 + [shape(2, 2, n, n)] * 2, terms, c1, c2)
        e1, e2 = both(*sends, "row")
        if len(weights) < batches and batch > 0:
            around, c1 = lax.optimization_barrier((around, c1))
            weights.append(light(batch + 1, around))
        terms, weights = lax.optimization_barrier((terms, weights))
        args = (offsets, ext, weights[batch], terms, s1, s2, m1, m2, e1, e2, probe, amps, tab, grads)
        if batch + 2 < batches:
            ext, terms, grads, *sends = call(
                functools.partial(next_kernel, batch + 1), plain + messages, *args, smem=1, flops=flops)
        else:
            ext, terms, keep, send, *sends = call(
                functools.partial(last_kernel, batch + 1),
                plain[:2] + [shape(maps, half, n)] * 2 + [shape(tall, n)] * 2,
                *args, smem=1, flops=flops, scratch=[pltpu.VMEM((maps, n, n), F32)])
    got = swap(send, "col", 0)
    got, sends = lax.optimization_barrier((got, sends))
    c1, c2 = both(*sends, "col")

    def rest(c1, c2):
        r1, r2 = both(*call(last_side_kernel, [shape(2, half, cols)] * 2, terms, c1, c2), "row")
        return call(object_kernel, [shape(2, rows, cols)], ext, weights[-1], terms, c1, c2, r1, r2)[0]

    probe_step, object_new = all_sum(keep, send, got, (c1, c2), rest)
    return object_new, probe_step.reshape(2, modes, n, n)


def all_sum(keep, send, got, beside, rest):
    maps, half, n = keep.shape
    axes = ("row", "col")
    across = lax.axis_size("col")
    devices = lax.axis_size("row") * across
    if across % 2 or half % (devices // 2):
        first = jnp.where(parity("col") == 0, keep, send)
        second = jnp.where(parity("col") == 0, send, keep)
        total = lax.psum(jnp.concatenate([first, second], axis=1), axes)
        return total[:-1] / jnp.sqrt(total[-1] + PROBE_REG), rest(*beside)
    groups = [list(range(k, devices, 2)) for k in range(2)]
    each = 2 * half // devices
    (parts,) = call(parts_kernel, [shape(devices // 2, maps * each, n)], keep, got)
    parts = lax.all_to_all(parts, axes, 0, 0, axis_index_groups=groups, tiled=True)
    parts, beside = lax.optimization_barrier((parts, beside))
    (steps,) = call(step_kernel, [shape(devices // 2, (maps - 1) * each, n)], parts)
    steps, beside = lax.optimization_barrier((steps, beside))
    steps = lax.all_to_all(steps, axes, 0, 0, axis_index_groups=groups, tiled=True)
    object_new = rest(*beside)
    steps, object_new = lax.optimization_barrier((steps, object_new))
    (out,) = call(join_kernel, [shape(maps - 1, n, n)], steps, swap(steps, "col", 0))
    return out, object_new


def solution(mesh):
    placed = (
        P(None, "row", "col"),
        P(),
        P("row", "col", None, None, None, None),
        P("row", "col", None, None, None),
    )
    return jax.shard_map(
        on_device,
        mesh=mesh,
        in_specs=placed,
        out_specs=(P(None, "row", "col"), P()),
        check_vma=False,
    )
```

```python
import functools
import math

import jax
import jax.numpy as jnp
import numpy as np
from jax import lax
from jax.experimental import pallas as pl
from jax.experimental.pallas import tpu as pltpu
from jax.sharding import PartitionSpec as P

AMP_FLOOR = 0.25
OBJECT_REG = 0.5
PROBE_REG = 1.0
MARK = 4096.0
F32 = jnp.float32
BF16 = jnp.bfloat16
LIMIT = 20 * 1024 * 1024


def tables(n):
    k = np.arange(n)
    angle = (np.outer(k, k) % n) * (2.0 * math.pi / n)
    re, im = np.cos(angle) / math.sqrt(n), -np.sin(angle) / math.sqrt(n)
    right = np.block([[re, im], [-im, re]]).astype(np.float32)
    left = np.block([[re, -im], [im, re]]).astype(np.float32)
    both = np.stack([right, left])
    high = both.astype(jnp.bfloat16)
    low = (both - high.astype(np.float32)).astype(jnp.bfloat16)
    return jnp.asarray(np.stack([high, low]))


def call(kernel, out, *args, smem=0, hbm=0, scratch=(), flops=0):
    vmem = pl.BlockSpec(memory_space=pltpu.VMEM)
    specs = [pl.BlockSpec(memory_space=pltpu.SMEM)] * smem + [pl.BlockSpec(memory_space=pltpu.HBM)] * hbm
    specs = specs + [vmem] * (len(args) - smem - hbm)
    nbytes = sum(math.prod(o.shape) * 4 for o in out) + sum(a.size * 4 for a in args)
    return pl.pallas_call(
        kernel,
        out_shape=tuple(out),
        in_specs=specs,
        out_specs=tuple([vmem] * len(out)),
        scratch_shapes=list(scratch),
        compiler_params=pltpu.CompilerParams(vmem_limit_bytes=LIMIT),
        cost_estimate=pl.CostEstimate(flops=flops, bytes_accessed=nbytes, transcendentals=0),
    )(*args)


def shape(*dims):
    return jax.ShapeDtypeStruct(dims, F32)


def split(x):
    high = x.astype(BF16)
    return high, (x - high.astype(F32)).astype(BF16)


def mm(a, b):
    return jnp.dot(a, b, preferred_element_type=F32)


def by_right(x, tab, which):
    high, low = split(x)
    t, u = tab[0, which], tab[1, which]
    return mm(high, t) + (mm(low, t) + mm(high, u))


def by_left(x, tab, which):
    high, low = split(x)
    t, u = tab[0, which], tab[1, which]
    return mm(t, high) + (mm(t, low) + mm(u, high))


def put(ref, lead, row, col, value):
    n = value.shape[0]
    tall, wide = ref.shape[len(lead) :]
    top = pl.multiple_of(jnp.minimum(row // 8, (tall - n) // 8 - 1) * 8, 8)
    base = pl.multiple_of(jnp.minimum(col // n, wide // n - 2) * n, n)
    down, right = row - top, col - base
    tiles = pltpu.roll(value.reshape(n // 8, 8, n), down & 7, 1)
    none = jnp.zeros((1, 8, n), F32)
    sub = lax.broadcasted_iota(jnp.int32, (1, 8, 1), 1)
    tiles = jnp.where(sub < down, jnp.concatenate([none, tiles], axis=0), jnp.concatenate([tiles, none], axis=0))
    moved = pltpu.roll(tiles.reshape(n + 8, n), right & (n - 1), 1)
    lane = lax.broadcasted_iota(jnp.int32, (1, n), 1)
    for at, here in ((base, lane >= right), (base + n, lane < right)):
        block = (*lead, pl.ds(top, n + 8), pl.ds(pl.multiple_of(at, n), n))
        ref[block] = ref[block] + jnp.where(here, moved, 0.0)


def cut(ref, lead, row, col, n):
    tall, wide = ref.shape[len(lead) :]
    top = pl.multiple_of(jnp.minimum(row // 8, (tall - n) // 8 - 1) * 8, 8)
    base = pl.multiple_of(jnp.minimum(col // n, wide // n - 2) * n, n)
    down, right = row - top, col - base
    lane = lax.broadcasted_iota(jnp.int32, (1, n), 1)
    left, after = (
        pltpu.roll(ref[(*lead, pl.ds(top, n + 8), pl.ds(pl.multiple_of(at, n), n))], (n - right) & (n - 1), 1)
        for at in (base, base + n)
    )
    tiles = jnp.where(lane < n - right, left, after).reshape(n // 8 + 1, 8, n)
    tiles = pltpu.roll(tiles, (8 - down) & 7, 1)
    sub = lax.broadcasted_iota(jnp.int32, (1, 8, 1), 1)
    return jnp.where(sub < 8 - down, tiles[:-1], tiles[1:]).reshape(n, n)


def positions(batch, offs, ext, probe, amps, tab, terms, grads, first):
    _, modes, n, _ = probe.shape
    half = n // 2
    terms[...] = jnp.zeros_like(terms)
    if first:
        grads[...] = jnp.zeros_like(grads)

    def one(p):
        row = offs[0, 0, batch, p, 0] + half
        col = offs[0, 0, batch, p, 1] + half
        pr, pi = cut(ext, (0,), row, col, n), cut(ext, (1,), row, col, n)
        waves = []
        for m in range(modes):
            qr, qi = probe[0, m], probe[1, m]
            waves.append(jnp.concatenate([qr * pr - qi * pi, qr * pi + qi * pr], axis=1))
        waves = jnp.concatenate(waves, axis=0)
        yield
        y = by_right(waves, tab, 0)
        z = jnp.concatenate(
            [
                jnp.concatenate([y[m * n : (m + 1) * n, :n] for m in range(modes)], axis=1),
                jnp.concatenate([y[m * n : (m + 1) * n, n:] for m in range(modes)], axis=1),
            ],
            axis=0,
        )
        yield
        far = by_left(z, tab, 1)
        yield
        square = far * far
        square = square[:n] + square[n:]
        intensity = square[:, :n]
        for m in range(1, modes):
            intensity = intensity + square[:, m * n : (m + 1) * n]
        factor = amps[batch, p] / jnp.maximum(jnp.sqrt(intensity), AMP_FLOOR) - 1.0
        wide = jnp.concatenate([factor] * modes, axis=1)
        far = far * jnp.concatenate([wide, wide], axis=0)
        yield
        h = by_left(far, tab, 0)
        h = jnp.concatenate(
            [
                jnp.concatenate([h[:n, m * n : (m + 1) * n], h[n:, m * n : (m + 1) * n]], axis=1)
                for m in range(modes)
            ],
            axis=0,
        )
        yield
        change = by_right(h, tab, 1)
        yield
        tr = ti = None
        for m in range(modes):
            cr, ci = change[m * n : (m + 1) * n, :n], change[m * n : (m + 1) * n, n:]
            qr, qi = probe[0, m], probe[1, m]
            ar, ai = qr * cr + qi * ci, qr * ci - qi * cr
            tr, ti = (ar, ai) if tr is None else (tr + ar, ti + ai)
            grads[m] = grads[m] + (pr * cr + pi * ci)
            grads[modes + m] = grads[modes + m] + (pr * ci - pi * cr)
        grads[2 * modes] = grads[2 * modes] + (pr * pr + pi * pi)
        put(terms, (0,), row, col, tr)
        put(terms, (1,), row, col, ti)

    works = [one(p) for p in range(amps.shape[1])]
    while works:
        works = [work for work in works if next(work, works) is not works]


def parity(axis):
    return lax.axis_index(axis) % 2


def ends(axis, length, width):
    near = (1 - parity(axis)) * (length - width)
    return pl.multiple_of(near, width), pl.multiple_of(length - width - near, width)


def lower(n):
    return lax.broadcasted_iota(jnp.int32, (1, n), 1) < n // 2


def pack_sides(re_low, im_low, re_high, im_high):
    half = re_low.shape[1] // 2
    keep = lower(2 * half)
    left = jnp.where(keep, re_low, pltpu.roll(im_low, half, 1))
    right = jnp.where(keep, pltpu.roll(re_high, half, 1), im_high)
    even = parity("col") == 0
    return jnp.where(even, right, left), jnp.where(even, left, right)


def by_side(first, second):
    even = parity("col") == 0
    return jnp.where(even, second, first), jnp.where(even, first, second)


def lines(offs):
    return -(-offs.shape[2] * offs.shape[3] // 8) * 8


def code(offs):
    _, _, batches, pos, dims = offs.shape
    rows = [offs[0, 0, b] + int(MARK) for b in range(batches)]
    spare = lines(offs) - batches * pos
    if spare:
        rows.append(jnp.zeros((spare, dims), jnp.int32))
    return jnp.concatenate(rows, axis=0)


def send_kernel(offs, tile, rows_1, rows_2, cols_1, cols_2):
    _, rows, cols = tile.shape
    n = cols_1.shape[1]
    half = n // 2
    coded = code(offs).astype(F32)
    for out, at in zip((rows_1, rows_2), ends("row", rows, half)):
        out[:, :half] = tile[:, pl.ds(at, half)]
        out[:, half:] = jnp.zeros((2, lines(offs), cols), F32)
        out[0, half:, : coded.shape[1]] = coded
    first, second = pack_sides(tile[0, :, :n], tile[1, :, :n], tile[0, :, cols - n :], tile[1, :, cols - n :])
    for out, value in ((cols_1, first), (cols_2, second)):
        out[:rows] = value
        out[rows:] = jnp.zeros((lines(offs), n), F32)
        out[rows:, : coded.shape[1]] = coded


def corner_kernel(cols_1, cols_2, out_1, out_2):
    n = cols_1.shape[1]
    half = n // 2
    rows = cols_1.shape[0] - (out_1.shape[1] - half)
    for out, at in zip((out_1, out_2), ends("row", rows, half)):
        for k, ref in enumerate((cols_1, cols_2)):
            out[k, :half] = ref[pl.ds(at, half)]
            out[k, half:] = ref[rows:]


def put_halo(ext, tile, rows_1, rows_2, cols_1, cols_2, corner_1, corner_2):
    _, rows, cols = tile.shape
    n = cols_1.shape[1]
    half = n // 2
    keep = lower(n)
    even = parity("row") == 0
    above = jnp.where(even, rows_2[:, :half], rows_1[:, :half])
    below = jnp.where(even, rows_1[:, :half], rows_2[:, :half])
    strips = []
    for k, ref in enumerate((cols_1, cols_2)):
        c1, c2 = corner_1[k, :half], corner_2[k, :half]
        strips.append(jnp.concatenate([jnp.where(even, c2, c1), ref[:rows], jnp.where(even, c1, c2)], axis=0))
    left, right = by_side(*strips)
    for ch in range(2):
        body = jnp.concatenate([above[ch], tile[ch], below[ch]], axis=0)
        lf = left if ch == 0 else pltpu.roll(left, half, 1)
        rt = right if ch == 1 else pltpu.roll(right, half, 1)
        turned = [lf] + [pltpu.roll(body[:, k : k + n], half, 1) for k in range(0, cols, n)] + [rt]
        for k in range(len(turned) - 1):
            ext[ch, :, k * n : (k + 1) * n] = jnp.where(keep, turned[k], turned[k + 1])


def give(n, terms, cols_1, cols_2, mid_1, mid_2):
    _, rows, cols = terms.shape
    for out, at in zip((cols_1, cols_2), ends("col", cols, n)):
        out[...] = terms[:, :, pl.ds(at, n)]
    for out, at in zip((mid_1, mid_2), ends("row", rows, n)):
        out[...] = terms[:, pl.ds(at, n), n : cols - n]


def stage_kernel(*refs):
    count = len(refs) // 2
    for src, dst in zip(refs[:count], refs[count:]):
        dst[...] = src[: dst.shape[0]]


def first_kernel(offs, own, tile, probe, amps, tab, rows_1, rows_2, cols_1, cols_2, corner_1, corner_2,
                 ext, terms, grads, around, *sends):
    n = cols_1.shape[1]
    half = n // 2
    rows = tile.shape[1]
    size = lines(own)
    blocks = [code(own)] + [ref[rows:].astype(jnp.int32) for ref in (cols_1, cols_2)]
    for ref, corner in ((rows_1, corner_1), (rows_2, corner_2)):
        blocks += [b.astype(jnp.int32) for b in (ref[0, half:, :n], corner[0, half:], corner[1, half:])]
    lane = lax.broadcasted_iota(jnp.int32, (size, n), 1)
    for dim in range(2):
        value = jnp.zeros((size, n), jnp.int32)
        for k, block in enumerate(blocks):
            value = jnp.where(lane == k, block[:, dim : dim + 1], value)
        around[dim * size : (dim + 1) * size] = value
    put_halo(ext, tile, rows_1, rows_2, cols_1, cols_2, corner_1, corner_2)
    positions(0, offs, ext, probe, amps, tab, terms, grads, True)
    give(n, terms, *sends)


def side_kernel(terms, got_1, got_2, side_1, side_2, send_1, send_2):
    n = got_1.shape[2]
    _, rows, cols = terms.shape
    for side, got, at in zip((side_1, side_2), (got_1, got_2), ends("col", cols, n)):
        side[...] = terms[:, :, pl.ds(at, n)] + got[...]
    for out, at in zip((send_1, send_2), ends("row", rows, n)):
        for k, side in enumerate((side_1, side_2)):
            out[k] = side[:, pl.ds(at, n)]


def update(ext, old, weight, terms, side_1, side_2, mid_1, mid_2, ends_1, ends_2):
    n = side_1.shape[2]
    _, rows, cols = old.shape
    at_rows = ends("row", rows, n)
    inner = slice(n, cols - n)
    for ch in range(2):
        for k, (side, at) in enumerate(zip((side_1, side_2), ends("col", cols, n))):
            here = pl.ds(at, n)
            ext[ch, :, here] = old[ch, :, here] + side[ch] * weight[:, here]
            for got, top in zip((ends_1, ends_2), at_rows):
                there = pl.ds(top, n)
                ext[ch, there, here] = ext[ch, there, here] + got[k, ch] * weight[there, here]
        ext[ch, :, inner] = old[ch, :, inner] + terms[ch, :, inner] * weight[:, inner]
        for got, top in zip((mid_1, mid_2), at_rows):
            there = pl.ds(top, n)
            ext[ch, there, inner] = ext[ch, there, inner] + got[ch] * weight[there, inner]


def next_kernel(batch, offs, old, weight, old_terms, side_1, side_2, mid_1, mid_2, ends_1, ends_2, probe, amps, tab,
                grads_in, ext, terms, grads, *sends):
    update(ext, old, weight, old_terms, side_1, side_2, mid_1, mid_2, ends_1, ends_2)
    grads[...] = grads_in[...]
    positions(batch, offs, ext, probe, amps, tab, terms, grads, False)
    give(probe.shape[2], terms, *sends)


def last_kernel(batch, offs, old, weight, old_terms, side_1, side_2, mid_1, mid_2, ends_1, ends_2, probe, amps, tab,
                grads_in, ext, terms, keep, send, cols_1, cols_2, grads):
    n = probe.shape[2]
    half = n // 2
    update(ext, old, weight, old_terms, side_1, side_2, mid_1, mid_2, ends_1, ends_2)
    grads[...] = grads_in[...]
    positions(batch, offs, ext, probe, amps, tab, terms, grads, False)
    mine = pl.multiple_of(parity("col") * half, half)
    keep[...] = grads[:, pl.ds(mine, half)]
    send[...] = grads[:, pl.ds(pl.multiple_of(half - mine, half), half)]
    cols = terms.shape[2]
    cols_1[...], cols_2[...] = pack_sides(*(terms[ch, :, k : k + n] for k in (0, cols - n) for ch in range(2)))


def own_cols(terms, ch, cols_1, cols_2, at):
    n = cols_1.shape[1]
    cols = terms.shape[2]
    keep = lower(n)
    left, right = by_side(cols_1[at], cols_2[at])
    if ch == 0:
        left = pltpu.roll(left, n // 2, 1)
    else:
        right = pltpu.roll(right, n // 2, 1)
    blocks = [terms[ch, at, k : k + n] for k in range(0, cols, n)]
    blocks[0] = blocks[0] + jnp.where(keep, 0.0, left)
    blocks[-1] = blocks[-1] + jnp.where(keep, right, 0.0)
    return blocks


def turned(blocks):
    n = blocks[0].shape[1]
    keep = lower(n)
    moved = [pltpu.roll(block, n // 2, 1) for block in blocks]
    return [jnp.where(keep, moved[k], moved[k + 1]) for k in range(len(moved) - 1)]


def last_side_kernel(terms, cols_1, cols_2, rows_1, rows_2):
    n = cols_1.shape[1]
    half = n // 2
    for out, at in zip((rows_1, rows_2), ends("row", terms.shape[1], half)):
        for ch in range(2):
            for k, block in enumerate(turned(own_cols(terms, ch, cols_1, cols_2, pl.ds(at, half)))):
                out[ch, :, k * n : (k + 1) * n] = block


def object_kernel(old, weight, terms, cols_1, cols_2, rows_1, rows_2, out):
    _, rows, cols = old.shape
    n = cols_1.shape[1]
    half = n // 2
    tile = rows - n
    own = pl.ds(half, tile)
    gap = jnp.zeros((tile - n, n), F32)
    even = parity("row") == 0
    scales = turned([weight[own, k : k + n] for k in range(0, cols, n)])
    for ch in range(2):
        blocks = turned(own_cols(terms, ch, cols_1, cols_2, own))
        olds = turned([old[ch, own, k : k + n] for k in range(0, cols, n)])
        for k, block in enumerate(blocks):
            at = slice(k * n, (k + 1) * n)
            first, second = rows_1[ch, :, at], rows_2[ch, :, at]
            got = [jnp.where(even, second, first), gap, jnp.where(even, first, second)]
            out[ch, :, at] = olds[k] + (block + jnp.concatenate(got, axis=0)) * scales[k]


def light_kernel(batch, pos, around, probe, weight, light):
    _, modes, n, _ = probe.shape
    half = n // 2
    rows, cols = weight.shape
    size = around.shape[0] // 2
    lit = None
    for m in range(modes):
        s = probe[0, m] * probe[0, m] + probe[1, m] * probe[1, m]
        lit = s if lit is None else lit + s
    light[...] = jnp.zeros_like(light)
    odd_r, odd_c = parity("row"), parity("col")
    up, down = 2 - odd_r, 1 + odd_r
    left, right = 2 - odd_c, 1 + odd_c

    def there(k):
        return jnp.where(around[0, k] > 0, 1.0, 0.0)

    for top, first, count in (
        (n, n, 1.0 + there(3 * up + left)),
        (n, cols, there(right) + there(3 * up)),
        (rows, n, there(3 * down) + there(left)),
        (rows, cols, 1.0 + there(3 * down + right)),
    ):
        light[top : top + n, first : first + n] = lit * count

    def side(which, odd):
        step = 1 - 2 * odd
        return jnp.where(which == 0, 0, jnp.where(which == 1, step, -step))

    def one(i, carry):
        k, p = i // (pos - 2), 2 + i % (pos - 2)
        at = batch * pos + p
        row = around[at, k] - int(MARK) + half + side(k // 3, odd_r) * (rows - n)
        col = around[size + at, k] - int(MARK) + half + side(k % 3, odd_c) * (cols - n)

        @pl.when((around[at, k] > 0) & (row > -n) & (row < rows) & (col > -n) & (col < cols))
        def _():
            put(light, (), row + n, col + n, lit)

        return carry

    lax.fori_loop(0, 9 * (pos - 2), one, 0)
    low_r = jnp.where(around[0, 3 * up] > 0, 0, half)
    high_r = jnp.where(around[0, 3 * down] > 0, rows, rows - half)
    low_c = jnp.where(around[0, left] > 0, 0, half)
    high_c = jnp.where(around[0, right] > 0, cols, cols - half)
    r = lax.broadcasted_iota(jnp.int32, (rows, cols), 0)
    c = lax.broadcasted_iota(jnp.int32, (rows, cols), 1)
    inside = (r >= low_r) & (r < high_r) & (c >= low_c) & (c < high_c)
    total = light[n : n + rows, n : n + cols]
    weight[...] = jnp.where(inside, 1.0 / (total + OBJECT_REG), 0.0)


def parts_kernel(keep, got, parts):
    maps = keep.shape[0]
    each = parts.shape[1] // maps
    for m in range(maps):
        total = keep[m] + got[m]
        for i in range(parts.shape[0]):
            parts[i, m * each : (m + 1) * each] = total[i * each : (i + 1) * each]


def step_kernel(parts, out):
    total = parts[0]
    for i in range(1, parts.shape[0]):
        total = total + parts[i]
    each = total.shape[0] - out.shape[1]
    maps = total.shape[0] // each
    scale = 1.0 / jnp.sqrt(total[(maps - 1) * each :] + PROBE_REG)
    step = jnp.concatenate([total[m * each : (m + 1) * each] * scale for m in range(maps - 1)], axis=0)
    for i in range(out.shape[0]):
        out[i] = step


def join_kernel(mine, other, out):
    maps, n, _ = out.shape
    half = n // 2
    each = mine.shape[1] // maps
    at = pl.multiple_of(parity("col") * half, half)
    for ref, top in ((mine, at), (other, pl.multiple_of(half - at, half))):
        for m in range(maps):
            out[m, pl.ds(top, half)] = jnp.concatenate(
                [ref[i, m * each : (m + 1) * each] for i in range(ref.shape[0])], axis=0)


def swap(value, axis, phase):
    size = lax.axis_size(axis)
    pairs = [(i, i + 1) for i in range(phase, size - 1, 2)]
    return lax.ppermute(value, axis, pairs + [(j, i) for i, j in pairs])


def both(first, second, axis):
    return swap(first, axis, 0), swap(second, axis, 1)


def on_device(tile, probe, amplitudes, offsets):
    _, modes, n, _ = probe.shape
    half = n // 2
    _, rows, cols = tile.shape
    tall, wide = rows + n, cols + n
    amps = amplitudes[0, 0]
    batches, pos = offsets.shape[2:4]
    maps = 2 * modes + 1
    tab = tables(n)
    flops = pos * modes * 2 * 2 * 4 * 2 * n**3 * 3

    size = lines(offsets)
    sends = call(send_kernel, [shape(2, half + size, cols)] * 2 + [shape(rows + size, n)] * 2, offsets, tile)
    c1, c2 = both(*sends[2:], "col")
    r1, r2 = both(*sends[:2], "row")
    corners = call(corner_kernel, [shape(2, half + size, n)] * 2, c1, c2)
    corners, tile, probe, amps_now, tab = lax.optimization_barrier((corners, tile, probe, amps, tab))
    k1, k2 = both(*corners, "row")
    tile, probe, amps_now, tab = call(
        stage_kernel,
        [shape(*tile.shape), shape(*probe.shape), shape(1, *amps.shape[1:]), jax.ShapeDtypeStruct(tab.shape, BF16)],
        tile, probe, amps_now, tab, flops=10**9)

    plain = [shape(2, tall, wide), shape(2, tall, wide), shape(maps, n, n)]
    messages = [shape(2, tall, n)] * 2 + [shape(2, n, cols - n)] * 2
    ext, terms, grads, around, *sends = call(
        first_kernel, plain + [jax.ShapeDtypeStruct((2 * size, n), jnp.int32)] + messages,
        offsets, offsets, tile, probe, amps_now, tab, r1, r2, c1, c2, k1, k2, smem=1, flops=flops)

    def light(batch, around):
        return call(
            functools.partial(light_kernel, batch, pos), [shape(tall, wide)], around, probe, smem=1,
            scratch=[pltpu.VMEM((tall + 2 * n, wide + 2 * n), F32)], flops=10**9)[0]

    weights = [light(batch, around) for batch in range(min(2, batches))]
    for batch in range(batches - 1):
        c1, c2 = both(*sends[:2], "col")
        m1, m2 = both(*sends[2:4], "row")
        s1, s2, *sends = call(
            side_kernel, [shape(2, tall, n)] * 2 + [shape(2, 2, n, n)] * 2, terms, c1, c2)
        e1, e2 = both(*sends, "row")
        if len(weights) < batches and batch > 0:
            around, c1 = lax.optimization_barrier((around, c1))
            weights.append(light(batch + 1, around))
        terms, weights = lax.optimization_barrier((terms, weights))
        args = (offsets, ext, weights[batch], terms, s1, s2, m1, m2, e1, e2, probe, amps, tab, grads)
        if batch + 2 < batches:
            ext, terms, grads, *sends = call(
                functools.partial(next_kernel, batch + 1), plain + messages, *args, smem=1, flops=flops)
        else:
            ext, terms, keep, send, *sends = call(
                functools.partial(last_kernel, batch + 1),
                plain[:2] + [shape(maps, half, n)] * 2 + [shape(tall, n)] * 2,
                *args, smem=1, flops=flops, scratch=[pltpu.VMEM((maps, n, n), F32)])
    got = swap(send, "col", 0)
    got, sends = lax.optimization_barrier((got, sends))
    c1, c2 = both(*sends, "col")

    def send_rows(c1, c2):
        return both(*call(last_side_kernel, [shape(2, half, cols)] * 2, terms, c1, c2), "row")

    probe_step, (c1, c2), (r1, r2) = all_sum(keep, send, got, (c1, c2), send_rows)
    (object_new,) = call(
        object_kernel, [shape(2, rows, cols)], ext, weights[-1], terms, c1, c2, r1, r2, flops=10**9)
    return object_new, probe_step.reshape(2, modes, n, n)


def all_sum(keep, send, got, beside, then):
    maps, half, n = keep.shape
    axes = ("row", "col")
    across = lax.axis_size("col")
    devices = lax.axis_size("row") * across
    if across % 2 or half % (devices // 2):
        first = jnp.where(parity("col") == 0, keep, send)
        second = jnp.where(parity("col") == 0, send, keep)
        total = lax.psum(jnp.concatenate([first, second], axis=1), axes)
        return total[:-1] / jnp.sqrt(total[-1] + PROBE_REG), beside, then(*beside)
    groups = [list(range(k, devices, 2)) for k in range(2)]
    each = 2 * half // devices
    (parts,) = call(parts_kernel, [shape(devices // 2, maps * each, n)], keep, got)
    parts = lax.all_to_all(parts, axes, 0, 0, axis_index_groups=groups, tiled=True)
    parts, beside = lax.optimization_barrier((parts, beside))
    (steps,) = call(step_kernel, [shape(devices // 2, (maps - 1) * each, n)], parts)
    steps, beside = lax.optimization_barrier((steps, beside))
    steps = lax.all_to_all(steps, axes, 0, 0, axis_index_groups=groups, tiled=True)
    after = then(*beside)
    steps, after = lax.optimization_barrier((steps, after))
    (out,) = call(join_kernel, [shape(maps - 1, n, n)], steps, swap(steps, "col", 0))
    return out, beside, after


def solution(mesh):
    placed = (
        P(None, "row", "col"),
        P(),
        P("row", "col", None, None, None, None),
        P("row", "col", None, None, None),
    )
    return jax.shard_map(
        on_device,
        mesh=mesh,
        in_specs=placed,
        out_specs=(P(None, "row", "col"), P()),
        check_vma=False,
    )
```

```python
import functools
import math

import jax
import jax.numpy as jnp
import numpy as np
from jax import lax
from jax.experimental import pallas as pl
from jax.experimental.pallas import tpu as pltpu
from jax.sharding import PartitionSpec as P

AMP_FLOOR = 0.25
OBJECT_REG = 0.5
PROBE_REG = 1.0
MARK = 4096.0
F32 = jnp.float32
BF16 = jnp.bfloat16
LIMIT = 20 * 1024 * 1024


def tables(n):
    k = np.arange(n)
    angle = (np.outer(k, k) % n) * (2.0 * math.pi / n)
    re, im = np.cos(angle) / math.sqrt(n), -np.sin(angle) / math.sqrt(n)
    right = np.block([[re, im], [-im, re]]).astype(np.float32)
    left = np.block([[re, -im], [im, re]]).astype(np.float32)
    both = np.stack([right, left])
    high = both.astype(jnp.bfloat16)
    low = (both - high.astype(np.float32)).astype(jnp.bfloat16)
    return jnp.asarray(np.stack([high, low]))


def call(kernel, out, *args, smem=0, hbm=0, scratch=(), flops=0):
    vmem = pl.BlockSpec(memory_space=pltpu.VMEM)
    specs = [pl.BlockSpec(memory_space=pltpu.SMEM)] * smem + [pl.BlockSpec(memory_space=pltpu.HBM)] * hbm
    specs = specs + [vmem] * (len(args) - smem - hbm)
    nbytes = sum(math.prod(o.shape) * 4 for o in out) + sum(a.size * 4 for a in args)
    return pl.pallas_call(
        kernel,
        out_shape=tuple(out),
        in_specs=specs,
        out_specs=tuple([vmem] * len(out)),
        scratch_shapes=list(scratch),
        compiler_params=pltpu.CompilerParams(vmem_limit_bytes=LIMIT),
        cost_estimate=pl.CostEstimate(flops=flops, bytes_accessed=nbytes, transcendentals=0),
    )(*args)


def shape(*dims):
    return jax.ShapeDtypeStruct(dims, F32)


def split(x):
    high = x.astype(BF16)
    return high, (x - high.astype(F32)).astype(BF16)


def mm(a, b):
    return jnp.dot(a, b, preferred_element_type=F32)


def by_right(x, tab, which):
    high, low = split(x)
    t, u = tab[0, which], tab[1, which]
    return mm(high, t) + (mm(low, t) + mm(high, u))


def by_left(x, tab, which):
    high, low = split(x)
    t, u = tab[0, which], tab[1, which]
    return mm(t, high) + (mm(t, low) + mm(u, high))


def put(ref, lead, row, col, value):
    n = value.shape[0]
    tall, wide = ref.shape[len(lead) :]
    top = pl.multiple_of(jnp.minimum(row // 8, (tall - n) // 8 - 1) * 8, 8)
    base = pl.multiple_of(jnp.minimum(col // n, wide // n - 2) * n, n)
    down, right = row - top, col - base
    tiles = pltpu.roll(value.reshape(n // 8, 8, n), down & 7, 1)
    none = jnp.zeros((1, 8, n), F32)
    sub = lax.broadcasted_iota(jnp.int32, (1, 8, 1), 1)
    tiles = jnp.where(sub < down, jnp.concatenate([none, tiles], axis=0), jnp.concatenate([tiles, none], axis=0))
    moved = pltpu.roll(tiles.reshape(n + 8, n), right & (n - 1), 1)
    lane = lax.broadcasted_iota(jnp.int32, (1, n), 1)
    for at, here in ((base, lane >= right), (base + n, lane < right)):
        block = (*lead, pl.ds(top, n + 8), pl.ds(pl.multiple_of(at, n), n))
        ref[block] = ref[block] + jnp.where(here, moved, 0.0)


def cut(ref, lead, row, col, n):
    tall, wide = ref.shape[len(lead) :]
    top = pl.multiple_of(jnp.minimum(row // 8, (tall - n) // 8 - 1) * 8, 8)
    base = pl.multiple_of(jnp.minimum(col // n, wide // n - 2) * n, n)
    down, right = row - top, col - base
    lane = lax.broadcasted_iota(jnp.int32, (1, n), 1)
    left, after = (
        pltpu.roll(ref[(*lead, pl.ds(top, n + 8), pl.ds(pl.multiple_of(at, n), n))], (n - right) & (n - 1), 1)
        for at in (base, base + n)
    )
    tiles = jnp.where(lane < n - right, left, after).reshape(n // 8 + 1, 8, n)
    tiles = pltpu.roll(tiles, (8 - down) & 7, 1)
    sub = lax.broadcasted_iota(jnp.int32, (1, 8, 1), 1)
    return jnp.where(sub < 8 - down, tiles[:-1], tiles[1:]).reshape(n, n)


def positions(batch, offs, ext, probe, amps, tab, terms, grads, first):
    _, modes, n, _ = probe.shape
    half = n // 2
    terms[...] = jnp.zeros_like(terms)
    if first:
        grads[...] = jnp.zeros_like(grads)

    def one(p):
        row = offs[0, 0, batch, p, 0] + half
        col = offs[0, 0, batch, p, 1] + half
        pr, pi = cut(ext, (0,), row, col, n), cut(ext, (1,), row, col, n)
        waves = []
        for m in range(modes):
            qr, qi = probe[0, m], probe[1, m]
            waves.append(jnp.concatenate([qr * pr - qi * pi, qr * pi + qi * pr], axis=1))
        waves = jnp.concatenate(waves, axis=0)
        yield
        y = by_right(waves, tab, 0)
        z = jnp.concatenate(
            [
                jnp.concatenate([y[m * n : (m + 1) * n, :n] for m in range(modes)], axis=1),
                jnp.concatenate([y[m * n : (m + 1) * n, n:] for m in range(modes)], axis=1),
            ],
            axis=0,
        )
        yield
        far = by_left(z, tab, 1)
        yield
        square = far * far
        square = square[:n] + square[n:]
        intensity = square[:, :n]
        for m in range(1, modes):
            intensity = intensity + square[:, m * n : (m + 1) * n]
        factor = amps[batch, p] / jnp.maximum(jnp.sqrt(intensity), AMP_FLOOR) - 1.0
        wide = jnp.concatenate([factor] * modes, axis=1)
        far = far * jnp.concatenate([wide, wide], axis=0)
        yield
        h = by_left(far, tab, 0)
        h = jnp.concatenate(
            [
                jnp.concatenate([h[:n, m * n : (m + 1) * n], h[n:, m * n : (m + 1) * n]], axis=1)
                for m in range(modes)
            ],
            axis=0,
        )
        yield
        change = by_right(h, tab, 1)
        yield
        tr = ti = None
        for m in range(modes):
            cr, ci = change[m * n : (m + 1) * n, :n], change[m * n : (m + 1) * n, n:]
            qr, qi = probe[0, m], probe[1, m]
            ar, ai = qr * cr + qi * ci, qr * ci - qi * cr
            tr, ti = (ar, ai) if tr is None else (tr + ar, ti + ai)
            grads[m] = grads[m] + (pr * cr + pi * ci)
            grads[modes + m] = grads[modes + m] + (pr * ci - pi * cr)
        grads[2 * modes] = grads[2 * modes] + (pr * pr + pi * pi)
        put(terms, (0,), row, col, tr)
        put(terms, (1,), row, col, ti)

    works = [one(p) for p in range(amps.shape[1])]
    while works:
        works = [work for work in works if next(work, works) is not works]


def parity(axis):
    return lax.axis_index(axis) % 2


def ends(axis, length, width):
    near = (1 - parity(axis)) * (length - width)
    return pl.multiple_of(near, width), pl.multiple_of(length - width - near, width)


def lower(n):
    return lax.broadcasted_iota(jnp.int32, (1, n), 1) < n // 2


def pack_sides(re_low, im_low, re_high, im_high):
    half = re_low.shape[1] // 2
    keep = lower(2 * half)
    left = jnp.where(keep, re_low, pltpu.roll(im_low, half, 1))
    right = jnp.where(keep, pltpu.roll(re_high, half, 1), im_high)
    even = parity("col") == 0
    return jnp.where(even, right, left), jnp.where(even, left, right)


def by_side(first, second):
    even = parity("col") == 0
    return jnp.where(even, second, first), jnp.where(even, first, second)


def lines(offs):
    return -(-offs.shape[2] * offs.shape[3] // 8) * 8


def code(offs):
    _, _, batches, pos, dims = offs.shape
    rows = [offs[0, 0, b] + int(MARK) for b in range(batches)]
    spare = lines(offs) - batches * pos
    if spare:
        rows.append(jnp.zeros((spare, dims), jnp.int32))
    return jnp.concatenate(rows, axis=0)


def send_kernel(offs, tile, rows_1, rows_2, cols_1, cols_2):
    _, rows, cols = tile.shape
    n = cols_1.shape[1]
    half = n // 2
    coded = code(offs).astype(F32)
    for out, at in zip((rows_1, rows_2), ends("row", rows, half)):
        out[:, :half] = tile[:, pl.ds(at, half)]
        out[:, half:] = jnp.zeros((2, lines(offs), cols), F32)
        out[0, half:, : coded.shape[1]] = coded
    first, second = pack_sides(tile[0, :, :n], tile[1, :, :n], tile[0, :, cols - n :], tile[1, :, cols - n :])
    for out, value in ((cols_1, first), (cols_2, second)):
        out[:rows] = value
        out[rows:] = jnp.zeros((lines(offs), n), F32)
        out[rows:, : coded.shape[1]] = coded


def corner_kernel(cols_1, cols_2, out_1, out_2):
    n = cols_1.shape[1]
    half = n // 2
    rows = cols_1.shape[0] - (out_1.shape[1] - half)
    for out, at in zip((out_1, out_2), ends("row", rows, half)):
        for k, ref in enumerate((cols_1, cols_2)):
            out[k, :half] = ref[pl.ds(at, half)]
            out[k, half:] = ref[rows:]


def put_halo(ext, tile, rows_1, rows_2, cols_1, cols_2, corner_1, corner_2):
    _, rows, cols = tile.shape
    n = cols_1.shape[1]
    half = n // 2
    keep = lower(n)
    even = parity("row") == 0
    above = jnp.where(even, rows_2[:, :half], rows_1[:, :half])
    below = jnp.where(even, rows_1[:, :half], rows_2[:, :half])
    strips = []
    for k, ref in enumerate((cols_1, cols_2)):
        c1, c2 = corner_1[k, :half], corner_2[k, :half]
        strips.append(jnp.concatenate([jnp.where(even, c2, c1), ref[:rows], jnp.where(even, c1, c2)], axis=0))
    left, right = by_side(*strips)
    for ch in range(2):
        body = jnp.concatenate([above[ch], tile[ch], below[ch]], axis=0)
        lf = left if ch == 0 else pltpu.roll(left, half, 1)
        rt = right if ch == 1 else pltpu.roll(right, half, 1)
        turned = [lf] + [pltpu.roll(body[:, k : k + n], half, 1) for k in range(0, cols, n)] + [rt]
        for k in range(len(turned) - 1):
            ext[ch, :, k * n : (k + 1) * n] = jnp.where(keep, turned[k], turned[k + 1])


def give(n, terms, cols_1, cols_2):
    _, _, cols = terms.shape
    for out, at in zip((cols_1, cols_2), ends("col", cols, n)):
        out[...] = terms[:, :, pl.ds(at, n)]


def stage_kernel(*refs):
    count = len(refs) // 2
    for src, dst in zip(refs[:count], refs[count:]):
        dst[...] = src[: dst.shape[0]]


def first_kernel(offs, own, tile, probe, amps, tab, rows_1, rows_2, cols_1, cols_2, corner_1, corner_2,
                 ext, terms, grads, around, *sends):
    n = cols_1.shape[1]
    half = n // 2
    rows = tile.shape[1]
    size = lines(own)
    blocks = [code(own)] + [ref[rows:].astype(jnp.int32) for ref in (cols_1, cols_2)]
    for ref, corner in ((rows_1, corner_1), (rows_2, corner_2)):
        blocks += [b.astype(jnp.int32) for b in (ref[0, half:, :n], corner[0, half:], corner[1, half:])]
    lane = lax.broadcasted_iota(jnp.int32, (size, n), 1)
    for dim in range(2):
        value = jnp.zeros((size, n), jnp.int32)
        for k, block in enumerate(blocks):
            value = jnp.where(lane == k, block[:, dim : dim + 1], value)
        around[dim * size : (dim + 1) * size] = value
    put_halo(ext, tile, rows_1, rows_2, cols_1, cols_2, corner_1, corner_2)
    positions(0, offs, ext, probe, amps, tab, terms, grads, True)
    give(n, terms, *sends)


def near_kernel(terms, got, side, send_1, send_2):
    n = got.shape[2]
    _, rows, cols = terms.shape
    at, _ = ends("col", cols, n)
    side[...] = terms[:, :, pl.ds(at, n)] + got[...]
    for out, at in zip((send_1, send_2), ends("row", rows, n)):
        out[:, :, :n] = side[:, pl.ds(at, n)]
        out[:, :, n:] = terms[:, pl.ds(at, n), n : cols - n]


def far_kernel(terms, got, side, send_1, send_2):
    n = got.shape[2]
    _, rows, cols = terms.shape
    _, at = ends("col", cols, n)
    side[...] = terms[:, :, pl.ds(at, n)] + got[...]
    for out, at in zip((send_1, send_2), ends("row", rows, n)):
        out[...] = side[:, pl.ds(at, n)]


def update(ext, old, weight, terms, near, far, near_1, near_2, far_1, far_2):
    n = near.shape[2]
    _, rows, cols = old.shape
    at_near, at_far = ends("col", cols, n)
    inner = pl.ds(n, cols - 2 * n)
    for ch in range(2):
        for here, value, pieces in (
            (pl.ds(at_near, n), near[ch], (near_1[ch, :, :n], near_2[ch, :, :n])),
            (inner, terms[ch, :, n : cols - n], (near_1[ch, :, n:], near_2[ch, :, n:])),
            (pl.ds(at_far, n), far[ch], (far_1[ch], far_2[ch])),
        ):
            ext[ch, :, here] = old[ch, :, here] + value * weight[:, here]
            for piece, top in zip(pieces, ends("row", rows, n)):
                there = pl.ds(top, n)
                ext[ch, there, here] = ext[ch, there, here] + piece * weight[there, here]


def next_kernel(batch, offs, old, weight, old_terms, near, far, near_1, near_2, far_1, far_2, probe, amps, tab,
                grads_in, ext, terms, grads, *sends):
    update(ext, old, weight, old_terms, near, far, near_1, near_2, far_1, far_2)
    grads[...] = grads_in[...]
    positions(batch, offs, ext, probe, amps, tab, terms, grads, False)
    give(probe.shape[2], terms, *sends)


def last_kernel(batch, offs, old, weight, old_terms, near, far, near_1, near_2, far_1, far_2, probe, amps, tab,
                grads_in, ext, terms, keep, send, cols_1, cols_2, grads):
    n = probe.shape[2]
    half = n // 2
    update(ext, old, weight, old_terms, near, far, near_1, near_2, far_1, far_2)
    grads[...] = grads_in[...]
    positions(batch, offs, ext, probe, amps, tab, terms, grads, False)
    mine = pl.multiple_of(parity("col") * half, half)
    keep[...] = grads[:, pl.ds(mine, half)]
    send[...] = grads[:, pl.ds(pl.multiple_of(half - mine, half), half)]
    cols = terms.shape[2]
    cols_1[...], cols_2[...] = pack_sides(*(terms[ch, :, k : k + n] for k in (0, cols - n) for ch in range(2)))


def own_cols(terms, ch, cols_1, cols_2, at):
    n = cols_1.shape[1]
    cols = terms.shape[2]
    keep = lower(n)
    left, right = by_side(cols_1[at], cols_2[at])
    if ch == 0:
        left = pltpu.roll(left, n // 2, 1)
    else:
        right = pltpu.roll(right, n // 2, 1)
    blocks = [terms[ch, at, k : k + n] for k in range(0, cols, n)]
    blocks[0] = blocks[0] + jnp.where(keep, 0.0, left)
    blocks[-1] = blocks[-1] + jnp.where(keep, right, 0.0)
    return blocks


def turned(blocks):
    n = blocks[0].shape[1]
    keep = lower(n)
    moved = [pltpu.roll(block, n // 2, 1) for block in blocks]
    return [jnp.where(keep, moved[k], moved[k + 1]) for k in range(len(moved) - 1)]


def last_side_kernel(terms, cols_1, cols_2, rows_1, rows_2):
    n = cols_1.shape[1]
    half = n // 2
    for out, at in zip((rows_1, rows_2), ends("row", terms.shape[1], half)):
        for ch in range(2):
            for k, block in enumerate(turned(own_cols(terms, ch, cols_1, cols_2, pl.ds(at, half)))):
                out[ch, :, k * n : (k + 1) * n] = block


def object_kernel(old, weight, terms, cols_1, cols_2, rows_1, rows_2, out):
    _, rows, cols = old.shape
    n = cols_1.shape[1]
    half = n // 2
    tile = rows - n
    own = pl.ds(half, tile)
    gap = jnp.zeros((tile - n, n), F32)
    even = parity("row") == 0
    scales = turned([weight[own, k : k + n] for k in range(0, cols, n)])
    for ch in range(2):
        blocks = turned(own_cols(terms, ch, cols_1, cols_2, own))
        olds = turned([old[ch, own, k : k + n] for k in range(0, cols, n)])
        for k, block in enumerate(blocks):
            at = slice(k * n, (k + 1) * n)
            first, second = rows_1[ch, :, at], rows_2[ch, :, at]
            got = [jnp.where(even, second, first), gap, jnp.where(even, first, second)]
            out[ch, :, at] = olds[k] + (block + jnp.concatenate(got, axis=0)) * scales[k]


def light_kernel(batch, pos, around, probe, weight, light):
    _, modes, n, _ = probe.shape
    half = n // 2
    rows, cols = weight.shape
    size = around.shape[0] // 2
    lit = None
    for m in range(modes):
        s = probe[0, m] * probe[0, m] + probe[1, m] * probe[1, m]
        lit = s if lit is None else lit + s
    light[...] = jnp.zeros_like(light)
    odd_r, odd_c = parity("row"), parity("col")
    up, down = 2 - odd_r, 1 + odd_r
    left, right = 2 - odd_c, 1 + odd_c

    def there(k):
        return jnp.where(around[0, k] > 0, 1.0, 0.0)

    for top, first, count in (
        (n, n, 1.0 + there(3 * up + left)),
        (n, cols, there(right) + there(3 * up)),
        (rows, n, there(3 * down) + there(left)),
        (rows, cols, 1.0 + there(3 * down + right)),
    ):
        light[top : top + n, first : first + n] = lit * count

    def side(which, odd):
        step = 1 - 2 * odd
        return jnp.where(which == 0, 0, jnp.where(which == 1, step, -step))

    def one(i, carry):
        k, p = i // (pos - 2), 2 + i % (pos - 2)
        at = batch * pos + p
        row = around[at, k] - int(MARK) + half + side(k // 3, odd_r) * (rows - n)
        col = around[size + at, k] - int(MARK) + half + side(k % 3, odd_c) * (cols - n)

        @pl.when((around[at, k] > 0) & (row > -n) & (row < rows) & (col > -n) & (col < cols))
        def _():
            put(light, (), row + n, col + n, lit)

        return carry

    lax.fori_loop(0, 9 * (pos - 2), one, 0)
    low_r = jnp.where(around[0, 3 * up] > 0, 0, half)
    high_r = jnp.where(around[0, 3 * down] > 0, rows, rows - half)
    low_c = jnp.where(around[0, left] > 0, 0, half)
    high_c = jnp.where(around[0, right] > 0, cols, cols - half)
    r = lax.broadcasted_iota(jnp.int32, (rows, cols), 0)
    c = lax.broadcasted_iota(jnp.int32, (rows, cols), 1)
    inside = (r >= low_r) & (r < high_r) & (c >= low_c) & (c < high_c)
    total = light[n : n + rows, n : n + cols]
    weight[...] = jnp.where(inside, 1.0 / (total + OBJECT_REG), 0.0)


def parts_kernel(keep, got, parts):
    maps = keep.shape[0]
    each = parts.shape[1] // maps
    for m in range(maps):
        total = keep[m] + got[m]
        for i in range(parts.shape[0]):
            parts[i, m * each : (m + 1) * each] = total[i * each : (i + 1) * each]


def step_kernel(parts, out):
    total = parts[0]
    for i in range(1, parts.shape[0]):
        total = total + parts[i]
    each = total.shape[0] - out.shape[1]
    maps = total.shape[0] // each
    scale = 1.0 / jnp.sqrt(total[(maps - 1) * each :] + PROBE_REG)
    step = jnp.concatenate([total[m * each : (m + 1) * each] * scale for m in range(maps - 1)], axis=0)
    for i in range(out.shape[0]):
        out[i] = step


def join_kernel(mine, other, out):
    maps, n, _ = out.shape
    half = n // 2
    each = mine.shape[1] // maps
    at = pl.multiple_of(parity("col") * half, half)
    for ref, top in ((mine, at), (other, pl.multiple_of(half - at, half))):
        for m in range(maps):
            out[m, pl.ds(top, half)] = jnp.concatenate(
                [ref[i, m * each : (m + 1) * each] for i in range(ref.shape[0])], axis=0)


def swap(value, axis, phase):
    size = lax.axis_size(axis)
    pairs = [(i, i + 1) for i in range(phase, size - 1, 2)]
    return lax.ppermute(value, axis, pairs + [(j, i) for i, j in pairs])


def both(first, second, axis):
    return swap(first, axis, 0), swap(second, axis, 1)


def on_device(tile, probe, amplitudes, offsets):
    _, modes, n, _ = probe.shape
    half = n // 2
    _, rows, cols = tile.shape
    tall, wide = rows + n, cols + n
    amps = amplitudes[0, 0]
    batches, pos = offsets.shape[2:4]
    maps = 2 * modes + 1
    tab = tables(n)
    flops = pos * modes * 2 * 2 * 4 * 2 * n**3 * 3

    size = lines(offsets)
    sends = call(send_kernel, [shape(2, half + size, cols)] * 2 + [shape(rows + size, n)] * 2, offsets, tile)
    c1, c2 = both(*sends[2:], "col")
    r1, r2 = both(*sends[:2], "row")
    corners = call(corner_kernel, [shape(2, half + size, n)] * 2, c1, c2)
    corners, tile, probe, amps_now, tab = lax.optimization_barrier((corners, tile, probe, amps, tab))
    k1, k2 = both(*corners, "row")
    tile, probe, amps_now, tab = call(
        stage_kernel,
        [shape(*tile.shape), shape(*probe.shape), shape(1, *amps.shape[1:]), jax.ShapeDtypeStruct(tab.shape, BF16)],
        tile, probe, amps_now, tab, flops=10**9)

    plain = [shape(2, tall, wide), shape(2, tall, wide), shape(maps, n, n)]
    messages = [shape(2, tall, n)] * 2
    ext, terms, grads, around, *sends = call(
        first_kernel, plain + [jax.ShapeDtypeStruct((2 * size, n), jnp.int32)] + messages,
        offsets, offsets, tile, probe, amps_now, tab, r1, r2, c1, c2, k1, k2, smem=1, flops=flops)

    def light(batch, around):
        return call(
            functools.partial(light_kernel, batch, pos), [shape(tall, wide)], around, probe, smem=1,
            scratch=[pltpu.VMEM((tall + 2 * n, wide + 2 * n), F32)], flops=10**9)[0]

    for batch in range(batches - 1):
        c1, c2 = both(*sends, "col")
        near, *sends = call(near_kernel, [shape(2, tall, n)] + [shape(2, n, cols)] * 2, terms, c1)
        near_1, near_2 = both(*sends, "row")
        far, *sends = call(far_kernel, [shape(2, tall, n)] + [shape(2, n, n)] * 2, terms, c2)
        far_1, far_2 = both(*sends, "row")
        around, c1 = lax.optimization_barrier((around, c1))
        weight = light(batch, around)
        args = (offsets, ext, weight, terms, near, far, near_1, near_2, far_1, far_2, probe, amps, tab, grads)
        if batch + 2 < batches:
            ext, terms, grads, *sends = call(
                functools.partial(next_kernel, batch + 1), plain + messages, *args, smem=1, flops=flops)
        else:
            ext, terms, keep, send, *sends = call(
                functools.partial(last_kernel, batch + 1),
                plain[:2] + [shape(maps, half, n)] * 2 + [shape(tall, n)] * 2,
                *args, smem=1, flops=flops, scratch=[pltpu.VMEM((maps, n, n), F32)])
    got = swap(send, "col", 0)
    got, sends, around = lax.optimization_barrier((got, sends, around))
    c1, c2 = both(*sends, "col")
    weight = light(batches - 1, around)

    def send_rows(c1, c2, _):
        return both(*call(last_side_kernel, [shape(2, half, cols)] * 2, terms, c1, c2), "row")

    probe_step, (c1, c2, weight), (r1, r2) = all_sum(keep, send, got, (c1, c2, weight), send_rows)
    (object_new,) = call(
        object_kernel, [shape(2, rows, cols)], ext, weight, terms, c1, c2, r1, r2, flops=10**9)
    return object_new, probe_step.reshape(2, modes, n, n)


def all_sum(keep, send, got, beside, then):
    maps, half, n = keep.shape
    axes = ("row", "col")
    across = lax.axis_size("col")
    devices = lax.axis_size("row") * across
    if across % 2 or half % (devices // 2):
        first = jnp.where(parity("col") == 0, keep, send)
        second = jnp.where(parity("col") == 0, send, keep)
        total = lax.psum(jnp.concatenate([first, second], axis=1), axes)
        return total[:-1] / jnp.sqrt(total[-1] + PROBE_REG), beside, then(*beside)
    groups = [list(range(k, devices, 2)) for k in range(2)]
    each = 2 * half // devices
    (parts,) = call(parts_kernel, [shape(devices // 2, maps * each, n)], keep, got)
    parts = lax.all_to_all(parts, axes, 0, 0, axis_index_groups=groups, tiled=True)
    parts, beside = lax.optimization_barrier((parts, beside))
    (steps,) = call(step_kernel, [shape(devices // 2, (maps - 1) * each, n)], parts)
    steps, beside = lax.optimization_barrier((steps, beside))
    steps = lax.all_to_all(steps, axes, 0, 0, axis_index_groups=groups, tiled=True)
    after = then(*beside)
    steps, after = lax.optimization_barrier((steps, after))
    (out,) = call(join_kernel, [shape(maps - 1, n, n)], steps, swap(steps, "col", 0))
    return out, beside, after


def solution(mesh):
    placed = (
        P(None, "row", "col"),
        P(),
        P("row", "col", None, None, None, None),
        P("row", "col", None, None, None),
    )
    return jax.shard_map(
        on_device,
        mesh=mesh,
        in_specs=placed,
        out_specs=(P(None, "row", "col"), P()),
        check_vma=False,
    )
```
